32 devices in a mesh: groups: 2 (over y), gx: 4 (over z), gy: 2 (over x), vert: 2 (over core).
Axes of the slice: x: 2, y: 2, z: 4, core: 2. Of those that a mesh axis runs over, the one named last changes fastest.
Arguments:
- right_side: float32 [4, 512, 1024], P(('groups', 'vert'), 'gx', 'gy'), parts along dimension 0
- initial_guess: float32 [4, 512, 1024], P(('groups', 'vert'), 'gx', 'gy'), parts along dimension 0, may hold values from -4 to 4
- kappa_sq: float32 [4, 512, 1024], P(('groups', 'vert'), 'gx', 'gy'), parts along dimension 0, may hold values from 0.05 to 1
- smooth_weight: float32 [4], P(('groups', 'vert')), parts along dimension 0, may hold values from 0.5 to 2
- precond_scale: float32 [4, 512, 1024], P(('groups', 'vert'), 'gx', 'gy'), parts along dimension 0, may hold values from 0.01 to 0.05
- phi_vals: float32 [4, 4, 2, 16, 2, 256, 256], P(('groups', 'vert'), 'gx', 'gy'), parts along dimension 0, may hold values from -0.75 to 0.75
- phi_cols: int32 [4, 4, 2, 16, 2], P(('groups', 'vert'), 'gx', 'gy'), parts along dimension 0, may hold values from 0 to 511
- coarse_slots: int32 [8, 136], P(('groups', 'gx')), parts along dimension 0, may hold values from 0 to 271, as said below
- slot_count: int32 [8], P(('groups', 'gx')), parts along dimension 0, may hold values from 0 to 136, as said below
- coarse_rows: float32 [8, 136, 272], P(('groups', 'gx')), parts along dimension 0, as said below
Outputs:
- solution: float32 [4, 512, 1024], P(('groups', 'vert'), 'gx', 'gy'), parts along dimension 0
- residual: float32 [4, 512, 1024], P(('groups', 'vert'), 'gx', 'gy'), parts along dimension 0
The draws below stay inside these ranges and needn't reach their ends.
There are 2 independent parts, one for each index of `groups`. The reference program is written for one: setup_inputs(seed, part) draws one part's arguments, and reference() takes and returns one part's arrays. A program takes and returns all parts, laid end to end along the dimension named above; each array names one. Nothing has to cross between parts.
Inputs may be any that keep to these rules, and one draw needn't show every extreme that they name: `coarse_slots`: slots 0 to slot_count[d] - 1 of owner d hold coarse rows; over all owners these live slots name each of the 272 coarse rows exactly once. Other slots hold arbitrary row numbers. `slot_count`: the busiest owner has exactly 136 live slots; the counts sum to 272. `coarse_rows`: live slot s of owner d holds row coarse_slots[d, s] of one symmetric positive definite matrix G; rows of other slots are arbitrary.
All inputs are finite; a program needn't handle non-finite values.
Results may differ from the reference program's by a relative error of at most 0.0003.
Values sent between devices are 32-bit elements; how exact they have to be, the bound alone decides.
No kernel may reach another device: no remote copies, remote signals or barrier semaphores. Data moves between devices by JAX's collectives and lax.ppermute only.
A program may use at most 64 MiB of HBM per device.

```python
import math
import jax
import jax.numpy as jnp
from jax import lax

CX = 128
CY = 512
OBSB = 16
BSIDE = 16
PATCH = 64
REACH = 2
ITERS = 2
TILES_X = 4
TILES_Y = 2
NX = 512
NY = 1024
BLK = 256
NBLK = 256
NCO = 272
CAP = 136


def coarse_layout(key):
    layout_key = jax.random.fold_in(key, 11)
    key_list = jax.random.split(layout_key, 4)
    ordering = jax.random.permutation(key_list[0], NCO).astype(jnp.int32)
    others = TILES_X - 1
    remaining = NCO - CAP
    quota = remaining // others
    extra = remaining - quota * others
    baseline = quota + (jnp.arange(others, dtype=jnp.int32) < extra).astype(jnp.int32)
    pair_count = others // 2
    transfers = jax.random.randint(key_list[1], (pair_count,), 0, quota // 2 + 1).astype(jnp.int32)
    paired = jnp.stack([transfers, -transfers], axis=1).reshape(-1)
    adjust = jnp.concatenate([paired, jnp.zeros((others - 2 * pair_count,), jnp.int32)])
    busiest = jax.random.randint(key_list[2], (), 0, TILES_X)
    counts = jnp.concatenate([jnp.full((1,), CAP, jnp.int32), baseline + adjust])
    counts = jnp.roll(counts, busiest).astype(jnp.int32)
    offsets = jnp.cumsum(counts) - counts
    slot_ids = jnp.arange(CAP, dtype=jnp.int32)
    position = jnp.clip(offsets[:, None] + slot_ids[None, :], 0, NCO - 1)
    filler = jax.random.randint(key_list[3], (TILES_X, CAP), 0, NCO).astype(jnp.int32)
    slot_rows = jnp.where(slot_ids[None, :] < counts[:, None], ordering[position], filler)
    return (counts, slot_rows.astype(jnp.int32))


def draw_slot_count(key, part):
    return coarse_layout(key)[0]


def draw_coarse_slots(key, part):
    return coarse_layout(key)[1]


def draw_coarse_rows(key, part):
    counts, slot_rows = coarse_layout(key)
    matrix_key = jax.random.fold_in(key, 23)
    key_list = jax.random.split(matrix_key, 2)
    entries = jax.random.uniform(key_list[0], (NCO, NCO), jnp.float32, -1.0, 1.0)
    symmetric = (entries + entries.T) * (0.5 / NCO)
    identity = jnp.eye(NCO, dtype=jnp.float32)
    diagonal = 1.0 + jax.random.uniform(key_list[1], (NCO,), jnp.float32, 0.0, 0.5)
    matrix = symmetric * (1.0 - identity) + identity * diagonal[None, :]
    return matrix[slot_rows]


def draw_right_side(key, part):
    row_pos = jnp.arange(NX, dtype=jnp.float32) / NX
    ramp = (0.7 + 0.6 * row_pos)[None, :, None]
    return jax.random.normal(key, (2, NX, NY), jnp.float32) * ramp


def plant(drawn, key, smallest, high):
    shape = drawn.shape
    index_at = [jax.random.randint(jax.random.fold_in(key, axis), (), 0, shape[axis]) for axis in range(len(shape))]
    drawn = drawn.at[tuple(index_at)].set(smallest)
    longest = shape.index(max(shape))
    index_at[longest] = (index_at[longest] + 1) % shape[longest]
    return drawn.at[tuple(index_at)].set(high)


def block_scale(rng, extent, shards, low, top_value):
    loudness = 1.0
    for axis_at, parts in shards:
        steps = jax.random.uniform(jax.random.fold_in(jax.random.fold_in(rng, 6), axis_at), (parts,), jnp.float32, low / len(shards), top_value / len(shards))
        loudness = loudness * jnp.repeat(jnp.exp(steps), extent[axis_at] // parts).reshape((-1,) + (1,) * (len(extent) - 1 - axis_at))
    return loudness


def scatter_about(key, shape, deviation, bound, shards=(), kind=jnp.bfloat16):
    loudness = block_scale(key, shape, shards, -0.22, 0.18) if shards else 1.0
    result = jax.random.normal(key, shape, jnp.float32) * deviation * loudness
    return jnp.minimum(jnp.maximum(result, -bound), bound).astype(kind)


def setup_inputs(seed: int = 0, part: int = 0) -> dict:
    keys = jax.random.split(jax.random.key(seed), 11)
    part_splits = jax.random.split(jax.random.fold_in(keys[10], part), 11)
    return {
        "right_side": draw_right_side(jax.random.fold_in(jax.random.fold_in(keys[10], part), 71), part),
        "initial_guess": scatter_about(part_splits[1], (2, NX, NY), 0.5, 4.0, ((0, 2), (1, 4), (2, 2)), jnp.float32),
        "kappa_sq": jnp.clip(jnp.exp(math.log(1.0) - 2.9957323 * jax.random.uniform(part_splits[2], (2, NX, NY), jnp.float32) ** block_scale(part_splits[2], (2, NX, NY), ((0, 2), (1, 4), (2, 2)), -0.2, 0.2)), 0.05, 1.0),
        "smooth_weight": jnp.clip(jnp.exp(math.log(2.0) - 1.3862944 * jax.random.uniform(part_splits[3], (2,), jnp.float32) ** block_scale(part_splits[3], (2,), ((0, 2),), -0.2, 0.2)), 0.5, 2.0),
        "precond_scale": jnp.clip(jnp.exp(math.log(0.05) - 1.609438 * jax.random.uniform(part_splits[4], (2, NX, NY), jnp.float32) ** block_scale(part_splits[4], (2, NX, NY), ((0, 2), (1, 4), (2, 2)), -0.2, 0.2)), 0.01, 0.05),
        "phi_vals": scatter_about(part_splits[5], (2, TILES_X, TILES_Y, OBSB, REACH, BLK, BLK), 64 ** -0.5, 0.75, ((0, 2), (1, 4), (2, 2)), jnp.float32),
        "phi_cols": plant(jax.random.randint(part_splits[6], (2, TILES_X, TILES_Y, OBSB, REACH), 0, 2 * NBLK), jax.random.fold_in(part_splits[6], 1), 0, (2 * NBLK) - 1).astype(jnp.int32),
        "coarse_slots": draw_coarse_slots(jax.random.fold_in(jax.random.fold_in(keys[10], part), 71), part),
        "slot_count": draw_slot_count(jax.random.fold_in(jax.random.fold_in(keys[10], part), 71), part),
        "coarse_rows": draw_coarse_rows(jax.random.fold_in(jax.random.fold_in(keys[10], part), 71), part),
    }


PRECISE = lax.Precision.HIGHEST

def sar_apply(vector, kappa_sq):
    padded = jnp.pad(vector, ((0, 0), (1, 1), (1, 1)))
    beside = padded[:, 2:, 1:-1] + padded[:, :-2, 1:-1] + padded[:, 1:-1, 2:] + padded[:, 1:-1, :-2]
    return (4.0 + kappa_sq) * vector - beside

def to_blocks(vector):
    shaped = vector.reshape(2, TILES_X, CX // BSIDE, BSIDE, TILES_Y, CY // BSIDE, BSIDE)
    return shaped.transpose(0, 1, 4, 2, 5, 3, 6).reshape(2, TILES_X, TILES_Y, NBLK, BLK)

def from_blocks(blocks):
    shaped = blocks.reshape(2, TILES_X, TILES_Y, CX // BSIDE, CY // BSIDE, BSIDE, BSIDE)
    return shaped.transpose(0, 1, 3, 5, 2, 4, 6).reshape(2, NX, NY)

def data_apply(vector, phi_vals, phi_cols):
    blocks = to_blocks(vector)
    stacked = jnp.concatenate([blocks, blocks[::-1]], axis=3)
    targets = phi_cols.reshape(2, TILES_X, TILES_Y, OBSB * REACH, 1)
    selector = (targets == jnp.arange(2 * NBLK, dtype=jnp.int32)).astype(jnp.float32)
    chosen = jnp.einsum('vxyns,vxysj->vxynj', selector, stacked, precision=PRECISE)
    chosen = chosen.reshape(2, TILES_X, TILES_Y, OBSB, REACH, BLK)
    observed = jnp.einsum('vxyokij,vxyokj->vxyoi', phi_vals, chosen, precision=PRECISE)
    spread = jnp.einsum('vxyokij,vxyoi->vxyokj', phi_vals, observed, precision=PRECISE)
    spread = spread.reshape(2, TILES_X, TILES_Y, OBSB * REACH, BLK)
    block_terms = jnp.einsum('vxyns,vxynj->vxysj', selector, spread, precision=PRECISE)
    own_terms = block_terms[:, :, :, :NBLK] + block_terms[::-1][:, :, :, NBLK:]
    return from_blocks(own_terms)

def coarse_apply(residual_in, precond_scale, coarse_slots, slot_count, coarse_rows):
    whole_norm = math.sqrt(CX * CY)
    patch_norm = float(PATCH)
    coarsest = residual_in.reshape(2, TILES_X, CX, TILES_Y, CY).sum(axis=(2, 4)) / whole_norm
    middle = residual_in.reshape(2, NX // PATCH, PATCH, NY // PATCH, PATCH).sum(axis=(2, 4)) / patch_norm
    coarse_vec = jnp.concatenate([coarsest.reshape(2, -1), middle.reshape(2, -1)], axis=1).reshape(-1)
    live_mask = (jnp.arange(CAP, dtype=jnp.int32)[None, :] < slot_count[:, None]).astype(jnp.float32)
    products = jnp.dot(coarse_rows.reshape(-1, NCO), coarse_vec, precision=PRECISE) * live_mask.reshape(-1)
    coarse_out = jnp.zeros((NCO,), jnp.float32).at[coarse_slots.reshape(-1)].add(products).reshape(2, -1)
    lift_top = coarse_out[:, :TILES_X * TILES_Y].reshape(2, TILES_X, 1, TILES_Y, 1) / whole_norm
    lift_mid = coarse_out[:, TILES_X * TILES_Y:].reshape(2, NX // PATCH, 1, NY // PATCH, 1) / patch_norm
    lift_top = jnp.broadcast_to(lift_top, (2, TILES_X, CX, TILES_Y, CY)).reshape(2, NX, NY)
    lift_mid = jnp.broadcast_to(lift_mid, (2, NX // PATCH, PATCH, NY // PATCH, PATCH)).reshape(2, NX, NY)
    return precond_scale * residual_in + (lift_mid + lift_top)

def reference(right_side, initial_guess, kappa_sq, smooth_weight, precond_scale, phi_vals, phi_cols, coarse_slots, slot_count, coarse_rows):

    def apply_a(vector):
        smooth = sar_apply(sar_apply(vector, kappa_sq), kappa_sq)
        return smooth_weight[:, None, None] * smooth + data_apply(vector, phi_vals, phi_cols)

    def apply_m(vector):
        return coarse_apply(vector, precond_scale, coarse_slots, slot_count, coarse_rows)
    solution = initial_guess
    residual = right_side - apply_a(solution)
    precond = apply_m(residual)
    direction = precond
    gamma = jnp.sum(residual * precond)
    for iteration in range(ITERS):
        image = apply_a(direction)
        step_size = gamma / jnp.sum(direction * image)
        solution = solution + step_size * direction
        residual = residual - step_size * image
        if iteration + 1 < ITERS:
            precond = apply_m(residual)
            gamma_new = jnp.sum(residual * precond)
            direction = precond + gamma_new / gamma * direction
            gamma = gamma_new
    return (solution, residual)
```

```python
import functools
import math

import jax
import jax.numpy as jnp
import numpy as np
from jax import lax
from jax.experimental import pallas as pl
from jax.experimental.pallas import tpu as pltpu
from jax.sharding import PartitionSpec as P

BSIDE = 16
PATCH = 64
LANES = 128
PAD = 8
ALL = ("gx", "gy", "vert")
F32 = jnp.float32
VMEM = pl.BlockSpec(memory_space=pltpu.VMEM)
SMEM = pl.BlockSpec(memory_space=pltpu.SMEM)
ANY = pl.BlockSpec(memory_space=pl.ANY)
PARAMS = pltpu.CompilerParams(vmem_limit_bytes=40 * 1024 * 1024)


class Sizes:
    def __init__(self, tx, ty, tile_shape, obs, reach, nco):
        self.tx, self.ty = tx, ty
        self.rows, self.cols = tile_shape
        self.obs, self.reach = obs, reach
        self.nco = nco
        self.px, self.py = self.rows // PATCH, self.cols // PATCH
        self.groups = self.cols // LANES
        self.ext = (self.rows + 2 * PAD, self.cols + 2 * LANES)
        self.devices = tx * ty * 2
        self.per_var = tx * ty * (1 + self.px * self.py)
        self.vec_rows = -(-nco // LANES)
        self.head = PAD * (-(-(self.vec_rows + 1) // PAD))
        self.ext_patches = (self.px + 2) * (self.py + 2)
        self.lift_rows = PAD * (-(-(self.ext_patches + self.px * self.py) // PAD))
        self.blocks = (self.rows // BSIDE) * (self.cols // BSIDE)
        self.top_div = math.sqrt(self.rows * self.cols)
        self.mid_div = float(PATCH)


def iota(shape, dim):
    return lax.broadcasted_iota(jnp.int32, shape, dim)


def lift_ids(sz):
    mid = np.full((sz.tx, sz.ty, 2, sz.lift_rows), -1, np.int32)
    top = np.full((sz.tx, sz.ty, 2, sz.lift_rows), -1, np.int32)
    tiles = sz.tx * sz.ty
    for x in range(sz.tx):
        for y in range(sz.ty):
            for v in range(2):
                for i in range(-1, sz.px + 1):
                    for j in range(-1, sz.py + 1):
                        gi, gj = x * sz.px + i, y * sz.py + j
                        if 0 <= gi < sz.tx * sz.px and 0 <= gj < sz.ty * sz.py:
                            at = (i + 1) * (sz.py + 2) + j + 1
                            mid[x, y, v, at] = v * sz.per_var + tiles + gi * sz.ty * sz.py + gj
                            top[x, y, v, at] = (
                                v * sz.per_var + (gi // sz.px) * sz.ty + gj // sz.py
                            )
                for i in range(sz.px):
                    for j in range(sz.py):
                        gi, gj = x * sz.px + i, y * sz.py + j
                        at = sz.ext_patches + i * sz.py + j
                        mid[x, y, v, at] = (1 - v) * sz.per_var + tiles + gi * sz.ty * sz.py + gj
                        top[x, y, v, at] = (1 - v) * sz.per_var + x * sz.ty + y
    order = np.arange(sz.tx)[:, None] ^ np.arange(sz.tx)[None, :]
    shape = (sz.tx, sz.tx, sz.ty, 2, sz.lift_rows)
    moved = [a[order.reshape(-1)].reshape(shape).transpose(0, 2, 3, 1, 4) for a in (mid, top)]
    return np.stack(moved, axis=3)


def pack_edges(sz, x0_ref, s_ref, k_ref, xe_ref, xo_ref, ye_ref, yo_ref):
    xi, yi = lax.axis_index("gx"), lax.axis_index("gy")
    even_x, even_y = lax.rem(xi, 2) == 0, lax.rem(yi, 2) == 0
    r, g = sz.rows, sz.groups
    for at, (ref, width) in enumerate(((x0_ref, 2), (s_ref, 2), (k_ref, 1))):
        for j in range(g):
            lane = pl.ds(j * LANES, LANES)
            low = ref[0, pl.ds(0, width), lane]
            high = ref[0, pl.ds(r - width, width), lane]
            dst = pl.ds(at * 2 * g + j * width, width)
            xe_ref[dst, :] = jnp.where(even_x, high, low)
            xo_ref[dst, :] = jnp.where(even_x, low, high)
        low = ref[0, :, pl.ds(0, LANES)].T[0:width]
        high = ref[0, :, pl.ds(sz.cols - LANES, LANES)].T[LANES - width : LANES]
        dst = pl.ds(at * 2, width)
        ye_ref[dst, :] = jnp.where(even_y, high, low)
        yo_ref[dst, :] = jnp.where(even_y, low, high)


def put_sides(sz, ref, low, high):
    width = low.shape[0]
    zeros = jnp.zeros((LANES - width, LANES), F32)
    mid = pl.ds(PAD, sz.rows)
    ref[mid, pl.ds(0, LANES)] = jnp.concatenate([zeros, low], axis=0).T
    ref[mid, pl.ds(LANES + sz.cols, LANES)] = jnp.concatenate([high, zeros], axis=0).T


def clear_bands(sz, ref):
    blank = jnp.zeros((PAD, sz.ext[1]), F32)
    ref[pl.ds(0, PAD), :] = blank
    ref[pl.ds(PAD + sz.rows, PAD), :] = blank


def gather_patches(sz, v2_ref, cols_ref, chosen_ref):
    lane = iota((BSIDE, LANES), 1)
    row = iota((PAD, LANES), 0)
    diag = row == iota((PAD, LANES), 1) // BSIDE
    per_row = sz.cols // BSIDE
    per_lanes = LANES // BSIDE
    for q in range(sz.obs * sz.reach):
        m = cols_ref[0, 0, 0, q // sz.reach, q % sz.reach]
        var, n = m // sz.blocks, lax.rem(m, sz.blocks)
        i, j = n // per_row, lax.rem(n, per_row)
        at = pl.ds(pl.multiple_of(PAD + i * BSIDE, PAD), BSIDE)
        lanes = pl.ds(pl.multiple_of(LANES + (j // per_lanes) * LANES, LANES), LANES)
        block = v2_ref[var, at, lanes]
        block = jnp.where(lane // BSIDE == lax.rem(j, per_lanes), block, 0.0)
        for step in (16, 32, 64):
            block = block + pltpu.roll(block, step, 1)
        for h in range(2):
            part = jnp.where(diag, block[h * PAD : (h + 1) * PAD], 0.0)
            chosen_ref[q // sz.reach, pl.ds(q % sz.reach, 1), pl.ds(h * LANES, LANES)] = jnp.sum(
                part, axis=0, keepdims=True
            )


def scatter_patches(sz, t_ref, cols_ref, spread_ref, sign):
    lane = iota((PAD, LANES), 1)
    row = iota((PAD, LANES), 0)
    diag = row == lane // BSIDE
    per_row = sz.cols // BSIDE
    per_lanes = LANES // BSIDE
    for q in range(sz.obs * sz.reach):
        m = cols_ref[0, 0, 0, q // sz.reach, q % sz.reach]
        var, n = m // sz.blocks, lax.rem(m, sz.blocks)
        i, j = n // per_row, lax.rem(n, per_row)
        lanes = pl.ds(pl.multiple_of((j // per_lanes) * LANES, LANES), LANES)
        here = lane // BSIDE == lax.rem(j, per_lanes)
        for h in range(2):
            line = spread_ref[q // sz.reach, pl.ds(q % sz.reach, 1), pl.ds(h * LANES, LANES)]
            part = jnp.where(diag, line, 0.0)
            for step in (16, 32, 64):
                part = part + pltpu.roll(part, step, 1)
            at = pl.ds(pl.multiple_of(i * BSIDE + h * PAD, PAD), PAD)
            t_ref[var, at, lanes] = t_ref[var, at, lanes] + sign * jnp.where(here, part, 0.0)


def start_phi(sz, phi_ref, buf_ref, sems):
    for o in range(sz.obs):
        pltpu.make_async_copy(phi_ref.at[0, 0, 0, o], buf_ref.at[o], sems.at[o]).start()


def observe_spread(sz, phi_ref, buf_ref, sems, chosen_ref, spread_ref):
    halves = (BSIDE * BSIDE) // LANES

    def body(o, carry):
        pltpu.make_async_copy(phi_ref.at[0, 0, 0, o], buf_ref.at[o], sems.at[o]).wait()
        acc = None
        for k in range(sz.reach):
            line = chosen_ref[o, pl.ds(k, 1), :]
            for h in range(halves):
                lanes = pl.ds(h * LANES, LANES)
                term = buf_ref[o, k, :, lanes] * line[:, h * LANES : (h + 1) * LANES]
                acc = term if acc is None else acc + term
        observed = jnp.sum(acc, axis=1, keepdims=True)
        for k in range(sz.reach):
            for h in range(halves):
                lanes = pl.ds(h * LANES, LANES)
                spread_ref[o, pl.ds(k, 1), lanes] = jnp.sum(
                    buf_ref[o, k, :, lanes] * observed, axis=0, keepdims=True
                )
        return carry

    lax.fori_loop(0, sz.obs, body, 0)


def smooth(sz, v2_ref, ke_ref, y_ref):
    xi, yi = lax.axis_index("gx"), lax.axis_index("gy")
    rows, cols = sz.ext
    v = v2_ref[0]
    beside = (
        pltpu.roll(v, 1, 0)
        + pltpu.roll(v, rows - 1, 0)
        + pltpu.roll(v, 1, 1)
        + pltpu.roll(v, cols - 1, 1)
    )
    y_ref[...] = (4.0 + ke_ref[...]) * v - beside

    @pl.when(xi == 0)
    def _():
        y_ref[pl.ds(0, PAD), :] = jnp.zeros((PAD, cols), F32)

    @pl.when(xi == sz.tx - 1)
    def _():
        y_ref[pl.ds(PAD + sz.rows, PAD), :] = jnp.zeros((PAD, cols), F32)

    @pl.when(yi == 0)
    def _():
        y_ref[:, pl.ds(0, LANES)] = jnp.zeros((rows, LANES), F32)

    @pl.when(yi == sz.ty - 1)
    def _():
        y_ref[:, pl.ds(LANES + sz.cols, LANES)] = jnp.zeros((rows, LANES), F32)

    inner = pl.ds(LANES, sz.cols)
    mid = y_ref[pl.ds(PAD, sz.rows), :]
    side = pltpu.roll(mid, 1, 1) + pltpu.roll(mid, cols - 1, 1)
    beside = y_ref[pl.ds(PAD - 1, sz.rows), inner] + y_ref[pl.ds(PAD + 1, sz.rows), inner]
    beside = beside + side[:, LANES : LANES + sz.cols]
    kappa = ke_ref[pl.ds(PAD, sz.rows), inner]
    return (4.0 + kappa) * mid[:, LANES : LANES + sz.cols] - beside


def device_at(sz, x, y, v):
    return (x * sz.ty + y) * 2 + v


def pack_payload(sz, t_ref, pay_ref):
    xi, yi, vi = lax.axis_index("gx"), lax.axis_index("gy"), lax.axis_index("vert")
    flat = iota((sz.head, LANES), 0) * LANES + iota((sz.head, LANES), 1)
    lane = iota((1, LANES), 1)
    vec = jnp.zeros((sz.head, LANES), F32)
    tiles = sz.tx * sz.ty
    for t in range(2):
        var = vi if t == 0 else 1 - vi
        total = jnp.zeros((1, LANES), F32)
        for a in range(sz.px):
            for j in range(sz.groups):
                seg = jnp.sum(
                    t_ref[t, pl.ds(a * PATCH, PATCH), pl.ds(j * LANES, LANES)],
                    axis=0,
                    keepdims=True,
                )
                total = total + seg
                for half in range(2):
                    keep = (lane >= PATCH) if half else (lane < PATCH)
                    value = jnp.sum(jnp.where(keep, seg, 0.0), axis=1, keepdims=True)
                    at = (
                        var * sz.per_var
                        + tiles
                        + (xi * sz.px + a) * (sz.ty * sz.py)
                        + yi * sz.py
                        + 2 * j
                        + half
                    )
                    vec = jnp.where(flat == at, value * (1.0 / sz.mid_div), vec)
        value = jnp.sum(total, axis=1, keepdims=True)
        at = var * sz.per_var + xi * sz.ty + yi
        vec = jnp.where(flat == at, value * (1.0 / sz.top_div), vec)

    def fill(s, carry):
        pay_ref[s, pl.ds(0, sz.head), :] = vec
        return carry

    lax.fori_loop(0, sz.devices, fill, 0, unroll=True if sz.devices <= 16 else 1)

    r, c = sz.rows, sz.cols
    for t in range(2):
        var = vi if t == 0 else 1 - vi
        for dx, first in ((-1, 0), (1, r - 2)):
            @pl.when((xi + dx >= 0) & (xi + dx < sz.tx))
            def _(t=t, var=var, dx=dx, first=first):
                dest = device_at(sz, xi + dx, yi, var)
                for j in range(sz.groups):
                    pay_ref[dest, pl.ds(sz.head + 2 * j, 2), :] = t_ref[
                        t, pl.ds(first, 2), pl.ds(j * LANES, LANES)
                    ]

        for dy in (-1, 1):
            @pl.when((yi + dy >= 0) & (yi + dy < sz.ty))
            def _(t=t, var=var, dy=dy):
                dest = device_at(sz, xi, yi + dy, var)
                if dy < 0:
                    pair = t_ref[t, :, pl.ds(0, LANES)].T[0:2]
                else:
                    pair = t_ref[t, :, pl.ds(c - LANES, LANES)].T[LANES - 2 : LANES]
                pay_ref[dest, pl.ds(sz.head, 2), :] = pair

            for dx in (-1, 1):
                @pl.when(
                    (xi + dx >= 0) & (xi + dx < sz.tx) & (yi + dy >= 0) & (yi + dy < sz.ty)
                )
                def _(t=t, var=var, dx=dx, dy=dy):
                    dest = device_at(sz, xi + dx, yi + dy, var)
                    lanes = pl.ds(0 if dy < 0 else c - LANES, LANES)
                    pay_ref[dest, pl.ds(sz.head, 1), :] = t_ref[
                        t, pl.ds(0 if dx < 0 else r - 1, 1), lanes
                    ]


def from_neighbour(sz, recv_ref, dx, dy, count):
    xi, yi = lax.axis_index("gx"), lax.axis_index("gy")
    x, y = xi + dx, yi + dy
    inside = (x >= 0) & (x < sz.tx) & (y >= 0) & (y < sz.ty)
    source = device_at(sz, jnp.clip(x, 0, sz.tx - 1), jnp.clip(y, 0, sz.ty - 1), 0)
    rows = pl.ds(sz.head, count)
    both = recv_ref[source, rows, :] + recv_ref[source + 1, rows, :]
    return jnp.where(inside, both, 0.0)


def first_kernel(sz, x0_ref, s_ref, k_ref, b_ref, xp_ref, he_ref, ho_ref, hye_ref, hyo_ref,
                 cols_ref, w_ref, phi_ref, t_ref, pay_ref, se_ref, ke_ref,
                 v2_ref, y_ref, chosen_ref, spread_ref, buf_ref, sems):
    start_phi(sz, phi_ref, buf_ref, sems)
    xi, yi = lax.axis_index("gx"), lax.axis_index("gy")
    even_x, even_y = lax.rem(xi, 2) == 0, lax.rem(yi, 2) == 0
    r, c, g = sz.rows, sz.cols, sz.groups
    edge = PAD * (-(-5 * g // PAD))
    lane = iota((1, LANES), 1)
    mid, inner = pl.ds(PAD, r), pl.ds(LANES, c)

    def pick(odd_ref, even_ref, rows, inside_low, inside_high, parity):
        from_e, from_o = even_ref[rows, :], odd_ref[rows, :]
        low = jnp.where(inside_low, jnp.where(parity, from_o, from_e), 0.0)
        high = jnp.where(inside_high, jnp.where(parity, from_e, from_o), 0.0)
        return low, high

    for at, (ref, src, width) in enumerate(
        ((v2_ref.at[0], x0_ref, 2), (se_ref, s_ref, 2), (ke_ref, k_ref, 1))
    ):
        clear_bands(sz, ref)
        ref[mid, inner] = src[0]
        low, high = pick(
            hyo_ref, hye_ref, pl.ds(2 * at, width), yi > 0, yi < sz.ty - 1, even_y
        )
        put_sides(sz, ref, low, high)
        for j in range(g):
            low, high = pick(
                ho_ref, he_ref, pl.ds(at * 2 * g + j * width, width),
                xi > 0, xi < sz.tx - 1, even_x,
            )
            lanes = pl.ds(LANES + j * LANES, LANES)
            ref[pl.ds(PAD - width, width), lanes] = low
            ref[pl.ds(PAD + r, width), lanes] = high
        if width == 2:
            for side in range(2):
                y_in = (yi > 0) if side == 0 else (yi < sz.ty - 1)
                beside_e = even_y if side else jnp.logical_not(even_y)
                column = 2 * at + (1 if side == 0 else 0)
                low_e, high_e = pick(
                    ho_ref, he_ref, pl.ds(edge + column, 1),
                    (xi > 0) & y_in, (xi < sz.tx - 1) & y_in, even_x,
                )
                low_o, high_o = pick(
                    ho_ref, he_ref, pl.ds(edge + PAD + column, 1),
                    (xi > 0) & y_in, (xi < sz.tx - 1) & y_in, even_x,
                )
                low = jnp.where(beside_e, low_e, low_o)
                high = jnp.where(beside_e, high_e, high_o)
                spot = lane == (LANES - 1 if side == 0 else 0)
                lanes = pl.ds(0 if side == 0 else LANES + c, LANES)
                last = jnp.sum(jnp.where(lane == LANES - 1, low, 0.0), axis=1, keepdims=True)
                ref[pl.ds(PAD - 1, 1), lanes] = jnp.where(spot, last, 0.0)
                first = jnp.sum(jnp.where(lane == 0, high, 0.0), axis=1, keepdims=True)
                ref[pl.ds(PAD + r, 1), lanes] = jnp.where(spot, first, 0.0)
    v2_ref[1, mid, inner] = xp_ref[0]
    gather_patches(sz, v2_ref, cols_ref, chosen_ref)
    observe_spread(sz, phi_ref, buf_ref, sems, chosen_ref, spread_ref)
    t_ref[0] = b_ref[0] - w_ref[0] * smooth(sz, v2_ref, ke_ref, y_ref)
    t_ref[1] = jnp.zeros((r, c), F32)
    scatter_patches(sz, t_ref, cols_ref, spread_ref, -1.0)
    pack_payload(sz, t_ref, pay_ref)


def precondition(sz, recv_ref, lg_ref, to_ref, tm_ref, se_ref, sp_ref, v2_ref, res_ref):
    r, c, g = sz.rows, sz.cols, sz.groups
    lane = iota((1, LANES), 1)
    mid, inner = pl.ds(PAD, r), pl.ds(LANES, c)

    def add_head(s, vec):
        return vec + recv_ref[s, pl.ds(0, sz.head), :]

    vec = lax.fori_loop(
        1, sz.devices, add_head, recv_ref[0, pl.ds(0, sz.head), :],
        unroll=True if sz.devices <= 16 else 1,
    )
    acc = None
    for i in range(sz.vec_rows):
        term = lg_ref[pl.ds(i * sz.lift_rows, sz.lift_rows), :] * vec[i : i + 1]
        acc = term if acc is None else acc + term
    lift = jnp.broadcast_to(jnp.sum(acc, axis=1, keepdims=True), (sz.lift_rows, LANES))

    ext = v2_ref.at[0]
    clear_bands(sz, ext)
    whole = to_ref[0] + tm_ref[1]
    res_ref[...] = whole
    ext[mid, inner] = whole
    put_sides(
        sz, ext, from_neighbour(sz, recv_ref, 0, -1, 2), from_neighbour(sz, recv_ref, 0, 1, 2)
    )
    up = from_neighbour(sz, recv_ref, -1, 0, 2 * g)
    down = from_neighbour(sz, recv_ref, 1, 0, 2 * g)
    for j in range(g):
        lanes = pl.ds(LANES + j * LANES, LANES)
        ext[pl.ds(PAD - 2, 2), lanes] = up[2 * j : 2 * j + 2]
        ext[pl.ds(PAD + r, 2), lanes] = down[2 * j : 2 * j + 2]
    for dx in (-1, 1):
        for dy in (-1, 1):
            line = from_neighbour(sz, recv_ref, dx, dy, 1)
            lanes = pl.ds(0 if dy < 0 else LANES + c, LANES)
            ext[pl.ds(PAD - 1 if dx < 0 else PAD + r, 1), lanes] = line

    bands = [(0, PAD)] + [(PAD + a * PATCH, PATCH) for a in range(sz.px)] + [(PAD + r, PAD)]
    wide = sz.py + 2
    for a, (first, count) in enumerate(bands):
        rows = pl.ds(first, count)
        for j in range(g + 2):
            lanes = pl.ds(j * LANES, LANES)
            if j == 0:
                line = lift[a * wide : a * wide + 1]
            elif j == g + 1:
                line = lift[a * wide + wide - 1 : a * wide + wide]
            else:
                at = a * wide + 2 * j - 1
                line = jnp.where(lane < PATCH, lift[at : at + 1], lift[at + 1 : at + 2])
            ext[rows, lanes] = se_ref[rows, lanes] * ext[rows, lanes] + line
    for a in range(sz.px):
        rows = pl.ds(a * PATCH, PATCH)
        for j in range(g):
            lanes = pl.ds(j * LANES, LANES)
            at = sz.ext_patches + a * sz.py + 2 * j
            line = jnp.where(lane < PATCH, lift[at : at + 1], lift[at + 1 : at + 2])
            other = tm_ref[0, rows, lanes] + to_ref[1, rows, lanes]
            v2_ref[1, pl.ds(PAD + a * PATCH, PATCH), pl.ds(LANES + j * LANES, LANES)] = (
                sp_ref[0, rows, lanes] * other + line
            )


def fold(product):
    return jnp.sum(product, axis=0, keepdims=True)


def row_dot(sz, left, right):
    line = jnp.sum(left * right, axis=0, keepdims=True)
    total = line[:, 0:LANES]
    for j in range(1, sz.groups):
        total = total + line[:, j * LANES : (j + 1) * LANES]
    return total


def apply_kernel(sz, last, recv_ref, lg_ref, to_ref, tm_ref, se_ref, ke_ref, sp_ref, cols_ref,
                 w_ref, dots_ref, phi_ref, t_ref, pay_ref, res_ref, pre_ref, out_dots_ref,
                 v2_ref, y_ref, chosen_ref, spread_ref, buf_ref, sems):
    start_phi(sz, phi_ref, buf_ref, sems)
    r, c = sz.rows, sz.cols
    mid, inner = pl.ds(PAD, r), pl.ds(LANES, c)
    precondition(sz, recv_ref, lg_ref, to_ref, tm_ref, se_ref, sp_ref, v2_ref, res_ref)
    gather_patches(sz, v2_ref, cols_ref, chosen_ref)
    observe_spread(sz, phi_ref, buf_ref, sems, chosen_ref, spread_ref)
    t_ref[0] = w_ref[0] * smooth(sz, v2_ref, ke_ref, y_ref)
    t_ref[1] = jnp.zeros((r, c), F32)
    scatter_patches(sz, t_ref, cols_ref, spread_ref, 1.0)
    own = v2_ref[0, mid, inner]
    pre_ref[...] = own
    gamma = row_dot(sz, res_ref[...], own)
    curve = row_dot(sz, own, t_ref[0]) + row_dot(sz, v2_ref[1, mid, inner], t_ref[1])
    if last:
        lines = jnp.concatenate(
            [dots_ref[0:2], gamma, curve, jnp.zeros((PAD - 4, LANES), F32)], axis=0
        )
        out_dots_ref[...] = lines

        def fill(s, carry):
            pay_ref[s] = lines
            return carry

        lax.fori_loop(0, sz.devices, fill, 0, unroll=True if sz.devices <= 16 else 1)
    else:
        out_dots_ref[...] = jnp.concatenate(
            [gamma, curve, jnp.zeros((PAD - 2, LANES), F32)], axis=0
        )
        pack_payload(sz, t_ref, pay_ref)


def final_kernel(sz, recv_ref, x0_ref, r_ref, p_ref, w_ref, z_ref, to_ref, tm_ref, x_ref, res_ref):
    def add(s, lines):
        return lines + recv_ref[s]

    lines = lax.fori_loop(
        1, sz.devices, add, recv_ref[0], unroll=True if sz.devices <= 16 else 1
    )
    sums = jnp.sum(lines, axis=1, keepdims=True)
    gamma, delta, cross, far = (sums[i : i + 1] for i in range(4))
    step = gamma / delta
    gamma_new = step * step * cross - gamma
    growth = step * cross / delta
    curve = step * step * (far - cross * cross / delta)
    step_new = gamma_new / curve
    along = step + step_new * growth
    back = step_new * step
    x_ref[0] = x0_ref[0] + (along * p_ref[...] - back * z_ref[...])
    image = to_ref[0] + tm_ref[1]
    res_ref[0] = r_ref[...] - (along * w_ref[...] - back * image)


def shape(*dims):
    return jax.ShapeDtypeStruct(dims, F32)


def work_space(sz):
    block = BSIDE * BSIDE
    return [
        pltpu.VMEM((2,) + sz.ext, F32),
        pltpu.VMEM(sz.ext, F32),
        pltpu.VMEM((sz.obs, sz.reach, block), F32),
        pltpu.VMEM((sz.obs, sz.reach, block), F32),
        pltpu.VMEM((sz.obs, sz.reach, block, block), F32),
        pltpu.SemaphoreType.DMA((sz.obs,)),
    ]


def local(right_side, initial_guess, kappa_sq, smooth_weight, precond_scale, phi_vals, phi_cols,
          coarse_slots, slot_count, coarse_rows):
    tx, ty = lax.axis_size("gx"), lax.axis_size("gy")
    xi, yi, vi = lax.axis_index("gx"), lax.axis_index("gy"), lax.axis_index("vert")
    sz = Sizes(tx, ty, right_side.shape[1:], phi_vals.shape[3], phi_vals.shape[4],
               coarse_rows.shape[2])
    swap = [(0, 1), (1, 0)]
    edge_rows = PAD * (-(-5 * sz.groups // PAD))

    def paired(axis_size, k):
        return [(i, i ^ k) for i in range(axis_size)]

    def even_pairs(n):
        return [(i, i ^ 1) for i in range(n)]

    def odd_pairs(n):
        return [(i, (i + 1) % n if i % 2 else (i - 1) % n) for i in range(n)]

    x_partner = lax.ppermute(initial_guess, "vert", swap)
    s_partner = lax.ppermute(precond_scale, "vert", swap)

    xe, xo, ye, yo = pl.pallas_call(
        functools.partial(pack_edges, sz),
        out_shape=[shape(edge_rows, LANES)] * 2 + [shape(PAD, LANES)] * 2,
        in_specs=[VMEM] * 3,
        out_specs=[VMEM] * 4,
        compiler_params=PARAMS,
    )(initial_guess, precond_scale, kappa_sq)

    hye = lax.ppermute(ye, "gy", even_pairs(ty))
    hyo = lax.ppermute(yo, "gy", odd_pairs(ty)) if ty > 2 else hye

    ids = jnp.asarray(lift_ids(sz))[xi, yi, vi]
    ids = ids.reshape(2, tx * sz.lift_rows, 1)
    live = jnp.arange(coarse_slots.shape[1], dtype=jnp.int32) < slot_count[0]
    slots = jnp.where(live, coarse_slots[0], -2)[None, :]
    select = jnp.where(ids[0] == slots, 1.0 / sz.mid_div, 0.0) + jnp.where(
        ids[1] == slots, 1.0 / sz.top_div, 0.0
    )
    cleaned = jnp.where(live[:, None], coarse_rows[0], 0.0)
    padded = jnp.pad(cleaned, ((0, 0), (0, sz.vec_rows * LANES - sz.nco)))
    shares = jnp.dot(select, padded, precision=lax.Precision.HIGHEST)
    shares = shares.reshape(tx, sz.lift_rows, sz.vec_rows, LANES).transpose(0, 2, 1, 3)
    shares = shares.reshape(tx, sz.vec_rows * sz.lift_rows, LANES)
    messages = {}
    for k in range(1, tx):
        messages.setdefault(tuple(paired(tx, k)), []).append(("g", shares[k]))
    messages.setdefault(tuple(even_pairs(tx)), []).append(
        ("e", jnp.concatenate([xe, hye, hyo], axis=0))
    )
    messages.setdefault(tuple(odd_pairs(tx)), []).append(
        ("o", jnp.concatenate([xo, hye, hyo], axis=0))
    )
    lift_matrix = shares[0]
    edges = {}
    for perm, parts in messages.items():
        whole = parts[0][1] if len(parts) == 1 else jnp.concatenate([p[1] for p in parts], axis=0)
        got = lax.ppermute(whole, "gx", list(perm))
        at = 0
        for kind, part in parts:
            piece = got[at : at + part.shape[0]]
            at += part.shape[0]
            if kind == "g":
                lift_matrix = lift_matrix + piece
            else:
                edges[kind] = piece

    r, c = sz.rows, sz.cols
    pair = shape(2, r, c)
    payload = shape(sz.devices, sz.head + PAD, LANES)
    parts, sent, s_ext, k_ext = pl.pallas_call(
        functools.partial(first_kernel, sz),
        out_shape=[pair, payload, shape(*sz.ext), shape(*sz.ext)],
        in_specs=[VMEM] * 9 + [SMEM, SMEM, ANY],
        out_specs=[VMEM] * 4,
        scratch_shapes=work_space(sz),
        compiler_params=PARAMS,
    )(initial_guess, precond_scale, kappa_sq, right_side, x_partner, edges["e"], edges["o"],
      hye, hyo, phi_cols, smooth_weight, phi_vals)

    def exchange(array):
        return lax.all_to_all(array, ALL, 0, 0, tiled=True)

    def apply(last, received, parts, mirrored, dots):
        return pl.pallas_call(
            functools.partial(apply_kernel, sz, last),
            out_shape=[pair, shape(sz.devices, PAD, LANES) if last else payload,
                       shape(r, c), shape(r, c), shape(PAD, LANES)],
            in_specs=[VMEM] * 7 + [SMEM, SMEM, VMEM, ANY],
            out_specs=[VMEM] * 5,
            scratch_shapes=work_space(sz),
            compiler_params=PARAMS,
        )(received, lift_matrix, parts, mirrored, s_ext, k_ext, s_partner, phi_cols,
          smooth_weight, dots, phi_vals)

    dots = jnp.zeros((PAD, LANES), F32)
    mirrored = lax.ppermute(parts, "vert", swap)
    parts, sent, residual, precond, dots = apply(False, exchange(sent), parts, mirrored, dots)
    mirrored = lax.ppermute(parts, "vert", swap)
    parts, sent, image, second, dots = apply(True, exchange(sent), parts, mirrored, dots)
    mirrored = lax.ppermute(parts, "vert", swap)
    return tuple(pl.pallas_call(
        functools.partial(final_kernel, sz),
        out_shape=[shape(1, r, c)] * 2,
        in_specs=[VMEM] * 8,
        out_specs=[VMEM] * 2,
        compiler_params=PARAMS,
    )(exchange(sent), initial_guess, residual, precond, image, second, parts, mirrored))


def solution(mesh):
    return jax.shard_map(
        local,
        mesh=mesh,
        in_specs=(
            P(("groups", "vert"), "gx", "gy"),
            P(("groups", "vert"), "gx", "gy"),
            P(("groups", "vert"), "gx", "gy"),
            P(("groups", "vert")),
            P(("groups", "vert"), "gx", "gy"),
            P(("groups", "vert"), "gx", "gy", None, None, None, None),
            P(("groups", "vert"), "gx", "gy", None, None),
            P(("groups", "gx"), None),
            P(("groups", "gx")),
            P(("groups", "gx"), None, None),
        ),
        out_specs=(P(("groups", "vert"), "gx", "gy"), P(("groups", "vert"), "gx", "gy")),
        check_vma=False,
    )
```

```python
import functools
import math

import jax
import jax.numpy as jnp
from jax import lax
from jax.experimental import pallas as pl
from jax.experimental.pallas import tpu as pltpu
from jax.sharding import PartitionSpec as P

BSIDE = 16
PATCH = 64
LANES = 128
PAD = 8
ALL = ("gx", "gy", "vert")
FIELDS = ((0, 2), (1, 2), (2, 1))
F32 = jnp.float32
VMEM = pl.BlockSpec(memory_space=pltpu.VMEM)
SMEM = pl.BlockSpec(memory_space=pltpu.SMEM)
ANY = pl.BlockSpec(memory_space=pl.ANY)
PARAMS = pltpu.CompilerParams(vmem_limit_bytes=20 * 1024 * 1024)
EDGE_PARAMS = pltpu.CompilerParams(vmem_limit_bytes=58 * 1024 * 1024)
DATA_PARAMS = pltpu.CompilerParams(vmem_limit_bytes=50 * 1024 * 1024)


class Sizes:
    def __init__(self, tx, ty, tile_shape, obs, reach, nco):
        self.tx, self.ty = tx, ty
        self.rows, self.cols = tile_shape
        self.obs, self.reach = obs, reach
        self.nco = nco
        self.px, self.py = self.rows // PATCH, self.cols // PATCH
        self.groups = self.cols // LANES
        self.ext = (self.rows + 2 * PAD, self.cols + 2 * LANES)
        self.devices = tx * ty * 2
        self.per_var = tx * ty * (1 + self.px * self.py)
        self.vec_rows = -(-nco // LANES)
        self.head = PAD * (-(-(self.vec_rows + 1) // PAD))
        self.ext_patches = (self.px + 2) * (self.py + 2)
        self.lift_rows = PAD * (-(-(self.ext_patches + self.px * self.py) // PAD))
        self.blocks = (self.rows // BSIDE) * (self.cols // BSIDE)
        self.top_div = math.sqrt(self.rows * self.cols)
        self.mid_div = float(PATCH)


def iota(shape, dim):
    return lax.broadcasted_iota(jnp.int32, shape, dim)


def lift_ids(sz, xt):
    yi, vi = lax.axis_index("gy"), lax.axis_index("vert")
    at = iota((sz.lift_rows, 1), 0)
    wide, tiles = sz.py + 2, sz.tx * sz.ty

    def steps(index, width, count):
        total = jnp.zeros_like(index)
        for a in range(1, count):
            total = total + jnp.where(index >= a * width, 1, 0)
        return total

    band = steps(at, wide, sz.px + 2)
    spot = at - band * wide
    gi, gj = xt * sz.px + band - 1, yi * sz.py + spot - 1
    near_x = xt - jnp.where(band == 0, 1, 0) + jnp.where(band == sz.px + 1, 1, 0)
    near_y = yi - jnp.where(spot == 0, 1, 0) + jnp.where(spot == sz.py + 1, 1, 0)
    inside = (near_x >= 0) & (near_x < sz.tx) & (near_y >= 0) & (near_y < sz.ty)
    mid = vi * sz.per_var + tiles + gi * (sz.ty * sz.py) + gj
    top = vi * sz.per_var + near_x * sz.ty + near_y
    mid, top = jnp.where(inside, mid, -1), jnp.where(inside, top, -1)
    rest = at - sz.ext_patches
    band = steps(rest, sz.py, sz.px)
    other = (1 - vi) * sz.per_var
    place = (xt * sz.px + band) * (sz.ty * sz.py) + yi * sz.py + rest - band * sz.py
    last = sz.ext_patches + sz.px * sz.py
    own = at < sz.ext_patches
    mid = jnp.where(own, mid, jnp.where(at < last, other + tiles + place, -1))
    top = jnp.where(own, top, jnp.where(at < last, other + xt * sz.ty + yi, -1))
    return mid, top


def share_rows(sz, slots_ref, count_ref, rows_ref, outs):
    slots = slots_ref[...]
    live = iota(slots.shape, 1) < count_ref[0]
    slots = jnp.where(live, slots, -2)
    for k, out_ref in enumerate(outs):
        mid, top = lift_ids(sz, lax.bitwise_xor(lax.axis_index("gx"), k))
        select = jnp.where(mid == slots, 1.0 / sz.mid_div, 0.0) + jnp.where(
            top == slots, 1.0 / sz.top_div, 0.0
        )
        share = jnp.dot(
            select, rows_ref[...], precision=lax.Precision.HIGHEST, preferred_element_type=F32
        )
        for i in range(sz.vec_rows):
            part = share[:, i * LANES : min((i + 1) * LANES, sz.nco)]
            if part.shape[1] < LANES:
                blank = jnp.zeros((sz.lift_rows, LANES - part.shape[1]), F32)
                part = jnp.concatenate([part, blank], axis=1)
            out_ref[pl.ds(i * sz.lift_rows, sz.lift_rows), :] = part


def setup_kernel(sz, x0_ref, s_ref, k_ref, rows_ref, slots_ref, count_ref, pay_ref, *refs):
    outs, (tiles_ref, held_ref, sems) = refs[: sz.tx], refs[sz.tx :]
    copies = [
        pltpu.make_async_copy(ref.at[0], tiles_ref.at[at], sems.at[at])
        for at, ref in enumerate((x0_ref, s_ref, k_ref))
    ]
    copies = [pltpu.make_async_copy(rows_ref.at[0], held_ref, sems.at[3])] + copies
    for copy in copies:
        copy.start()
    copies[0].wait()
    share_rows(sz, slots_ref, count_ref, held_ref, outs)
    for copy in copies[1:]:
        copy.wait()
    xi, yi, vi = lax.axis_index("gx"), lax.axis_index("gy"), lax.axis_index("vert")
    r, c, g = sz.rows, sz.cols, sz.groups
    for dx in (-1, 1):
        @pl.when((xi + dx >= 0) & (xi + dx < sz.tx))
        def _(dx=dx):
            dest = device_at(sz, xi + dx, yi, vi)
            for at, width in FIELDS:
                rows = pl.ds(0 if dx < 0 else r - width, width)
                for j in range(g):
                    pay_ref[dest, pl.ds(at * 2 * g + j * width, width), :] = tiles_ref[
                        at, rows, pl.ds(j * LANES, LANES)
                    ]

    for dy in (-1, 1):
        @pl.when((yi + dy >= 0) & (yi + dy < sz.ty))
        def _(dy=dy):
            dest = device_at(sz, xi, yi + dy, vi)
            lanes = pl.ds(0 if dy < 0 else c - LANES, LANES)
            for at, width in FIELDS:
                first = 0 if dy < 0 else LANES - width
                pay_ref[dest, pl.ds(at * 2 * g, width), :] = tiles_ref[at, :, lanes].T[
                    first : first + width
                ]

        for dx in (-1, 1):
            @pl.when((xi + dx >= 0) & (xi + dx < sz.tx) & (yi + dy >= 0) & (yi + dy < sz.ty))
            def _(dx=dx, dy=dy):
                dest = device_at(sz, xi + dx, yi + dy, vi)
                lanes = pl.ds(0 if dy < 0 else c - LANES, LANES)
                rows = pl.ds(0 if dx < 0 else r - 1, 1)
                for at, width in FIELDS:
                    if width == 2:
                        pay_ref[dest, pl.ds(at * 2 * g, 1), :] = tiles_ref[at, rows, lanes]


def put_sides(sz, ref, low, high):
    width = low.shape[0]
    zeros = jnp.zeros((LANES - width, LANES), F32)
    mid = pl.ds(PAD, sz.rows)
    ref[mid, pl.ds(0, LANES)] = jnp.concatenate([zeros, low], axis=0).T
    ref[mid, pl.ds(LANES + sz.cols, LANES)] = jnp.concatenate([high, zeros], axis=0).T


def clear_bands(sz, ref):
    blank = jnp.zeros((PAD, sz.ext[1]), F32)
    ref[pl.ds(0, PAD), :] = blank
    ref[pl.ds(PAD + sz.rows, PAD), :] = blank


def put_corners(sz, ref, beside):
    for dx in (-1, 1):
        for dy in (-1, 1):
            lanes = pl.ds(0 if dy < 0 else LANES + sz.cols, LANES)
            ref[pl.ds(PAD - 1 if dx < 0 else PAD + sz.rows, 1), lanes] = beside(dx, dy, 1)


def gather_patches(sz, v2_ref, cols_ref, chosen_ref):
    lane = iota((BSIDE, LANES), 1)
    row = iota((PAD, LANES), 0)
    diag = row == iota((PAD, LANES), 1) // BSIDE
    per_row = sz.cols // BSIDE
    per_lanes = LANES // BSIDE
    for q in range(sz.obs * sz.reach):
        m = cols_ref[0, 0, 0, q // sz.reach, q % sz.reach]
        var, n = m // sz.blocks, lax.rem(m, sz.blocks)
        i, j = n // per_row, lax.rem(n, per_row)
        at = pl.ds(pl.multiple_of(i * BSIDE, BSIDE), BSIDE)
        lanes = pl.ds(pl.multiple_of((j // per_lanes) * LANES, LANES), LANES)
        block = v2_ref[var, at, lanes]
        block = jnp.where(lane // BSIDE == lax.rem(j, per_lanes), block, 0.0)
        for step in (16, 32, 64):
            block = block + pltpu.roll(block, step, 1)
        for h in range(2):
            part = jnp.where(diag, block[h * PAD : (h + 1) * PAD], 0.0)
            chosen_ref[q // sz.reach, pl.ds(q % sz.reach, 1), pl.ds(h * LANES, LANES)] = jnp.sum(
                part, axis=0, keepdims=True
            )


def scatter_patches(sz, t_ref, cols_ref, spread_ref, sign, flat_ref=None, lift_ref=None):
    side = PATCH // BSIDE
    lifts = []
    if flat_ref is not None:
        for q in range(sz.obs * sz.reach):
            m = cols_ref[0, 0, 0, q // sz.reach, q % sz.reach]
            n = lax.rem(m, sz.blocks)
            a = (n // (sz.cols // BSIDE)) // side
            b = lax.rem(n, sz.cols // BSIDE) // side
            at = jnp.where(
                m < sz.blocks,
                (a + 1) * (sz.py + 2) + b + 1,
                sz.ext_patches + a * sz.py + b,
            )
            lifts.append(lift_ref[pl.ds(at, 1), :])
    lane = iota((PAD, LANES), 1)
    row = iota((PAD, LANES), 0)
    diag = row == lane // BSIDE
    per_row = sz.cols // BSIDE
    per_lanes = LANES // BSIDE
    for q in range(sz.obs * sz.reach):
        m = cols_ref[0, 0, 0, q // sz.reach, q % sz.reach]
        var, n = m // sz.blocks, lax.rem(m, sz.blocks)
        i, j = n // per_row, lax.rem(n, per_row)
        lanes = pl.ds(pl.multiple_of((j // per_lanes) * LANES, LANES), LANES)
        here = lane // BSIDE == lax.rem(j, per_lanes)
        for h in range(2):
            line = spread_ref[q // sz.reach, pl.ds(q % sz.reach, 1), pl.ds(h * LANES, LANES)]
            if flat_ref is not None:
                o, k = q // sz.reach, q % sz.reach
                for i_k in range(sz.reach):
                    line = line + lifts[sz.reach * o + i_k] * flat_ref[
                        o, pl.ds(sz.reach * i_k + k, 1), pl.ds(h * LANES, LANES)
                    ]
            part = jnp.where(diag, line, 0.0)
            for step in (16, 32, 64):
                part = part + pltpu.roll(part, step, 1)
            at = pl.ds(pl.multiple_of(i * BSIDE + h * PAD, PAD), PAD)
            t_ref[var, at, lanes] = t_ref[var, at, lanes] + sign * jnp.where(here, part, 0.0)


def start_phi(sz, phi_ref, buf_ref, sems):
    for o in range(sz.obs):
        pltpu.make_async_copy(phi_ref.at[0, 0, 0, o], buf_ref.at[o], sems.at[o]).start()


def observe_spread(sz, phi_ref, buf_ref, sems, chosen_ref, spread_ref, flat_ref=None):
    parts = [(k, h) for k in range(sz.reach) for h in range(BSIDE * BSIDE // LANES)]

    def body(o, carry):
        pltpu.make_async_copy(phi_ref.at[0, 0, 0, o], buf_ref.at[o], sems.at[o]).wait()

        def block(k, h):
            return buf_ref[o, k, :, pl.ds(h * LANES, LANES)]

        acc = None
        for k, h in parts:
            term = block(k, h) * chosen_ref[o, pl.ds(k, 1), pl.ds(h * LANES, LANES)]
            acc = term if acc is None else acc + term
        sources = [(spread_ref, 0, jnp.sum(acc, axis=1, keepdims=True))]
        if flat_ref is not None:
            for k in range(sz.reach):
                total = block(k, 0)
                for h in range(1, BSIDE * BSIDE // LANES):
                    total = total + block(k, h)
                sources.append((flat_ref, k, jnp.sum(total, axis=1, keepdims=True)))
        for k, h in parts:
            for ref, first, observed in sources:
                ref[o, pl.ds(sz.reach * first + k, 1), pl.ds(h * LANES, LANES)] = jnp.sum(
                    block(k, h) * observed, axis=0, keepdims=True
                )
        return carry

    lax.fori_loop(0, sz.obs, body, 0)


def smooth(sz, v2_ref, ke_ref, y_ref):
    xi, yi = lax.axis_index("gx"), lax.axis_index("gy")
    rows, cols = sz.ext
    v = v2_ref[0]
    beside = (
        pltpu.roll(v, 1, 0)
        + pltpu.roll(v, rows - 1, 0)
        + pltpu.roll(v, 1, 1)
        + pltpu.roll(v, cols - 1, 1)
    )
    y_ref[...] = (4.0 + ke_ref[...]) * v - beside

    @pl.when(xi == 0)
    def _():
        y_ref[pl.ds(0, PAD), :] = jnp.zeros((PAD, cols), F32)

    @pl.when(xi == sz.tx - 1)
    def _():
        y_ref[pl.ds(PAD + sz.rows, PAD), :] = jnp.zeros((PAD, cols), F32)

    @pl.when(yi == 0)
    def _():
        y_ref[:, pl.ds(0, LANES)] = jnp.zeros((rows, LANES), F32)

    @pl.when(yi == sz.ty - 1)
    def _():
        y_ref[:, pl.ds(LANES + sz.cols, LANES)] = jnp.zeros((rows, LANES), F32)

    inner = pl.ds(LANES, sz.cols)
    mid = y_ref[pl.ds(PAD, sz.rows), :]
    side = pltpu.roll(mid, 1, 1) + pltpu.roll(mid, cols - 1, 1)
    beside = y_ref[pl.ds(PAD - 1, sz.rows), inner] + y_ref[pl.ds(PAD + 1, sz.rows), inner]
    beside = beside + side[:, LANES : LANES + sz.cols]
    kappa = ke_ref[pl.ds(PAD, sz.rows), inner]
    return (4.0 + kappa) * mid[:, LANES : LANES + sz.cols] - beside


def device_at(sz, x, y, v):
    return (x * sz.ty + y) * 2 + v


def pack_payload(sz, t_ref, pay_ref):
    xi, yi, vi = lax.axis_index("gx"), lax.axis_index("gy"), lax.axis_index("vert")
    flat = iota((sz.head, LANES), 0) * LANES + iota((sz.head, LANES), 1)
    lane = iota((1, LANES), 1)
    vec = jnp.zeros((sz.head, LANES), F32)
    tiles = sz.tx * sz.ty
    for t in range(2):
        var = vi if t == 0 else 1 - vi
        total = jnp.zeros((1, LANES), F32)
        for a in range(sz.px):
            for j in range(sz.groups):
                seg = jnp.sum(
                    t_ref[t, pl.ds(a * PATCH, PATCH), pl.ds(j * LANES, LANES)],
                    axis=0,
                    keepdims=True,
                )
                total = total + seg
                for half in range(2):
                    keep = (lane >= PATCH) if half else (lane < PATCH)
                    value = jnp.sum(jnp.where(keep, seg, 0.0), axis=1, keepdims=True)
                    at = (
                        var * sz.per_var
                        + tiles
                        + (xi * sz.px + a) * (sz.ty * sz.py)
                        + yi * sz.py
                        + 2 * j
                        + half
                    )
                    vec = jnp.where(flat == at, value * (1.0 / sz.mid_div), vec)
        value = jnp.sum(total, axis=1, keepdims=True)
        at = var * sz.per_var + xi * sz.ty + yi
        vec = jnp.where(flat == at, value * (1.0 / sz.top_div), vec)

    def fill(s, carry):
        pay_ref[s, pl.ds(0, sz.head), :] = vec
        return carry

    lax.fori_loop(0, sz.devices, fill, 0, unroll=True if sz.devices <= 16 else 1)

    r, c = sz.rows, sz.cols
    for t in range(2):
        var = vi if t == 0 else 1 - vi
        for dx, first in ((-1, 0), (1, r - 2)):
            @pl.when((xi + dx >= 0) & (xi + dx < sz.tx))
            def _(t=t, var=var, dx=dx, first=first):
                dest = device_at(sz, xi + dx, yi, var)
                for j in range(sz.groups):
                    pay_ref[dest, pl.ds(sz.head + 2 * j, 2), :] = t_ref[
                        t, pl.ds(first, 2), pl.ds(j * LANES, LANES)
                    ]

        for dy in (-1, 1):
            @pl.when((yi + dy >= 0) & (yi + dy < sz.ty))
            def _(t=t, var=var, dy=dy):
                dest = device_at(sz, xi, yi + dy, var)
                if dy < 0:
                    pair = t_ref[t, :, pl.ds(0, LANES)].T[0:2]
                else:
                    pair = t_ref[t, :, pl.ds(c - LANES, LANES)].T[LANES - 2 : LANES]
                pay_ref[dest, pl.ds(sz.head, 2), :] = pair

            for dx in (-1, 1):
                @pl.when(
                    (xi + dx >= 0) & (xi + dx < sz.tx) & (yi + dy >= 0) & (yi + dy < sz.ty)
                )
                def _(t=t, var=var, dx=dx, dy=dy):
                    dest = device_at(sz, xi + dx, yi + dy, var)
                    lanes = pl.ds(0 if dy < 0 else c - LANES, LANES)
                    pay_ref[dest, pl.ds(sz.head, 1), :] = t_ref[
                        t, pl.ds(0 if dx < 0 else r - 1, 1), lanes
                    ]


def from_neighbour(sz, recv_ref, dx, dy, first, count, var=None):
    xi, yi = lax.axis_index("gx"), lax.axis_index("gy")
    x, y = xi + dx, yi + dy
    inside = (x >= 0) & (x < sz.tx) & (y >= 0) & (y < sz.ty)
    source = device_at(sz, jnp.clip(x, 0, sz.tx - 1), jnp.clip(y, 0, sz.ty - 1), 0)
    rows = pl.ds(first, count)
    if var is None:
        found = recv_ref[source, rows, :] + recv_ref[source + 1, rows, :]
    else:
        found = recv_ref[source + var, rows, :]
    return jnp.where(inside, found, 0.0)


def data_kernel(sz, stage, *refs):
    if stage == 0:
        x_ref, xp_ref, cols_ref, phi_ref, spread_ref = refs[:5]
        flat_ref = None
    else:
        to_ref, tm_ref, s_ref, sp_ref, cols_ref, phi_ref, spread_ref = refs[:7]
        flat_ref = refs[7] if stage == 1 else None
    v2_ref, chosen_ref, buf_ref, sems = refs[-4:]
    start_phi(sz, phi_ref, buf_ref, sems)
    if stage == 0:
        v2_ref[0] = x_ref[0]
        v2_ref[1] = xp_ref[0]
    else:
        scale = s_ref[pl.ds(PAD, sz.rows), pl.ds(LANES, sz.cols)]
        v2_ref[0] = scale * (to_ref[0] + tm_ref[1])
        v2_ref[1] = sp_ref[0] * (tm_ref[0] + to_ref[1])
    gather_patches(sz, v2_ref, cols_ref, chosen_ref)
    observe_spread(sz, phi_ref, buf_ref, sems, chosen_ref, spread_ref, flat_ref)


def first_kernel(sz, recv_ref, x0_ref, s_ref, k_ref, b_ref, spread_ref, cols_ref, w_ref,
                 t_ref, pay_ref, se_ref, ke_ref, v2_ref, y_ref):
    vi = lax.axis_index("vert")
    r, c, g = sz.rows, sz.cols, sz.groups
    mid, inner = pl.ds(PAD, r), pl.ds(LANES, c)
    for (at, width), ref, src in zip(
        FIELDS, (v2_ref.at[0], se_ref, ke_ref), (x0_ref, s_ref, k_ref)
    ):
        first = at * 2 * g
        clear_bands(sz, ref)
        ref[mid, inner] = src[0]

        def beside(dx, dy, count):
            return from_neighbour(sz, recv_ref, dx, dy, first, count, vi)

        put_sides(sz, ref, beside(0, -1, width), beside(0, 1, width))
        up, down = beside(-1, 0, width * g), beside(1, 0, width * g)
        for j in range(g):
            lanes = pl.ds(LANES + j * LANES, LANES)
            ref[pl.ds(PAD - width, width), lanes] = up[j * width : (j + 1) * width]
            ref[pl.ds(PAD + r, width), lanes] = down[j * width : (j + 1) * width]
        if width == 2:
            put_corners(sz, ref, beside)
    t_ref[0] = b_ref[0] - w_ref[0] * smooth(sz, v2_ref, ke_ref, y_ref)
    t_ref[1] = jnp.zeros((r, c), F32)
    scatter_patches(sz, t_ref, cols_ref, spread_ref, -1.0)
    pack_payload(sz, t_ref, pay_ref)


def precondition(sz, recv_ref, lg_ref, to_ref, tm_ref, se_ref, sp_ref, v2_ref, res_ref, lift_ref):
    r, c, g = sz.rows, sz.cols, sz.groups
    lane = iota((1, LANES), 1)
    mid, inner = pl.ds(PAD, r), pl.ds(LANES, c)

    def add_head(s, vec):
        return vec + recv_ref[s, pl.ds(0, sz.head), :]

    vec = lax.fori_loop(
        1, sz.devices, add_head, recv_ref[0, pl.ds(0, sz.head), :],
        unroll=True if sz.devices <= 16 else 1,
    )
    acc = None
    for i in range(sz.vec_rows):
        term = lg_ref[pl.ds(i * sz.lift_rows, sz.lift_rows), :] * vec[i : i + 1]
        acc = term if acc is None else acc + term
    lift = jnp.broadcast_to(jnp.sum(acc, axis=1, keepdims=True), (sz.lift_rows, LANES))
    lift_ref[...] = lift

    ext = v2_ref.at[0]
    clear_bands(sz, ext)
    whole = to_ref[0] + tm_ref[1]
    res_ref[...] = whole
    ext[mid, inner] = whole

    def beside(dx, dy, count):
        return from_neighbour(sz, recv_ref, dx, dy, sz.head, count)

    put_sides(sz, ext, beside(0, -1, 2), beside(0, 1, 2))
    up, down = beside(-1, 0, 2 * g), beside(1, 0, 2 * g)
    for j in range(g):
        lanes = pl.ds(LANES + j * LANES, LANES)
        ext[pl.ds(PAD - 2, 2), lanes] = up[2 * j : 2 * j + 2]
        ext[pl.ds(PAD + r, 2), lanes] = down[2 * j : 2 * j + 2]
    put_corners(sz, ext, beside)

    bands = [(0, PAD)] + [(PAD + a * PATCH, PATCH) for a in range(sz.px)] + [(PAD + r, PAD)]
    wide = sz.py + 2
    for a, (first, count) in enumerate(bands):
        rows = pl.ds(first, count)
        for j in range(g + 2):
            lanes = pl.ds(j * LANES, LANES)
            if j == 0:
                line = lift[a * wide : a * wide + 1]
            elif j == g + 1:
                line = lift[a * wide + wide - 1 : a * wide + wide]
            else:
                at = a * wide + 2 * j - 1
                line = jnp.where(lane < PATCH, lift[at : at + 1], lift[at + 1 : at + 2])
            ext[rows, lanes] = se_ref[rows, lanes] * ext[rows, lanes] + line
    for a in range(sz.px):
        rows = pl.ds(a * PATCH, PATCH)
        for j in range(g):
            lanes = pl.ds(j * LANES, LANES)
            at = sz.ext_patches + a * sz.py + 2 * j
            line = jnp.where(lane < PATCH, lift[at : at + 1], lift[at + 1 : at + 2])
            other = tm_ref[0, rows, lanes] + to_ref[1, rows, lanes]
            v2_ref[1, pl.ds(PAD + a * PATCH, PATCH), pl.ds(LANES + j * LANES, LANES)] = (
                sp_ref[0, rows, lanes] * other + line
            )


def fold(product):
    return jnp.sum(product, axis=0, keepdims=True)


def row_dot(sz, left, right):
    line = jnp.sum(left * right, axis=0, keepdims=True)
    total = line[:, 0:LANES]
    for j in range(1, sz.groups):
        total = total + line[:, j * LANES : (j + 1) * LANES]
    return total


def apply_kernel(sz, last, recv_ref, lg_ref, to_ref, tm_ref, se_ref, ke_ref, sp_ref, cols_ref,
                 w_ref, dots_ref, spread_ref, flat_ref, t_ref, pay_ref, res_ref, pre_ref,
                 out_dots_ref, v2_ref, y_ref, lift_ref):
    r, c = sz.rows, sz.cols
    mid, inner = pl.ds(PAD, r), pl.ds(LANES, c)
    precondition(sz, recv_ref, lg_ref, to_ref, tm_ref, se_ref, sp_ref, v2_ref, res_ref, lift_ref)
    t_ref[0] = w_ref[0] * smooth(sz, v2_ref, ke_ref, y_ref)
    t_ref[1] = jnp.zeros((r, c), F32)
    scatter_patches(sz, t_ref, cols_ref, spread_ref, 1.0, flat_ref, lift_ref)
    own = v2_ref[0, mid, inner]
    pre_ref[...] = own
    gamma = row_dot(sz, res_ref[...], own)
    curve = row_dot(sz, own, t_ref[0]) + row_dot(sz, v2_ref[1, mid, inner], t_ref[1])
    if last:
        lines = jnp.concatenate(
            [dots_ref[0:2], gamma, curve, jnp.zeros((PAD - 4, LANES), F32)], axis=0
        )
        out_dots_ref[...] = lines

        def fill(s, carry):
            pay_ref[s] = lines
            return carry

        lax.fori_loop(0, sz.devices, fill, 0, unroll=True if sz.devices <= 16 else 1)
    else:
        out_dots_ref[...] = jnp.concatenate(
            [gamma, curve, jnp.zeros((PAD - 2, LANES), F32)], axis=0
        )
        pack_payload(sz, t_ref, pay_ref)


def final_kernel(sz, recv_ref, x0_ref, r_ref, p_ref, w_ref, z_ref, to_ref, tm_ref, x_ref, res_ref):
    def add(s, lines):
        return lines + recv_ref[s]

    lines = lax.fori_loop(
        1, sz.devices, add, recv_ref[0], unroll=True if sz.devices <= 16 else 1
    )
    sums = jnp.sum(lines, axis=1, keepdims=True)
    gamma, delta, cross, far = (sums[i : i + 1] for i in range(4))
    step = gamma / delta
    gamma_new = step * step * cross - gamma
    growth = step * cross / delta
    curve = step * step * (far - cross * cross / delta)
    step_new = gamma_new / curve
    along = step + step_new * growth
    back = step_new * step
    x_ref[0] = x0_ref[0] + (along * p_ref[...] - back * z_ref[...])
    image = to_ref[0] + tm_ref[1]
    res_ref[0] = r_ref[...] - (along * w_ref[...] - back * image)


def shape(*dims):
    return jax.ShapeDtypeStruct(dims, F32)


def data_space(sz):
    block = BSIDE * BSIDE
    return [
        pltpu.VMEM((2, sz.rows, sz.cols), F32),
        pltpu.VMEM((sz.obs, sz.reach, block), F32),
        pltpu.VMEM((sz.obs, sz.reach, block, block), F32),
        pltpu.SemaphoreType.DMA((sz.obs,)),
    ]


def cost(micros):
    return pl.CostEstimate(flops=0, bytes_accessed=int(micros * 3.0e6), transcendentals=0)


def local(right_side, initial_guess, kappa_sq, smooth_weight, precond_scale, phi_vals, phi_cols,
          coarse_slots, slot_count, coarse_rows):
    tx, ty = lax.axis_size("gx"), lax.axis_size("gy")
    sz = Sizes(tx, ty, right_side.shape[1:], phi_vals.shape[3], phi_vals.shape[4],
               coarse_rows.shape[2])
    swap = [(0, 1), (1, 0)]
    x_partner = lax.ppermute(initial_guess, "vert", swap)
    s_partner = lax.ppermute(precond_scale, "vert", swap)

    def exchange(array):
        return lax.all_to_all(array, ALL, 0, 0, tiled=True)

    cap = coarse_slots.shape[1]
    edges, *shares = pl.pallas_call(
        functools.partial(setup_kernel, sz),
        out_shape=[shape(sz.devices, PAD * (-(-5 * sz.groups // PAD)), LANES)]
        + [shape(sz.vec_rows * sz.lift_rows, LANES)] * tx,
        in_specs=[ANY] * 4 + [VMEM, SMEM],
        out_specs=[VMEM] * (1 + tx),
        scratch_shapes=[pltpu.VMEM((3, sz.rows, sz.cols), F32), pltpu.VMEM((cap, sz.nco), F32),
                        pltpu.SemaphoreType.DMA((4,))],
        compiler_params=EDGE_PARAMS,
        cost_estimate=cost(1.5),
    )(initial_guess, precond_scale, kappa_sq, coarse_rows, coarse_slots, slot_count)
    got = [lax.ppermute(shares[k], "gx", [(i, i ^ k) for i in range(tx)]) for k in range(1, tx)]
    lift_matrix = sum(got, shares[0])
    edges = exchange(edges)

    r, c = sz.rows, sz.cols
    block = BSIDE * BSIDE
    pair = shape(2, r, c)
    payload = shape(sz.devices, sz.head + PAD, LANES)
    spread_shape = shape(sz.obs, sz.reach, block)
    flat_shape = shape(sz.obs, sz.reach * sz.reach, block)

    def data(stage, *fields):
        return pl.pallas_call(
            functools.partial(data_kernel, sz, stage),
            out_shape=[spread_shape, flat_shape] if stage == 1 else [spread_shape],
            in_specs=[VMEM] * len(fields) + [SMEM, ANY],
            out_specs=[VMEM] * (2 if stage == 1 else 1),
            scratch_shapes=data_space(sz),
            compiler_params=DATA_PARAMS,
            cost_estimate=cost(4),
        )(*fields, phi_cols, phi_vals)

    (spread,) = data(0, initial_guess, x_partner)
    parts, sent, s_ext, k_ext = pl.pallas_call(
        functools.partial(first_kernel, sz),
        out_shape=[pair, payload, shape(*sz.ext), shape(*sz.ext)],
        in_specs=[VMEM] * 6 + [SMEM, SMEM],
        out_specs=[VMEM] * 4,
        scratch_shapes=[pltpu.VMEM((1,) + sz.ext, F32), pltpu.VMEM(sz.ext, F32)],
        compiler_params=PARAMS,
        cost_estimate=cost(3),
    )(edges, initial_guess, precond_scale, kappa_sq, right_side, spread, phi_cols, smooth_weight)

    def apply(last, received, parts, mirrored, dots, spread, flat):
        return pl.pallas_call(
            functools.partial(apply_kernel, sz, last),
            out_shape=[pair, shape(sz.devices, PAD, LANES) if last else payload,
                       shape(r, c), shape(r, c), shape(PAD, LANES)],
            in_specs=[VMEM] * 7 + [SMEM, SMEM] + [VMEM] * 3,
            out_specs=[VMEM] * 5,
            scratch_shapes=[pltpu.VMEM((2,) + sz.ext, F32), pltpu.VMEM(sz.ext, F32),
                            pltpu.VMEM((sz.lift_rows, LANES), F32)],
            compiler_params=PARAMS,
            cost_estimate=cost(3),
        )(received, lift_matrix, parts, mirrored, s_ext, k_ext, s_partner, phi_cols,
          smooth_weight, dots, spread, flat)

    dots = jnp.zeros((PAD, LANES), F32)
    mirrored = lax.ppermute(parts, "vert", swap)
    received = exchange(sent)
    spread, flat = data(1, parts, mirrored, s_ext, s_partner)
    parts, sent, residual, precond, dots = apply(
        False, received, parts, mirrored, dots, spread, flat
    )
    mirrored = lax.ppermute(parts, "vert", swap)
    received = exchange(sent)
    (spread,) = data(2, parts, mirrored, s_ext, s_partner)
    parts, sent, image, second, dots = apply(
        True, received, parts, mirrored, dots, spread, flat
    )
    mirrored = lax.ppermute(parts, "vert", swap)
    return tuple(pl.pallas_call(
        functools.partial(final_kernel, sz),
        out_shape=[shape(1, r, c)] * 2,
        in_specs=[VMEM] * 8,
        out_specs=[VMEM] * 2,
        compiler_params=PARAMS,
        cost_estimate=cost(1),
    )(exchange(sent), initial_guess, residual, precond, image, second, parts, mirrored))


def solution(mesh):
    return jax.shard_map(
        local,
        mesh=mesh,
        in_specs=(
            P(("groups", "vert"), "gx", "gy"),
            P(("groups", "vert"), "gx", "gy"),
            P(("groups", "vert"), "gx", "gy"),
            P(("groups", "vert")),
            P(("groups", "vert"), "gx", "gy"),
            P(("groups", "vert"), "gx", "gy", None, None, None, None),
            P(("groups", "vert"), "gx", "gy", None, None),
            P(("groups", "gx"), None),
            P(("groups", "gx")),
            P(("groups", "gx"), None, None),
        ),
        out_specs=(P(("groups", "vert"), "gx", "gy"), P(("groups", "vert"), "gx", "gy")),
        check_vma=False,
    )
```

```python
import functools
import math

import jax
import jax.numpy as jnp
from jax import lax
from jax.experimental import pallas as pl
from jax.experimental.pallas import tpu as pltpu
from jax.sharding import PartitionSpec as P

BSIDE = 16
PATCH = 64
LANES = 128
PAD = 8
ALL = ("gx", "gy", "vert")
FIELDS = ((0, 2), (1, 2), (2, 1))
F32 = jnp.float32
VMEM = pl.BlockSpec(memory_space=pltpu.VMEM)
SMEM = pl.BlockSpec(memory_space=pltpu.SMEM)
ANY = pl.BlockSpec(memory_space=pl.ANY)
PARAMS = pltpu.CompilerParams(vmem_limit_bytes=20 * 1024 * 1024)
EDGE_PARAMS = pltpu.CompilerParams(vmem_limit_bytes=58 * 1024 * 1024)
DATA_PARAMS = pltpu.CompilerParams(vmem_limit_bytes=50 * 1024 * 1024)


class Sizes:
    def __init__(self, tx, ty, tile_shape, obs, reach, nco):
        self.tx, self.ty = tx, ty
        self.rows, self.cols = tile_shape
        self.obs, self.reach = obs, reach
        self.nco = nco
        self.px, self.py = self.rows // PATCH, self.cols // PATCH
        self.groups = self.cols // LANES
        self.ext = (self.rows + PAD, self.cols + LANES)
        self.devices = tx * ty * 2
        self.per_var = tx * ty * (1 + self.px * self.py)
        self.vec_rows = -(-nco // LANES)
        self.head = PAD * (-(-(self.vec_rows + 1) // PAD))
        self.ext_patches = (self.px + 2) * (self.py + 2)
        self.lift_rows = PAD * (-(-(self.ext_patches + self.px * self.py) // PAD))
        self.blocks = (self.rows // BSIDE) * (self.cols // BSIDE)
        self.top_div = math.sqrt(self.rows * self.cols)
        self.mid_div = float(PATCH)


def iota(shape, dim):
    return lax.broadcasted_iota(jnp.int32, shape, dim)


def lift_ids(sz, xt):
    yi, vi = lax.axis_index("gy"), lax.axis_index("vert")
    at = iota((sz.lift_rows, 1), 0)
    wide, tiles = sz.py + 2, sz.tx * sz.ty

    def steps(index, width, count):
        total = jnp.zeros_like(index)
        for a in range(1, count):
            total = total + jnp.where(index >= a * width, 1, 0)
        return total

    band = steps(at, wide, sz.px + 2)
    spot = at - band * wide
    gi, gj = xt * sz.px + band - 1, yi * sz.py + spot - 1
    near_x = xt - jnp.where(band == 0, 1, 0) + jnp.where(band == sz.px + 1, 1, 0)
    near_y = yi - jnp.where(spot == 0, 1, 0) + jnp.where(spot == sz.py + 1, 1, 0)
    inside = (near_x >= 0) & (near_x < sz.tx) & (near_y >= 0) & (near_y < sz.ty)
    mid = vi * sz.per_var + tiles + gi * (sz.ty * sz.py) + gj
    top = vi * sz.per_var + near_x * sz.ty + near_y
    mid, top = jnp.where(inside, mid, -1), jnp.where(inside, top, -1)
    rest = at - sz.ext_patches
    band = steps(rest, sz.py, sz.px)
    other = (1 - vi) * sz.per_var
    place = (xt * sz.px + band) * (sz.ty * sz.py) + yi * sz.py + rest - band * sz.py
    last = sz.ext_patches + sz.px * sz.py
    own = at < sz.ext_patches
    mid = jnp.where(own, mid, jnp.where(at < last, other + tiles + place, -1))
    top = jnp.where(own, top, jnp.where(at < last, other + xt * sz.ty + yi, -1))
    return mid, top


def share_rows(sz, slots_ref, count_ref, rows_ref, outs):
    slots = slots_ref[...]
    live = iota(slots.shape, 1) < count_ref[0]
    slots = jnp.where(live, slots, -2)
    for k, out_ref in enumerate(outs):
        mid, top = lift_ids(sz, lax.bitwise_xor(lax.axis_index("gx"), k))
        select = jnp.where(mid == slots, 1.0 / sz.mid_div, 0.0) + jnp.where(
            top == slots, 1.0 / sz.top_div, 0.0
        )
        share = jnp.dot(
            select, rows_ref[...], precision=lax.Precision.HIGHEST, preferred_element_type=F32
        )
        for i in range(sz.vec_rows):
            part = share[:, i * LANES : min((i + 1) * LANES, sz.nco)]
            if part.shape[1] < LANES:
                blank = jnp.zeros((sz.lift_rows, LANES - part.shape[1]), F32)
                part = jnp.concatenate([part, blank], axis=1)
            out_ref[pl.ds(i * sz.lift_rows, sz.lift_rows), :] = part


def setup_kernel(sz, x0_ref, s_ref, k_ref, rows_ref, slots_ref, count_ref, pay_ref, *refs):
    outs, (tiles_ref, held_ref, sems) = refs[: sz.tx], refs[sz.tx :]
    copies = [
        pltpu.make_async_copy(ref.at[0], tiles_ref.at[at], sems.at[at])
        for at, ref in enumerate((x0_ref, s_ref, k_ref))
    ]
    copies = [pltpu.make_async_copy(rows_ref.at[0], held_ref, sems.at[3])] + copies
    for copy in copies:
        copy.start()
    copies[0].wait()
    share_rows(sz, slots_ref, count_ref, held_ref, outs)
    for copy in copies[1:]:
        copy.wait()
    xi, yi, vi = lax.axis_index("gx"), lax.axis_index("gy"), lax.axis_index("vert")
    r, c, g = sz.rows, sz.cols, sz.groups
    for dx in (-1, 1):
        @pl.when((xi + dx >= 0) & (xi + dx < sz.tx))
        def _(dx=dx):
            dest = device_at(sz, xi + dx, yi, vi)
            for at, width in FIELDS:
                rows = pl.ds(0 if dx < 0 else r - width, width)
                for j in range(g):
                    pay_ref[dest, pl.ds(at * 2 * g + j * width, width), :] = tiles_ref[
                        at, rows, pl.ds(j * LANES, LANES)
                    ]

    for dy in (-1, 1):
        @pl.when((yi + dy >= 0) & (yi + dy < sz.ty))
        def _(dy=dy):
            dest = device_at(sz, xi, yi + dy, vi)
            lanes = pl.ds(0 if dy < 0 else c - LANES, LANES)
            for at, width in FIELDS:
                first = 0 if dy < 0 else LANES - width
                pay_ref[dest, pl.ds(at * 2 * g, width), :] = tiles_ref[at, :, lanes].T[
                    first : first + width
                ]

        for dx in (-1, 1):
            @pl.when((xi + dx >= 0) & (xi + dx < sz.tx) & (yi + dy >= 0) & (yi + dy < sz.ty))
            def _(dx=dx, dy=dy):
                dest = device_at(sz, xi + dx, yi + dy, vi)
                lanes = pl.ds(0 if dy < 0 else c - LANES, LANES)
                rows = pl.ds(0 if dx < 0 else r - 1, 1)
                for at, width in FIELDS:
                    if width == 2:
                        pay_ref[dest, pl.ds(at * 2 * g, 1), :] = tiles_ref[at, rows, lanes]


def put_borders(sz, ref, width, beside):
    r, c, g = sz.rows, sz.cols, sz.groups
    gap = jnp.zeros((LANES - 2 * width, LANES), F32)
    sides = [beside(0, 1, width), gap, beside(0, -1, width)]
    ref[pl.ds(0, r), pl.ds(c, LANES)] = jnp.concatenate(sides, axis=0).T
    up, down = beside(-1, 0, width * g), beside(1, 0, width * g)
    gap = jnp.zeros((PAD - 2 * width, LANES), F32)
    for j in range(g):
        rows = slice(j * width, (j + 1) * width)
        ref[pl.ds(r, PAD), pl.ds(j * LANES, LANES)] = jnp.concatenate(
            [down[rows], gap, up[rows]], axis=0
        )
    if width == 2:
        left = iota((1, LANES), 1) >= LANES // 2
        lines = [jnp.where(left, beside(dx, -1, 1), beside(dx, 1, 1)) for dx in (1, -1)]
        gap = jnp.zeros((PAD - 2, LANES), F32)
        block = jnp.concatenate([lines[0], gap, lines[1]], axis=0)
    else:
        block = jnp.zeros((PAD, LANES), F32)
    ref[pl.ds(r, PAD), pl.ds(c, LANES)] = block


def gather_patches(sz, v2_ref, cols_ref, out_ref):
    lane = iota((BSIDE, LANES), 1)
    row = iota((PAD, LANES), 0)
    diag = row == iota((PAD, LANES), 1) // BSIDE
    per_row = sz.cols // BSIDE
    per_lanes = LANES // BSIDE
    for q in range(sz.obs * sz.reach):
        m = cols_ref[0, 0, 0, q % sz.reach, q // sz.reach]
        var, n = m // sz.blocks, lax.rem(m, sz.blocks)
        i, j = n // per_row, lax.rem(n, per_row)
        at = pl.ds(pl.multiple_of(i * BSIDE, BSIDE), BSIDE)
        lanes = pl.ds(pl.multiple_of((j // per_lanes) * LANES, LANES), LANES)
        block = v2_ref[var, at, lanes]
        block = jnp.where(lane // BSIDE == lax.rem(j, per_lanes), block, 0.0)
        for step in (16, 32, 64):
            block = block + pltpu.roll(block, step, 1)
        for h in range(2):
            part = jnp.where(diag, block[h * PAD : (h + 1) * PAD], 0.0)
            out_ref[q // sz.reach, pl.ds(sz.reach + q % sz.reach, 1), pl.ds(h * LANES, LANES)] = jnp.sum(
                part, axis=0, keepdims=True
            )


def scatter_patches(sz, t_ref, cols_ref, spread_ref, sign, flat_ref=None, lift_ref=None):
    side = PATCH // BSIDE
    lifts = []
    crossed = jnp.zeros((1, LANES), F32)
    if flat_ref is not None:
        for q in range(sz.obs * sz.reach):
            m = cols_ref[0, 0, 0, q % sz.reach, q // sz.reach]
            n = lax.rem(m, sz.blocks)
            a = (n // (sz.cols // BSIDE)) // side
            b = lax.rem(n, sz.cols // BSIDE) // side
            at = jnp.where(
                m < sz.blocks,
                (a + 1) * (sz.py + 2) + b + 1,
                sz.ext_patches + a * sz.py + b,
            )
            lifts.append(lift_ref[pl.ds(at, 1), :])
    lane = iota((PAD, LANES), 1)
    row = iota((PAD, LANES), 0)
    diag = row == lane // BSIDE
    per_row = sz.cols // BSIDE
    per_lanes = LANES // BSIDE
    for q in range(sz.obs * sz.reach):
        m = cols_ref[0, 0, 0, q % sz.reach, q // sz.reach]
        var, n = m // sz.blocks, lax.rem(m, sz.blocks)
        i, j = n // per_row, lax.rem(n, per_row)
        lanes = pl.ds(pl.multiple_of((j // per_lanes) * LANES, LANES), LANES)
        here = lane // BSIDE == lax.rem(j, per_lanes)
        for h in range(2):
            line = spread_ref[q // sz.reach, pl.ds(q % sz.reach, 1), pl.ds(h * LANES, LANES)]
            if flat_ref is not None:
                o, k = q // sz.reach, q % sz.reach
                for i_k in range(sz.reach):
                    line = line + lifts[sz.reach * o + i_k] * flat_ref[
                        o, pl.ds(sz.reach * (i_k + 2) + k, 1), pl.ds(h * LANES, LANES)
                    ]
                value = spread_ref[o, pl.ds(sz.reach + k, 1), pl.ds(h * LANES, LANES)] + lifts[q]
                crossed = crossed + jnp.where(m >= sz.blocks, line * value, 0.0)
            part = jnp.where(diag, line, 0.0)
            for step in (16, 32, 64):
                part = part + pltpu.roll(part, step, 1)
            at = pl.ds(pl.multiple_of(i * BSIDE + h * PAD, PAD), PAD)
            t_ref[var, at, lanes] = t_ref[var, at, lanes] + sign * jnp.where(here, part, 0.0)
    return crossed


def start_phi(sz, phi_ref, buf_ref, sems):
    for o in range(sz.obs):
        pltpu.make_async_copy(phi_ref.at[0, 0, 0, o], buf_ref.at[o], sems.at[o]).start()


def observe_spread(sz, phi_ref, buf_ref, sems, out_ref, flat):
    parts = [(k, h) for k in range(sz.reach) for h in range(BSIDE * BSIDE // LANES)]

    def body(o, carry):
        pltpu.make_async_copy(phi_ref.at[0, 0, 0, o], buf_ref.at[o], sems.at[o]).wait()

        def block(k, h):
            return buf_ref[o, k, :, pl.ds(h * LANES, LANES)]

        acc = None
        for k, h in parts:
            term = block(k, h) * out_ref[o, pl.ds(sz.reach + k, 1), pl.ds(h * LANES, LANES)]
            acc = term if acc is None else acc + term
        sources = [(0, jnp.sum(acc, axis=1, keepdims=True))]
        if flat:
            for k in range(sz.reach):
                total = block(k, 0)
                for h in range(1, BSIDE * BSIDE // LANES):
                    total = total + block(k, h)
                sources.append((k + 2, jnp.sum(total, axis=1, keepdims=True)))
        for k, h in parts:
            for first, observed in sources:
                out_ref[o, pl.ds(sz.reach * first + k, 1), pl.ds(h * LANES, LANES)] = jnp.sum(
                    block(k, h) * observed, axis=0, keepdims=True
                )
        return carry

    lax.fori_loop(0, sz.obs, body, 0)


def smooth(sz, v_ref, ke_ref, y_ref):
    xi, yi = lax.axis_index("gx"), lax.axis_index("gy")
    r, c = sz.rows, sz.cols
    rows, cols = sz.ext
    v = v_ref[...]
    beside = (
        pltpu.roll(v, 1, 0)
        + pltpu.roll(v, rows - 1, 0)
        + pltpu.roll(v, 1, 1)
        + pltpu.roll(v, cols - 1, 1)
    )
    y_ref[...] = (4.0 + ke_ref[...]) * v - beside

    row = iota((PAD, c), 0)
    keep = ((row < PAD // 2) & (xi < sz.tx - 1)) | ((row >= PAD // 2) & (xi > 0))
    below = pl.ds(r, PAD)
    y_ref[below, pl.ds(0, c)] = jnp.where(keep, y_ref[below, pl.ds(0, c)], 0.0)
    lane = iota((r, LANES), 1)
    keep = ((lane < LANES // 2) & (yi < sz.ty - 1)) | ((lane >= LANES // 2) & (yi > 0))
    side = pl.ds(c, LANES)
    y_ref[pl.ds(0, r), side] = jnp.where(keep, y_ref[pl.ds(0, r), side], 0.0)

    wide = y_ref[pl.ds(0, r), :]
    beside = (pltpu.roll(wide, 1, 1) + pltpu.roll(wide, cols - 1, 1))[:, 0:c]
    tall = y_ref[:, pl.ds(0, c)]
    beside = beside + (pltpu.roll(tall, 1, 0) + pltpu.roll(tall, rows - 1, 0))[0:r]
    return (4.0 + ke_ref[pl.ds(0, r), pl.ds(0, c)]) * wide[:, 0:c] - beside


def device_at(sz, x, y, v):
    return (x * sz.ty + y) * 2 + v


def pack_payload(sz, t_ref, pay_ref):
    xi, yi, vi = lax.axis_index("gx"), lax.axis_index("gy"), lax.axis_index("vert")
    flat = iota((sz.head, LANES), 0) * LANES + iota((sz.head, LANES), 1)
    lane = iota((1, LANES), 1)
    vec = jnp.zeros((sz.head, LANES), F32)
    tiles = sz.tx * sz.ty
    for t in range(2):
        var = vi if t == 0 else 1 - vi
        total = jnp.zeros((1, LANES), F32)
        for a in range(sz.px):
            for j in range(sz.groups):
                seg = jnp.sum(
                    t_ref[t, pl.ds(a * PATCH, PATCH), pl.ds(j * LANES, LANES)],
                    axis=0,
                    keepdims=True,
                )
                total = total + seg
                for half in range(2):
                    keep = (lane >= PATCH) if half else (lane < PATCH)
                    value = jnp.sum(jnp.where(keep, seg, 0.0), axis=1, keepdims=True)
                    at = (
                        var * sz.per_var
                        + tiles
                        + (xi * sz.px + a) * (sz.ty * sz.py)
                        + yi * sz.py
                        + 2 * j
                        + half
                    )
                    vec = jnp.where(flat == at, value * (1.0 / sz.mid_div), vec)
        value = jnp.sum(total, axis=1, keepdims=True)
        at = var * sz.per_var + xi * sz.ty + yi
        vec = jnp.where(flat == at, value * (1.0 / sz.top_div), vec)

    def fill(s, carry):
        pay_ref[s, pl.ds(0, sz.head), :] = vec
        return carry

    lax.fori_loop(0, sz.devices, fill, 0, unroll=True if sz.devices <= 16 else 1)

    r, c = sz.rows, sz.cols
    for t in range(2):
        var = vi if t == 0 else 1 - vi
        for dx, first in ((-1, 0), (1, r - 2)):
            @pl.when((xi + dx >= 0) & (xi + dx < sz.tx))
            def _(t=t, var=var, dx=dx, first=first):
                dest = device_at(sz, xi + dx, yi, var)
                for j in range(sz.groups):
                    pay_ref[dest, pl.ds(sz.head + 2 * j, 2), :] = t_ref[
                        t, pl.ds(first, 2), pl.ds(j * LANES, LANES)
                    ]

        for dy in (-1, 1):
            @pl.when((yi + dy >= 0) & (yi + dy < sz.ty))
            def _(t=t, var=var, dy=dy):
                dest = device_at(sz, xi, yi + dy, var)
                if dy < 0:
                    pair = t_ref[t, :, pl.ds(0, LANES)].T[0:2]
                else:
                    pair = t_ref[t, :, pl.ds(c - LANES, LANES)].T[LANES - 2 : LANES]
                pay_ref[dest, pl.ds(sz.head, 2), :] = pair

            for dx in (-1, 1):
                @pl.when(
                    (xi + dx >= 0) & (xi + dx < sz.tx) & (yi + dy >= 0) & (yi + dy < sz.ty)
                )
                def _(t=t, var=var, dx=dx, dy=dy):
                    dest = device_at(sz, xi + dx, yi + dy, var)
                    lanes = pl.ds(0 if dy < 0 else c - LANES, LANES)
                    pay_ref[dest, pl.ds(sz.head, 1), :] = t_ref[
                        t, pl.ds(0 if dx < 0 else r - 1, 1), lanes
                    ]


def from_neighbour(sz, recv_ref, dx, dy, first, count, var=None):
    xi, yi = lax.axis_index("gx"), lax.axis_index("gy")
    x, y = xi + dx, yi + dy
    inside = (x >= 0) & (x < sz.tx) & (y >= 0) & (y < sz.ty)
    source = device_at(sz, jnp.clip(x, 0, sz.tx - 1), jnp.clip(y, 0, sz.ty - 1), 0)
    rows = pl.ds(first, count)
    if var is None:
        found = recv_ref[source, rows, :] + recv_ref[source + 1, rows, :]
    else:
        found = recv_ref[source + var, rows, :]
    return jnp.where(inside, found, 0.0)


def data_kernel(sz, stage, *refs):
    if stage == 0:
        x_ref, xp_ref, cols_ref, phi_ref, out_ref = refs[:5]
    else:
        to_ref, tm_ref, s_ref, sp_ref, cols_ref, phi_ref, out_ref = refs[:7]
    v2_ref, buf_ref, sems = refs[-3:]
    start_phi(sz, phi_ref, buf_ref, sems)
    if stage == 0:
        v2_ref[0] = x_ref[0]
        v2_ref[1] = xp_ref[0]
    else:
        scale = s_ref[pl.ds(0, sz.rows), pl.ds(0, sz.cols)]
        v2_ref[0] = scale * (to_ref[0] + tm_ref[1])
        v2_ref[1] = sp_ref[0] * (tm_ref[0] + to_ref[1])
    gather_patches(sz, v2_ref, cols_ref, out_ref)
    observe_spread(sz, phi_ref, buf_ref, sems, out_ref, stage == 0)


def first_kernel(sz, recv_ref, x0_ref, s_ref, k_ref, b_ref, spread_ref, cols_ref, w_ref,
                 t_ref, pay_ref, se_ref, ke_ref, v_ref, y_ref):
    vi = lax.axis_index("vert")
    r, c, g = sz.rows, sz.cols, sz.groups
    for (at, width), ref, src in zip(FIELDS, (v_ref, se_ref, ke_ref), (x0_ref, s_ref, k_ref)):
        first = at * 2 * g

        def beside(dx, dy, count):
            return from_neighbour(sz, recv_ref, dx, dy, first, count, vi)

        ref[pl.ds(0, r), pl.ds(0, c)] = src[0]
        put_borders(sz, ref, width, beside)
    t_ref[0] = b_ref[0] - w_ref[0] * smooth(sz, v_ref, ke_ref, y_ref)
    t_ref[1] = jnp.zeros((r, c), F32)
    scatter_patches(sz, t_ref, cols_ref, spread_ref, -1.0)
    pack_payload(sz, t_ref, pay_ref)


def precondition(sz, recv_ref, lg_ref, to_ref, tm_ref, se_ref, v_ref, state_ref, lift_ref):
    r, c, g = sz.rows, sz.cols, sz.groups
    lane = iota((1, LANES), 1)

    def add_head(s, vec):
        return vec + recv_ref[s, pl.ds(0, sz.head), :]

    vec = lax.fori_loop(
        1, sz.devices, add_head, recv_ref[0, pl.ds(0, sz.head), :],
        unroll=True if sz.devices <= 16 else 1,
    )
    acc = None
    for i in range(sz.vec_rows):
        term = lg_ref[pl.ds(i * sz.lift_rows, sz.lift_rows), :] * vec[i : i + 1]
        acc = term if acc is None else acc + term
    lift = jnp.broadcast_to(jnp.sum(acc, axis=1, keepdims=True), (sz.lift_rows, LANES))
    lift_ref[...] = lift

    whole = to_ref[0] + tm_ref[1]
    state_ref[0] = whole
    v_ref[pl.ds(0, r), pl.ds(0, c)] = whole

    def beside(dx, dy, count):
        return from_neighbour(sz, recv_ref, dx, dy, sz.head, count)

    put_borders(sz, v_ref, 2, beside)
    wide = sz.py + 2

    def line(band, j):
        low, high = (2 * j + 1, 2 * j + 2) if j < g else (wide - 1, 0)
        low, high = band * wide + low, band * wide + high
        return jnp.where(lane < PATCH, lift[low : low + 1], lift[high : high + 1])

    row = iota((PAD, LANES), 0)
    for j in range(g + 1):
        lanes = pl.ds(j * LANES, LANES)
        for a in range(sz.px):
            rows = pl.ds(a * PATCH, PATCH)
            v_ref[rows, lanes] = se_ref[rows, lanes] * v_ref[rows, lanes] + line(a + 1, j)
        rows = pl.ds(r, PAD)
        both = jnp.where(row < PAD // 2, line(sz.px + 1, j), line(0, j))
        v_ref[rows, lanes] = se_ref[rows, lanes] * v_ref[rows, lanes] + both


def row_dot(sz, left, right):
    line = jnp.sum(left * right, axis=0, keepdims=True)
    total = line[:, 0:LANES]
    for j in range(1, sz.groups):
        total = total + line[:, j * LANES : (j + 1) * LANES]
    return total


def apply_kernel(sz, last, recv_ref, lg_ref, to_ref, tm_ref, se_ref, ke_ref, cols_ref,
                 w_ref, dots_ref, spread_ref, flat_ref, t_ref, pay_ref, state_ref, out_dots_ref,
                 v_ref, y_ref, lift_ref):
    r, c = sz.rows, sz.cols
    precondition(sz, recv_ref, lg_ref, to_ref, tm_ref, se_ref, v_ref, state_ref, lift_ref)
    t_ref[0] = w_ref[0] * smooth(sz, v_ref, ke_ref, y_ref)
    t_ref[1] = jnp.zeros((r, c), F32)
    crossed = scatter_patches(sz, t_ref, cols_ref, spread_ref, 1.0, flat_ref, lift_ref)
    own = v_ref[pl.ds(0, r), pl.ds(0, c)]
    state_ref[1] = own
    gamma = row_dot(sz, state_ref[0], own)
    curve = row_dot(sz, own, t_ref[0]) + crossed
    if last:
        out_dots_ref[...] = dots_ref[...]
        lane = iota((1, LANES), 1)
        lines = jnp.zeros((1, LANES), F32)
        for i, part in enumerate((dots_ref[0:1], dots_ref[1:2], gamma, curve)):
            lines = jnp.where(lane == i, jnp.sum(part, axis=1, keepdims=True), lines)

        def fill(s, carry):
            pay_ref[s] = lines
            return carry

        lax.fori_loop(0, sz.devices, fill, 0, unroll=True if sz.devices <= 16 else 1)
    else:
        out_dots_ref[...] = jnp.concatenate(
            [gamma, curve, jnp.zeros((PAD - 2, LANES), F32)], axis=0
        )
        pack_payload(sz, t_ref, pay_ref)


def final_kernel(sz, recv_ref, x0_ref, rp_ref, wz_ref, to_ref, tm_ref, x_ref, res_ref):
    def add(s, lines):
        return lines + recv_ref[s]

    lines = lax.fori_loop(
        1, sz.devices, add, recv_ref[0], unroll=True if sz.devices <= 16 else 1
    )
    lane = iota((1, LANES), 1)
    gamma, delta, cross, far = (
        jnp.sum(jnp.where(lane == i, lines, 0.0), axis=1, keepdims=True) for i in range(4)
    )
    step = gamma / delta
    gamma_new = step * step * cross - gamma
    growth = step * cross / delta
    curve = step * step * (far - cross * cross / delta)
    step_new = gamma_new / curve
    along = step + step_new * growth
    back = step_new * step
    x_ref[0] = x0_ref[0] + (along * rp_ref[1] - back * wz_ref[1])
    image = to_ref[0] + tm_ref[1]
    res_ref[0] = rp_ref[0] - (along * wz_ref[0] - back * image)


def shape(*dims):
    return jax.ShapeDtypeStruct(dims, F32)


def data_space(sz):
    block = BSIDE * BSIDE
    return [
        pltpu.VMEM((2, sz.rows, sz.cols), F32),
        pltpu.VMEM((sz.obs, sz.reach, block, block), F32),
        pltpu.SemaphoreType.DMA((sz.obs,)),
    ]


def cost(micros):
    return pl.CostEstimate(flops=0, bytes_accessed=int(micros * 3.0e6), transcendentals=0)


def local(right_side, initial_guess, kappa_sq, smooth_weight, precond_scale, phi_vals, phi_cols,
          coarse_slots, slot_count, coarse_rows):
    tx, ty = lax.axis_size("gx"), lax.axis_size("gy")
    phi_cols = jnp.swapaxes(phi_cols, 3, 4)
    sz = Sizes(tx, ty, right_side.shape[1:], phi_vals.shape[3], phi_vals.shape[4],
               coarse_rows.shape[2])
    swap = [(0, 1), (1, 0)]
    x_partner = lax.ppermute(initial_guess, "vert", swap)
    s_partner = lax.ppermute(precond_scale, "vert", swap)

    def exchange(array):
        return lax.all_to_all(array, ALL, 0, 0, tiled=True)

    cap = coarse_slots.shape[1]
    edges, *shares = pl.pallas_call(
        functools.partial(setup_kernel, sz),
        out_shape=[shape(sz.devices, PAD * (-(-5 * sz.groups // PAD)), LANES)]
        + [shape(sz.vec_rows * sz.lift_rows, LANES)] * tx,
        in_specs=[ANY] * 4 + [VMEM, SMEM],
        out_specs=[VMEM] * (1 + tx),
        scratch_shapes=[pltpu.VMEM((3, sz.rows, sz.cols), F32), pltpu.VMEM((cap, sz.nco), F32),
                        pltpu.SemaphoreType.DMA((4,))],
        compiler_params=EDGE_PARAMS,
        cost_estimate=cost(1.5),
    )(initial_guess, precond_scale, kappa_sq, coarse_rows, coarse_slots, slot_count)
    got = [lax.ppermute(shares[k], "gx", [(i, i ^ k) for i in range(tx)]) for k in range(1, tx)]
    lift_matrix = sum(got, shares[0])
    edges = exchange(edges)

    r, c = sz.rows, sz.cols
    block = BSIDE * BSIDE
    pair = shape(2, r, c)
    payload = shape(sz.devices, sz.head + PAD, LANES)

    def data(stage, *fields):
        return pl.pallas_call(
            functools.partial(data_kernel, sz, stage),
            out_shape=shape(sz.obs, sz.reach * (2 + sz.reach * (stage == 0)), block),
            in_specs=[VMEM] * len(fields) + [SMEM, ANY],
            out_specs=VMEM,
            scratch_shapes=data_space(sz),
            compiler_params=DATA_PARAMS,
            cost_estimate=cost(4),
        )(*fields, phi_cols, phi_vals)

    flat = data(0, initial_guess, x_partner)
    parts, sent, s_ext, k_ext = pl.pallas_call(
        functools.partial(first_kernel, sz),
        out_shape=[pair, payload, shape(*sz.ext), shape(*sz.ext)],
        in_specs=[VMEM] * 6 + [SMEM, SMEM],
        out_specs=[VMEM] * 4,
        scratch_shapes=[pltpu.VMEM(sz.ext, F32)] * 2,
        compiler_params=PARAMS,
        cost_estimate=cost(3),
    )(edges, initial_guess, precond_scale, kappa_sq, right_side, flat, phi_cols, smooth_weight)

    def apply(last, received, parts, mirrored, dots, spread):
        return pl.pallas_call(
            functools.partial(apply_kernel, sz, last),
            out_shape=[pair, shape(sz.devices, 1, LANES) if last else payload,
                       pair, shape(PAD, LANES)],
            in_specs=[VMEM] * 6 + [SMEM, SMEM] + [VMEM] * 3,
            out_specs=[VMEM] * 4,
            scratch_shapes=[pltpu.VMEM(sz.ext, F32), pltpu.VMEM(sz.ext, F32),
                            pltpu.VMEM((sz.lift_rows, LANES), F32)],
            compiler_params=PARAMS,
            cost_estimate=cost(3),
        )(received, lift_matrix, parts, mirrored, s_ext, k_ext, phi_cols,
          smooth_weight, dots, spread, flat)

    dots = jnp.zeros((PAD, LANES), F32)
    mirrored = lax.ppermute(parts, "vert", swap)
    received = exchange(sent)
    spread = data(1, parts, mirrored, s_ext, s_partner)
    parts, sent, early, dots = apply(
        False, received, parts, mirrored, dots, spread
    )
    mirrored = lax.ppermute(parts, "vert", swap)
    received = exchange(sent)
    spread = data(2, parts, mirrored, s_ext, s_partner)
    parts, sent, late, dots = apply(
        True, received, parts, mirrored, dots, spread
    )
    mirrored = lax.ppermute(parts, "vert", swap)
    return tuple(pl.pallas_call(
        functools.partial(final_kernel, sz),
        out_shape=[shape(1, r, c)] * 2,
        in_specs=[VMEM] * 6,
        out_specs=[VMEM] * 2,
        compiler_params=PARAMS,
        cost_estimate=cost(1),
    )(exchange(sent), initial_guess, early, late, parts, mirrored))


def solution(mesh):
    return jax.shard_map(
        local,
        mesh=mesh,
        in_specs=(
            P(("groups", "vert"), "gx", "gy"),
            P(("groups", "vert"), "gx", "gy"),
            P(("groups", "vert"), "gx", "gy"),
            P(("groups", "vert")),
            P(("groups", "vert"), "gx", "gy"),
            P(("groups", "vert"), "gx", "gy", None, None, None, None),
            P(("groups", "vert"), "gx", "gy", None, None),
            P(("groups", "gx"), None),
            P(("groups", "gx")),
            P(("groups", "gx"), None, None),
        ),
        out_specs=(P(("groups", "vert"), "gx", "gy"), P(("groups", "vert"), "gx", "gy")),
        check_vma=False,
    )
```

```python
import functools
import math

import jax
import jax.numpy as jnp
from jax import lax
from jax.experimental import pallas as pl
from jax.experimental.pallas import tpu as pltpu
from jax.sharding import PartitionSpec as P

BSIDE = 16
PATCH = 64
LANES = 128
PAD = 8
ALL = ("gx", "gy", "vert")
FIELDS = ((0, 2), (1, 2), (2, 1))
F32 = jnp.float32
VMEM = pl.BlockSpec(memory_space=pltpu.VMEM)
SMEM = pl.BlockSpec(memory_space=pltpu.SMEM)
ANY = pl.BlockSpec(memory_space=pl.ANY)
PARAMS = pltpu.CompilerParams(vmem_limit_bytes=20 * 1024 * 1024)
EDGE_PARAMS = pltpu.CompilerParams(vmem_limit_bytes=58 * 1024 * 1024)
DATA_PARAMS = pltpu.CompilerParams(vmem_limit_bytes=50 * 1024 * 1024)


class Sizes:
    def __init__(self, tx, ty, tile_shape, obs, reach, nco):
        self.tx, self.ty = tx, ty
        self.rows, self.cols = tile_shape
        self.obs, self.reach = obs, reach
        self.nco = nco
        self.px, self.py = self.rows // PATCH, self.cols // PATCH
        self.groups = self.cols // LANES
        self.ext = (self.rows + PAD, self.cols + LANES)
        self.devices = tx * ty * 2
        self.per_var = tx * ty * (1 + self.px * self.py)
        self.vec_rows = -(-nco // LANES)
        self.head = PAD * (-(-(self.vec_rows + 1) // PAD))
        self.ext_patches = (self.px + 2) * (self.py + 2)
        self.lift_rows = PAD * (-(-(self.ext_patches + self.px * self.py) // PAD))
        self.blocks = (self.rows // BSIDE) * (self.cols // BSIDE)
        self.top_div = math.sqrt(self.rows * self.cols)
        self.mid_div = float(PATCH)


def iota(shape, dim):
    return lax.broadcasted_iota(jnp.int32, shape, dim)


def lift_ids(sz, xt):
    yi, vi = lax.axis_index("gy"), lax.axis_index("vert")
    at = iota((sz.lift_rows, 1), 0)
    wide, tiles = sz.py + 2, sz.tx * sz.ty

    def steps(index, width, count):
        total = jnp.zeros_like(index)
        for a in range(1, count):
            total = total + jnp.where(index >= a * width, 1, 0)
        return total

    band = steps(at, wide, sz.px + 2)
    spot = at - band * wide
    gi, gj = xt * sz.px + band - 1, yi * sz.py + spot - 1
    near_x = xt - jnp.where(band == 0, 1, 0) + jnp.where(band == sz.px + 1, 1, 0)
    near_y = yi - jnp.where(spot == 0, 1, 0) + jnp.where(spot == sz.py + 1, 1, 0)
    inside = (near_x >= 0) & (near_x < sz.tx) & (near_y >= 0) & (near_y < sz.ty)
    mid = vi * sz.per_var + tiles + gi * (sz.ty * sz.py) + gj
    top = vi * sz.per_var + near_x * sz.ty + near_y
    mid, top = jnp.where(inside, mid, -1), jnp.where(inside, top, -1)
    rest = at - sz.ext_patches
    band = steps(rest, sz.py, sz.px)
    other = (1 - vi) * sz.per_var
    place = (xt * sz.px + band) * (sz.ty * sz.py) + yi * sz.py + rest - band * sz.py
    last = sz.ext_patches + sz.px * sz.py
    own = at < sz.ext_patches
    mid = jnp.where(own, mid, jnp.where(at < last, other + tiles + place, -1))
    top = jnp.where(own, top, jnp.where(at < last, other + xt * sz.ty + yi, -1))
    return mid, top


def share_rows(sz, slots_ref, count_ref, rows_ref, outs):
    slots = slots_ref[...]
    live = iota(slots.shape, 1) < count_ref[0]
    slots = jnp.where(live, slots, -2)
    for k, out_ref in enumerate(outs):
        mid, top = lift_ids(sz, lax.bitwise_xor(lax.axis_index("gx"), k))
        select = jnp.where(mid == slots, 1.0 / sz.mid_div, 0.0) + jnp.where(
            top == slots, 1.0 / sz.top_div, 0.0
        )
        share = jnp.dot(
            select, rows_ref[...], precision=lax.Precision.HIGHEST, preferred_element_type=F32
        )
        for i in range(sz.vec_rows):
            part = share[:, i * LANES : min((i + 1) * LANES, sz.nco)]
            if part.shape[1] < LANES:
                blank = jnp.zeros((sz.lift_rows, LANES - part.shape[1]), F32)
                part = jnp.concatenate([part, blank], axis=1)
            out_ref[pl.ds(i * sz.lift_rows, sz.lift_rows), :] = part


def put_rows(pay_ref, dest, first, block):
    for i in range(block.shape[0]):
        pay_ref[dest, first + i] = block[i : i + 1]


def setup_kernel(sz, x0_ref, s_ref, k_ref, rows_ref, slots_ref, count_ref, pay_ref, *refs):
    outs, (tiles_ref, held_ref, sems) = refs[: sz.tx], refs[sz.tx :]
    copies = [
        pltpu.make_async_copy(ref.at[0], tiles_ref.at[at], sems.at[at])
        for at, ref in enumerate((x0_ref, s_ref, k_ref))
    ]
    copies = [pltpu.make_async_copy(rows_ref.at[0], held_ref, sems.at[3])] + copies
    for copy in copies:
        copy.start()
    copies[0].wait()
    share_rows(sz, slots_ref, count_ref, held_ref, outs)
    for copy in copies[1:]:
        copy.wait()
    xi, yi, vi = lax.axis_index("gx"), lax.axis_index("gy"), lax.axis_index("vert")
    r, c, g = sz.rows, sz.cols, sz.groups
    for dx in (-1, 1):
        @pl.when((xi + dx >= 0) & (xi + dx < sz.tx))
        def _(dx=dx):
            dest = device_at(sz, xi + dx, yi, vi)
            for at, width in FIELDS:
                rows = pl.ds(0 if dx < 0 else r - width, width)
                for j in range(g):
                    put_rows(
                        pay_ref, dest, at * 2 * g + j * width,
                        tiles_ref[at, rows, pl.ds(j * LANES, LANES)],
                    )

    for dy in (-1, 1):
        @pl.when((yi + dy >= 0) & (yi + dy < sz.ty))
        def _(dy=dy):
            dest = device_at(sz, xi, yi + dy, vi)
            lanes = pl.ds(0 if dy < 0 else c - LANES, LANES)
            for at, width in FIELDS:
                first = 0 if dy < 0 else LANES - width
                pair = tiles_ref[at, :, lanes].T[first : first + width]
                put_rows(pay_ref, dest, at * 2 * g, pair)

        for dx in (-1, 1):
            @pl.when((xi + dx >= 0) & (xi + dx < sz.tx) & (yi + dy >= 0) & (yi + dy < sz.ty))
            def _(dx=dx, dy=dy):
                dest = device_at(sz, xi + dx, yi + dy, vi)
                lanes = pl.ds(0 if dy < 0 else c - LANES, LANES)
                rows = pl.ds(0 if dx < 0 else r - 1, 1)
                for at, width in FIELDS:
                    if width == 2:
                        put_rows(pay_ref, dest, at * 2 * g, tiles_ref[at, rows, lanes])


def put_borders(sz, ref, width, beside):
    r, c, g = sz.rows, sz.cols, sz.groups
    gap = jnp.zeros((LANES - 2 * width, LANES), F32)
    sides = [beside(0, 1, width), gap, beside(0, -1, width)]
    ref[pl.ds(0, r), pl.ds(c, LANES)] = jnp.concatenate(sides, axis=0).T
    up, down = beside(-1, 0, width * g), beside(1, 0, width * g)
    gap = jnp.zeros((PAD - 2 * width, LANES), F32)
    for j in range(g):
        rows = slice(j * width, (j + 1) * width)
        ref[pl.ds(r, PAD), pl.ds(j * LANES, LANES)] = jnp.concatenate(
            [down[rows], gap, up[rows]], axis=0
        )
    if width == 2:
        left = iota((1, LANES), 1) >= LANES // 2
        lines = [jnp.where(left, beside(dx, -1, 1), beside(dx, 1, 1)) for dx in (1, -1)]
        gap = jnp.zeros((PAD - 2, LANES), F32)
        block = jnp.concatenate([lines[0], gap, lines[1]], axis=0)
    else:
        block = jnp.zeros((PAD, LANES), F32)
    ref[pl.ds(r, PAD), pl.ds(c, LANES)] = block


def gather_patches(sz, v2_ref, cols_ref, out_ref):
    lane = iota((BSIDE, LANES), 1)
    row = iota((PAD, LANES), 0)
    diag = row == iota((PAD, LANES), 1) // BSIDE
    per_row = sz.cols // BSIDE
    per_lanes = LANES // BSIDE
    for q in range(sz.obs * sz.reach):
        m = cols_ref[0, 0, 0, q % sz.reach, q // sz.reach]
        var, n = m // sz.blocks, lax.rem(m, sz.blocks)
        i, j = n // per_row, lax.rem(n, per_row)
        at = pl.ds(pl.multiple_of(i * BSIDE, BSIDE), BSIDE)
        lanes = pl.ds(pl.multiple_of((j // per_lanes) * LANES, LANES), LANES)
        block = v2_ref[var, at, lanes]
        block = jnp.where(lane // BSIDE == lax.rem(j, per_lanes), block, 0.0)
        for step in (16, 32, 64):
            block = block + pltpu.roll(block, step, 1)
        for h in range(2):
            part = jnp.where(diag, block[h * PAD : (h + 1) * PAD], 0.0)
            out_ref[q // sz.reach, pl.ds(sz.reach + q % sz.reach, 1), pl.ds(h * LANES, LANES)] = jnp.sum(
                part, axis=0, keepdims=True
            )


def scatter_patches(sz, t_ref, cols_ref, spread_ref, sign, flat_ref=None, lift_ref=None):
    side = PATCH // BSIDE
    lifts = []
    crossed = jnp.zeros((1, LANES), F32)
    if flat_ref is not None:
        for q in range(sz.obs * sz.reach):
            m = cols_ref[0, 0, 0, q % sz.reach, q // sz.reach]
            n = lax.rem(m, sz.blocks)
            a = (n // (sz.cols // BSIDE)) // side
            b = lax.rem(n, sz.cols // BSIDE) // side
            at = jnp.where(
                m < sz.blocks,
                (a + 1) * (sz.py + 2) + b + 1,
                sz.ext_patches + a * sz.py + b,
            )
            lifts.append(lift_ref[pl.ds(at, 1), :])
    lane = iota((PAD, LANES), 1)
    row = iota((PAD, LANES), 0)
    diag = row == lane // BSIDE
    per_row = sz.cols // BSIDE
    per_lanes = LANES // BSIDE
    for q in range(sz.obs * sz.reach):
        m = cols_ref[0, 0, 0, q % sz.reach, q // sz.reach]
        var, n = m // sz.blocks, lax.rem(m, sz.blocks)
        i, j = n // per_row, lax.rem(n, per_row)
        lanes = pl.ds(pl.multiple_of((j // per_lanes) * LANES, LANES), LANES)
        here = lane // BSIDE == lax.rem(j, per_lanes)
        both = []
        for h in range(2):
            line = spread_ref[q // sz.reach, pl.ds(q % sz.reach, 1), pl.ds(h * LANES, LANES)]
            if flat_ref is not None:
                o, k = q // sz.reach, q % sz.reach
                for i_k in range(sz.reach):
                    line = line + lifts[sz.reach * o + i_k] * flat_ref[
                        o, pl.ds(sz.reach * (i_k + 2) + k, 1), pl.ds(h * LANES, LANES)
                    ]
                value = spread_ref[o, pl.ds(sz.reach + k, 1), pl.ds(h * LANES, LANES)] + lifts[q]
                crossed = crossed + jnp.where(m >= sz.blocks, line * value, 0.0)
            part = jnp.where(diag, line, 0.0)
            for step in (16, 32, 64):
                part = part + pltpu.roll(part, step, 1)
            both.append(jnp.where(here, part, 0.0))
        at = pl.ds(pl.multiple_of(i * BSIDE, BSIDE), BSIDE)
        t_ref[var, at, lanes] = t_ref[var, at, lanes] + sign * jnp.concatenate(both, axis=0)
    return crossed


def start_phi(sz, phi_ref, buf_ref, sems):
    for o in range(sz.obs):
        pltpu.make_async_copy(phi_ref.at[0, 0, 0, o], buf_ref.at[o], sems.at[o]).start()


def observe_spread(sz, phi_ref, buf_ref, sems, out_ref, flat):
    parts = [(k, h) for k in range(sz.reach) for h in range(BSIDE * BSIDE // LANES)]

    def body(o, carry):
        pltpu.make_async_copy(phi_ref.at[0, 0, 0, o], buf_ref.at[o], sems.at[o]).wait()

        def block(k, h):
            return buf_ref[o, k, :, pl.ds(h * LANES, LANES)]

        acc = None
        for k, h in parts:
            term = block(k, h) * out_ref[o, pl.ds(sz.reach + k, 1), pl.ds(h * LANES, LANES)]
            acc = term if acc is None else acc + term
        sources = [(0, jnp.sum(acc, axis=1, keepdims=True))]
        if flat:
            for k in range(sz.reach):
                total = block(k, 0)
                for h in range(1, BSIDE * BSIDE // LANES):
                    total = total + block(k, h)
                sources.append((k + 2, jnp.sum(total, axis=1, keepdims=True)))
        for k, h in parts:
            for first, observed in sources:
                out_ref[o, pl.ds(sz.reach * first + k, 1), pl.ds(h * LANES, LANES)] = jnp.sum(
                    block(k, h) * observed, axis=0, keepdims=True
                )
        return carry

    lax.fori_loop(0, sz.obs, body, 0)


def smooth(sz, v_ref, ke_ref, y_ref):
    xi, yi = lax.axis_index("gx"), lax.axis_index("gy")
    r, c = sz.rows, sz.cols
    rows, cols = sz.ext
    v = v_ref[...]
    beside = (
        pltpu.roll(v, 1, 0)
        + pltpu.roll(v, rows - 1, 0)
        + pltpu.roll(v, 1, 1)
        + pltpu.roll(v, cols - 1, 1)
    )
    y_ref[...] = (4.0 + ke_ref[...]) * v - beside

    row = iota((PAD, c), 0)
    keep = ((row < PAD // 2) & (xi < sz.tx - 1)) | ((row >= PAD // 2) & (xi > 0))
    below = pl.ds(r, PAD)
    y_ref[below, pl.ds(0, c)] = jnp.where(keep, y_ref[below, pl.ds(0, c)], 0.0)
    lane = iota((r, LANES), 1)
    keep = ((lane < LANES // 2) & (yi < sz.ty - 1)) | ((lane >= LANES // 2) & (yi > 0))
    side = pl.ds(c, LANES)
    y_ref[pl.ds(0, r), side] = jnp.where(keep, y_ref[pl.ds(0, r), side], 0.0)

    wide = y_ref[pl.ds(0, r), :]
    beside = (pltpu.roll(wide, 1, 1) + pltpu.roll(wide, cols - 1, 1))[:, 0:c]
    tall = y_ref[:, pl.ds(0, c)]
    beside = beside + (pltpu.roll(tall, 1, 0) + pltpu.roll(tall, rows - 1, 0))[0:r]
    return (4.0 + ke_ref[pl.ds(0, r), pl.ds(0, c)]) * wide[:, 0:c] - beside


def device_at(sz, x, y, v):
    return (x * sz.ty + y) * 2 + v


def pack_payload(sz, t_ref, pay_ref):
    xi, yi, vi = lax.axis_index("gx"), lax.axis_index("gy"), lax.axis_index("vert")
    flat = iota((sz.head, LANES), 0) * LANES + iota((sz.head, LANES), 1)
    lane = iota((1, LANES), 1)
    vec = jnp.zeros((sz.head, LANES), F32)
    tiles = sz.tx * sz.ty
    for t in range(2):
        var = vi if t == 0 else 1 - vi
        total = jnp.zeros((1, LANES), F32)
        for a in range(sz.px):
            for j in range(sz.groups):
                seg = jnp.sum(
                    t_ref[t, pl.ds(a * PATCH, PATCH), pl.ds(j * LANES, LANES)],
                    axis=0,
                    keepdims=True,
                )
                total = total + seg
                for half in range(2):
                    keep = (lane >= PATCH) if half else (lane < PATCH)
                    value = jnp.sum(jnp.where(keep, seg, 0.0), axis=1, keepdims=True)
                    at = (
                        var * sz.per_var
                        + tiles
                        + (xi * sz.px + a) * (sz.ty * sz.py)
                        + yi * sz.py
                        + 2 * j
                        + half
                    )
                    vec = jnp.where(flat == at, value * (1.0 / sz.mid_div), vec)
        value = jnp.sum(total, axis=1, keepdims=True)
        at = var * sz.per_var + xi * sz.ty + yi
        vec = jnp.where(flat == at, value * (1.0 / sz.top_div), vec)

    def fill(s, carry):
        pay_ref[s, pl.ds(0, sz.head), :] = vec
        return carry

    lax.fori_loop(0, sz.devices, fill, 0, unroll=True if sz.devices <= 16 else 1)

    r, c = sz.rows, sz.cols
    for t in range(2):
        var = vi if t == 0 else 1 - vi
        for dx, first in ((-1, 0), (1, r - 2)):
            @pl.when((xi + dx >= 0) & (xi + dx < sz.tx))
            def _(t=t, var=var, dx=dx, first=first):
                dest = device_at(sz, xi + dx, yi, var)
                for j in range(sz.groups):
                    pay_ref[dest, pl.ds(sz.head + 2 * j, 2), :] = t_ref[
                        t, pl.ds(first, 2), pl.ds(j * LANES, LANES)
                    ]

        for dy in (-1, 1):
            @pl.when((yi + dy >= 0) & (yi + dy < sz.ty))
            def _(t=t, var=var, dy=dy):
                dest = device_at(sz, xi, yi + dy, var)
                if dy < 0:
                    pair = t_ref[t, :, pl.ds(0, LANES)].T[0:2]
                else:
                    pair = t_ref[t, :, pl.ds(c - LANES, LANES)].T[LANES - 2 : LANES]
                pay_ref[dest, pl.ds(sz.head, 2), :] = pair

            for dx in (-1, 1):
                @pl.when(
                    (xi + dx >= 0) & (xi + dx < sz.tx) & (yi + dy >= 0) & (yi + dy < sz.ty)
                )
                def _(t=t, var=var, dx=dx, dy=dy):
                    dest = device_at(sz, xi + dx, yi + dy, var)
                    lanes = pl.ds(0 if dy < 0 else c - LANES, LANES)
                    pay_ref[dest, pl.ds(sz.head, 1), :] = t_ref[
                        t, pl.ds(0 if dx < 0 else r - 1, 1), lanes
                    ]


def from_neighbour(sz, recv_ref, dx, dy, first, count, var=None):
    xi, yi = lax.axis_index("gx"), lax.axis_index("gy")
    x, y = xi + dx, yi + dy
    inside = (x >= 0) & (x < sz.tx) & (y >= 0) & (y < sz.ty)
    source = device_at(sz, jnp.clip(x, 0, sz.tx - 1), jnp.clip(y, 0, sz.ty - 1), 0)
    rows = pl.ds(first, count)
    if var is None:
        found = recv_ref[source, rows, :] + recv_ref[source + 1, rows, :]
    else:
        found = [recv_ref[source + var, row] for row in range(first, first + count)]
        found = jnp.concatenate(found, axis=0)
    return jnp.where(inside, found, 0.0)


def data_kernel(sz, stage, *refs):
    if stage == 0:
        x_ref, xp_ref, cols_ref, phi_ref, out_ref = refs[:5]
    else:
        to_ref, tm_ref, s_ref, sp_ref, cols_ref, phi_ref, out_ref = refs[:7]
    v2_ref, buf_ref, sems = refs[-3:]
    start_phi(sz, phi_ref, buf_ref, sems)
    if stage == 0:
        v2_ref[0] = x_ref[0]
        v2_ref[1] = xp_ref[0]
    else:
        scale = s_ref[pl.ds(0, sz.rows), pl.ds(0, sz.cols)]
        v2_ref[0] = scale * (to_ref[0] + tm_ref[1])
        v2_ref[1] = sp_ref[0] * (tm_ref[0] + to_ref[1])
    gather_patches(sz, v2_ref, cols_ref, out_ref)
    observe_spread(sz, phi_ref, buf_ref, sems, out_ref, stage == 1)


def first_kernel(sz, recv_ref, x0_ref, s_ref, k_ref, b_ref, spread_ref, cols_ref, w_ref,
                 t_ref, pay_ref, se_ref, ke_ref, v_ref, y_ref):
    vi = lax.axis_index("vert")
    r, c, g = sz.rows, sz.cols, sz.groups
    for (at, width), ref, src in zip(FIELDS, (v_ref, se_ref, ke_ref), (x0_ref, s_ref, k_ref)):
        first = at * 2 * g

        def beside(dx, dy, count):
            return from_neighbour(sz, recv_ref, dx, dy, first, count, vi)

        ref[pl.ds(0, r), pl.ds(0, c)] = src[0]
        put_borders(sz, ref, width, beside)
    t_ref[0] = b_ref[0] - w_ref[0] * smooth(sz, v_ref, ke_ref, y_ref)
    t_ref[1] = jnp.zeros((r, c), F32)
    scatter_patches(sz, t_ref, cols_ref, spread_ref, -1.0)
    pack_payload(sz, t_ref, pay_ref)


def precondition(sz, recv_ref, lg_ref, to_ref, tm_ref, se_ref, v_ref, state_ref, lift_ref):
    r, c, g = sz.rows, sz.cols, sz.groups
    lane = iota((1, LANES), 1)

    def add_head(s, vec):
        return vec + recv_ref[s, pl.ds(0, sz.head), :]

    vec = lax.fori_loop(
        1, sz.devices, add_head, recv_ref[0, pl.ds(0, sz.head), :],
        unroll=True if sz.devices <= 16 else 1,
    )
    acc = None
    for i in range(sz.vec_rows):
        term = lg_ref[pl.ds(i * sz.lift_rows, sz.lift_rows), :] * vec[i : i + 1]
        acc = term if acc is None else acc + term
    lift = jnp.broadcast_to(jnp.sum(acc, axis=1, keepdims=True), (sz.lift_rows, LANES))
    lift_ref[...] = lift

    whole = to_ref[0] + tm_ref[1]
    state_ref[0] = whole
    v_ref[pl.ds(0, r), pl.ds(0, c)] = whole

    def beside(dx, dy, count):
        return from_neighbour(sz, recv_ref, dx, dy, sz.head, count)

    put_borders(sz, v_ref, 2, beside)
    wide = sz.py + 2

    def line(band, j):
        low, high = (2 * j + 1, 2 * j + 2) if j < g else (wide - 1, 0)
        low, high = band * wide + low, band * wide + high
        return jnp.where(lane < PATCH, lift[low : low + 1], lift[high : high + 1])

    row = iota((PAD, LANES), 0)
    for j in range(g + 1):
        lanes = pl.ds(j * LANES, LANES)
        for a in range(sz.px):
            rows = pl.ds(a * PATCH, PATCH)
            v_ref[rows, lanes] = se_ref[rows, lanes] * v_ref[rows, lanes] + line(a + 1, j)
        rows = pl.ds(r, PAD)
        both = jnp.where(row < PAD // 2, line(sz.px + 1, j), line(0, j))
        v_ref[rows, lanes] = se_ref[rows, lanes] * v_ref[rows, lanes] + both


def row_dot(sz, left, right):
    line = jnp.sum(left * right, axis=0, keepdims=True)
    total = line[:, 0:LANES]
    for j in range(1, sz.groups):
        total = total + line[:, j * LANES : (j + 1) * LANES]
    return total


def apply_kernel(sz, last, recv_ref, lg_ref, to_ref, tm_ref, se_ref, ke_ref, cols_ref,
                 w_ref, dots_ref, spread_ref, flat_ref, t_ref, pay_ref, state_ref, out_dots_ref,
                 v_ref, y_ref, lift_ref):
    r, c = sz.rows, sz.cols
    precondition(sz, recv_ref, lg_ref, to_ref, tm_ref, se_ref, v_ref, state_ref, lift_ref)
    t_ref[0] = w_ref[0] * smooth(sz, v_ref, ke_ref, y_ref)
    t_ref[1] = jnp.zeros((r, c), F32)
    crossed = scatter_patches(sz, t_ref, cols_ref, spread_ref, 1.0, flat_ref, lift_ref)
    own = v_ref[pl.ds(0, r), pl.ds(0, c)]
    state_ref[1] = own
    gamma = row_dot(sz, state_ref[0], own)
    curve = row_dot(sz, own, t_ref[0]) + crossed
    if last:
        out_dots_ref[...] = dots_ref[...]
        lane = iota((1, LANES), 1)
        lines = jnp.zeros((1, LANES), F32)
        for i, part in enumerate((dots_ref[0:1], dots_ref[1:2], gamma, curve)):
            lines = jnp.where(lane == i, jnp.sum(part, axis=1, keepdims=True), lines)

        def fill(s, carry):
            pay_ref[s] = lines
            return carry

        lax.fori_loop(0, sz.devices, fill, 0, unroll=True if sz.devices <= 16 else 1)
    else:
        out_dots_ref[...] = jnp.concatenate(
            [gamma, curve, jnp.zeros((PAD - 2, LANES), F32)], axis=0
        )
        pack_payload(sz, t_ref, pay_ref)


def final_kernel(sz, recv_ref, x0_ref, rp_ref, wz_ref, to_ref, tm_ref, x_ref, res_ref):
    def add(s, lines):
        return lines + recv_ref[s]

    lines = lax.fori_loop(
        1, sz.devices, add, recv_ref[0], unroll=True if sz.devices <= 16 else 1
    )
    lane = iota((1, LANES), 1)
    gamma, delta, cross, far = (
        jnp.sum(jnp.where(lane == i, lines, 0.0), axis=1, keepdims=True) for i in range(4)
    )
    step = gamma / delta
    gamma_new = step * step * cross - gamma
    growth = step * cross / delta
    curve = step * step * (far - cross * cross / delta)
    step_new = gamma_new / curve
    along = step + step_new * growth
    back = step_new * step
    x_ref[0] = x0_ref[0] + (along * rp_ref[1] - back * wz_ref[1])
    image = to_ref[0] + tm_ref[1]
    res_ref[0] = rp_ref[0] - (along * wz_ref[0] - back * image)


def shape(*dims):
    return jax.ShapeDtypeStruct(dims, F32)


def data_space(sz):
    block = BSIDE * BSIDE
    return [
        pltpu.VMEM((2, sz.rows, sz.cols), F32),
        pltpu.VMEM((sz.obs, sz.reach, block, block), F32),
        pltpu.SemaphoreType.DMA((sz.obs,)),
    ]


def cost(micros):
    return pl.CostEstimate(flops=0, bytes_accessed=int(micros * 3.0e6), transcendentals=0)


def local(right_side, initial_guess, kappa_sq, smooth_weight, precond_scale, phi_vals, phi_cols,
          coarse_slots, slot_count, coarse_rows):
    tx, ty = lax.axis_size("gx"), lax.axis_size("gy")
    phi_cols = jnp.swapaxes(phi_cols, 3, 4)
    sz = Sizes(tx, ty, right_side.shape[1:], phi_vals.shape[3], phi_vals.shape[4],
               coarse_rows.shape[2])
    swap = [(0, 1), (1, 0)]
    x_partner = lax.ppermute(initial_guess, "vert", swap)
    s_partner = lax.ppermute(precond_scale, "vert", swap)

    def exchange(array):
        return lax.all_to_all(array, ALL, 0, 0, tiled=True)

    cap = coarse_slots.shape[1]
    edges, *shares = pl.pallas_call(
        functools.partial(setup_kernel, sz),
        out_shape=[shape(sz.devices, 5 * sz.groups, 1, LANES)]
        + [shape(sz.vec_rows * sz.lift_rows, LANES)] * tx,
        in_specs=[ANY] * 4 + [VMEM, SMEM],
        out_specs=[VMEM] * (1 + tx),
        scratch_shapes=[pltpu.VMEM((3, sz.rows, sz.cols), F32), pltpu.VMEM((cap, sz.nco), F32),
                        pltpu.SemaphoreType.DMA((4,))],
        compiler_params=EDGE_PARAMS,
        cost_estimate=cost(1.5),
    )(initial_guess, precond_scale, kappa_sq, coarse_rows, coarse_slots, slot_count)
    got = [lax.ppermute(shares[k], "gx", [(i, i ^ k) for i in range(tx)]) for k in range(1, tx)]
    lift_matrix = sum(got, shares[0])
    edges, x_partner = lax.optimization_barrier((edges, x_partner))
    edges = exchange(edges)

    r, c = sz.rows, sz.cols
    block = BSIDE * BSIDE
    pair = shape(2, r, c)
    payload = shape(sz.devices, sz.head + PAD, LANES)

    def data(stage, *fields):
        return pl.pallas_call(
            functools.partial(data_kernel, sz, stage),
            out_shape=shape(sz.obs, sz.reach * (2 + sz.reach * (stage == 1)), block),
            in_specs=[VMEM] * len(fields) + [SMEM, ANY],
            out_specs=VMEM,
            scratch_shapes=data_space(sz),
            compiler_params=DATA_PARAMS,
            cost_estimate=cost(4),
        )(*fields, phi_cols, phi_vals)

    first_spread = data(0, initial_guess, x_partner)
    parts, sent, s_ext, k_ext = pl.pallas_call(
        functools.partial(first_kernel, sz),
        out_shape=[pair, payload, shape(*sz.ext), shape(*sz.ext)],
        in_specs=[VMEM] * 6 + [SMEM, SMEM],
        out_specs=[VMEM] * 4,
        scratch_shapes=[pltpu.VMEM(sz.ext, F32)] * 2,
        compiler_params=PARAMS,
        cost_estimate=cost(3),
    )(edges, initial_guess, precond_scale, kappa_sq, right_side, first_spread, phi_cols, smooth_weight)

    def apply(last, received, parts, mirrored, dots, spread, flat):
        return pl.pallas_call(
            functools.partial(apply_kernel, sz, last),
            out_shape=[pair, shape(sz.devices, 1, LANES) if last else payload,
                       pair, shape(PAD, LANES)],
            in_specs=[VMEM] * 6 + [SMEM, SMEM] + [VMEM] * 3,
            out_specs=[VMEM] * 4,
            scratch_shapes=[pltpu.VMEM(sz.ext, F32), pltpu.VMEM(sz.ext, F32),
                            pltpu.VMEM((sz.lift_rows, LANES), F32)],
            compiler_params=PARAMS,
            cost_estimate=cost(3),
        )(received, lift_matrix, parts, mirrored, s_ext, k_ext, phi_cols,
          smooth_weight, dots, spread, flat)

    dots = jnp.zeros((PAD, LANES), F32)
    mirrored = lax.ppermute(parts, "vert", swap)
    received = exchange(sent)
    flat = data(1, parts, mirrored, s_ext, s_partner)
    parts, sent, early, dots = apply(
        False, received, parts, mirrored, dots, flat, flat
    )
    mirrored = lax.ppermute(parts, "vert", swap)
    received = exchange(sent)
    spread = data(2, parts, mirrored, s_ext, s_partner)
    parts, sent, late, dots = apply(
        True, received, parts, mirrored, dots, spread, flat
    )
    mirrored = lax.ppermute(parts, "vert", swap)
    return tuple(pl.pallas_call(
        functools.partial(final_kernel, sz),
        out_shape=[shape(1, r, c)] * 2,
        in_specs=[VMEM] * 6,
        out_specs=[VMEM] * 2,
        compiler_params=PARAMS,
        cost_estimate=cost(1),
    )(exchange(sent), initial_guess, early, late, parts, mirrored))


def solution(mesh):
    return jax.shard_map(
        local,
        mesh=mesh,
        in_specs=(
            P(("groups", "vert"), "gx", "gy"),
            P(("groups", "vert"), "gx", "gy"),
            P(("groups", "vert"), "gx", "gy"),
            P(("groups", "vert")),
            P(("groups", "vert"), "gx", "gy"),
            P(("groups", "vert"), "gx", "gy", None, None, None, None),
            P(("groups", "vert"), "gx", "gy", None, None),
            P(("groups", "gx"), None),
            P(("groups", "gx")),
            P(("groups", "gx"), None, None),
        ),
        out_specs=(P(("groups", "vert"), "gx", "gy"), P(("groups", "vert"), "gx", "gy")),
        check_vma=False,
    )
```

```python
import functools
import math

import jax
import jax.numpy as jnp
from jax import lax
from jax.experimental import pallas as pl
from jax.experimental.pallas import tpu as pltpu
from jax.sharding import PartitionSpec as P

BSIDE = 16
PATCH = 64
LANES = 128
PAD = 8
ALL = ("gx", "gy", "vert")
FIELDS = ((0, 2), (1, 2), (2, 1))
F32 = jnp.float32
VMEM = pl.BlockSpec(memory_space=pltpu.VMEM)
SMEM = pl.BlockSpec(memory_space=pltpu.SMEM)
ANY = pl.BlockSpec(memory_space=pl.ANY)
PARAMS = pltpu.CompilerParams(vmem_limit_bytes=20 * 1024 * 1024)
EDGE_PARAMS = pltpu.CompilerParams(vmem_limit_bytes=58 * 1024 * 1024)
DATA_PARAMS = pltpu.CompilerParams(vmem_limit_bytes=50 * 1024 * 1024)


class Sizes:
    def __init__(self, tx, ty, tile_shape, obs, reach, nco):
        self.tx, self.ty = tx, ty
        self.rows, self.cols = tile_shape
        self.obs, self.reach = obs, reach
        self.nco = nco
        self.px, self.py = self.rows // PATCH, self.cols // PATCH
        self.groups = self.cols // LANES
        self.ext = (self.rows + PAD, self.cols + LANES)
        self.devices = tx * ty * 2
        self.per_var = tx * ty * (1 + self.px * self.py)
        self.vec_rows = -(-nco // LANES)
        self.head = PAD * (-(-(self.vec_rows + 1) // PAD))
        self.ext_patches = (self.px + 2) * (self.py + 2)
        self.lift_rows = PAD * (-(-(self.ext_patches + self.px * self.py) // PAD))
        self.blocks = (self.rows // BSIDE) * (self.cols // BSIDE)
        self.top_div = math.sqrt(self.rows * self.cols)
        self.mid_div = float(PATCH)


def iota(shape, dim):
    return lax.broadcasted_iota(jnp.int32, shape, dim)


def lift_ids(sz, xt):
    yi, vi = lax.axis_index("gy"), lax.axis_index("vert")
    at = iota((sz.lift_rows, 1), 0)
    wide, tiles = sz.py + 2, sz.tx * sz.ty

    def steps(index, width, count):
        total = jnp.zeros_like(index)
        for a in range(1, count):
            total = total + jnp.where(index >= a * width, 1, 0)
        return total

    band = steps(at, wide, sz.px + 2)
    spot = at - band * wide
    gi, gj = xt * sz.px + band - 1, yi * sz.py + spot - 1
    near_x = xt - jnp.where(band == 0, 1, 0) + jnp.where(band == sz.px + 1, 1, 0)
    near_y = yi - jnp.where(spot == 0, 1, 0) + jnp.where(spot == sz.py + 1, 1, 0)
    inside = (near_x >= 0) & (near_x < sz.tx) & (near_y >= 0) & (near_y < sz.ty)
    mid = vi * sz.per_var + tiles + gi * (sz.ty * sz.py) + gj
    top = vi * sz.per_var + near_x * sz.ty + near_y
    mid, top = jnp.where(inside, mid, -1), jnp.where(inside, top, -1)
    rest = at - sz.ext_patches
    band = steps(rest, sz.py, sz.px)
    other = (1 - vi) * sz.per_var
    place = (xt * sz.px + band) * (sz.ty * sz.py) + yi * sz.py + rest - band * sz.py
    last = sz.ext_patches + sz.px * sz.py
    own = at < sz.ext_patches
    mid = jnp.where(own, mid, jnp.where(at < last, other + tiles + place, -1))
    top = jnp.where(own, top, jnp.where(at < last, other + xt * sz.ty + yi, -1))
    return mid, top


def share_rows(sz, slots_ref, count_ref, rows_ref, outs):
    slots = slots_ref[...]
    live = iota(slots.shape, 1) < count_ref[0]
    slots = jnp.where(live, slots, -2)
    for k, out_ref in enumerate(outs):
        mid, top = lift_ids(sz, lax.bitwise_xor(lax.axis_index("gx"), k))
        select = jnp.where(mid == slots, 1.0 / sz.mid_div, 0.0) + jnp.where(
            top == slots, 1.0 / sz.top_div, 0.0
        )
        share = jnp.dot(
            select, rows_ref[...], precision=lax.Precision.HIGHEST, preferred_element_type=F32
        )
        for i in range(sz.vec_rows):
            part = share[:, i * LANES : min((i + 1) * LANES, sz.nco)]
            if part.shape[1] < LANES:
                blank = jnp.zeros((sz.lift_rows, LANES - part.shape[1]), F32)
                part = jnp.concatenate([part, blank], axis=1)
            out_ref[pl.ds(i * sz.lift_rows, sz.lift_rows), :] = part


def put_rows(pay_ref, dest, first, block):
    for i in range(block.shape[0]):
        pay_ref[dest, first + i] = block[i : i + 1]


def setup_kernel(sz, x0_ref, s_ref, k_ref, rows_ref, slots_ref, count_ref, pay_ref, *refs):
    outs, (tiles_ref, held_ref, sems) = refs[: sz.tx], refs[sz.tx :]
    copies = [
        pltpu.make_async_copy(ref.at[0], tiles_ref.at[at], sems.at[at])
        for at, ref in enumerate((x0_ref, s_ref, k_ref))
    ]
    copies = [pltpu.make_async_copy(rows_ref.at[0], held_ref, sems.at[3])] + copies
    for copy in copies:
        copy.start()
    copies[0].wait()
    share_rows(sz, slots_ref, count_ref, held_ref, outs)
    for copy in copies[1:]:
        copy.wait()
    xi, yi, vi = lax.axis_index("gx"), lax.axis_index("gy"), lax.axis_index("vert")
    r, c, g = sz.rows, sz.cols, sz.groups
    for dx in (-1, 1):
        @pl.when((xi + dx >= 0) & (xi + dx < sz.tx))
        def _(dx=dx):
            dest = device_at(sz, xi + dx, yi, vi)
            for at, width in FIELDS:
                rows = pl.ds(0 if dx < 0 else r - width, width)
                for j in range(g):
                    put_rows(
                        pay_ref, dest, at * 2 * g + j * width,
                        tiles_ref[at, rows, pl.ds(j * LANES, LANES)],
                    )

    for dy in (-1, 1):
        @pl.when((yi + dy >= 0) & (yi + dy < sz.ty))
        def _(dy=dy):
            dest = device_at(sz, xi, yi + dy, vi)
            lanes = pl.ds(0 if dy < 0 else c - LANES, LANES)
            for at, width in FIELDS:
                first = 0 if dy < 0 else LANES - width
                pair = tiles_ref[at, :, lanes].T[first : first + width]
                put_rows(pay_ref, dest, at * 2 * g, pair)

        for dx in (-1, 1):
            @pl.when((xi + dx >= 0) & (xi + dx < sz.tx) & (yi + dy >= 0) & (yi + dy < sz.ty))
            def _(dx=dx, dy=dy):
                dest = device_at(sz, xi + dx, yi + dy, vi)
                lanes = pl.ds(0 if dy < 0 else c - LANES, LANES)
                rows = pl.ds(0 if dx < 0 else r - 1, 1)
                for at, width in FIELDS:
                    if width == 2:
                        put_rows(pay_ref, dest, at * 2 * g, tiles_ref[at, rows, lanes])


def put_borders(sz, ref, width, beside):
    r, c, g = sz.rows, sz.cols, sz.groups
    gap = jnp.zeros((LANES - 2 * width, LANES), F32)
    sides = [beside(0, 1, width), gap, beside(0, -1, width)]
    ref[pl.ds(0, r), pl.ds(c, LANES)] = jnp.concatenate(sides, axis=0).T
    up, down = beside(-1, 0, width * g), beside(1, 0, width * g)
    gap = jnp.zeros((PAD - 2 * width, LANES), F32)
    for j in range(g):
        rows = slice(j * width, (j + 1) * width)
        ref[pl.ds(r, PAD), pl.ds(j * LANES, LANES)] = jnp.concatenate(
            [down[rows], gap, up[rows]], axis=0
        )
    if width == 2:
        left = iota((1, LANES), 1) >= LANES // 2
        lines = [jnp.where(left, beside(dx, -1, 1), beside(dx, 1, 1)) for dx in (1, -1)]
        gap = jnp.zeros((PAD - 2, LANES), F32)
        block = jnp.concatenate([lines[0], gap, lines[1]], axis=0)
    else:
        block = jnp.zeros((PAD, LANES), F32)
    ref[pl.ds(r, PAD), pl.ds(c, LANES)] = block


def gather_patches(sz, v2_ref, cols_ref, out_ref):
    lane = iota((BSIDE, LANES), 1)
    row = iota((PAD, LANES), 0)
    diag = row == iota((PAD, LANES), 1) // BSIDE
    per_row = sz.cols // BSIDE
    per_lanes = LANES // BSIDE
    for q in range(sz.obs * sz.reach):
        m = cols_ref[0, 0, 0, q % sz.reach, q // sz.reach]
        var, n = m // sz.blocks, lax.rem(m, sz.blocks)
        i, j = n // per_row, lax.rem(n, per_row)
        at = pl.ds(pl.multiple_of(i * BSIDE, BSIDE), BSIDE)
        lanes = pl.ds(pl.multiple_of((j // per_lanes) * LANES, LANES), LANES)
        block = v2_ref[var, at, lanes]
        block = jnp.where(lane // BSIDE == lax.rem(j, per_lanes), block, 0.0)
        for step in (16, 32, 64):
            block = block + pltpu.roll(block, step, 1)
        for h in range(2):
            part = jnp.where(diag, block[h * PAD : (h + 1) * PAD], 0.0)
            out_ref[q // sz.reach, pl.ds(sz.reach + q % sz.reach, 1), pl.ds(h * LANES, LANES)] = jnp.sum(
                part, axis=0, keepdims=True
            )


def scatter_patches(sz, t_ref, cols_ref, spread_ref, sign, flat_ref=None, lift_ref=None):
    side = PATCH // BSIDE
    lifts = []
    crossed = jnp.zeros((1, LANES), F32)
    if flat_ref is not None:
        for q in range(sz.obs * sz.reach):
            m = cols_ref[0, 0, 0, q % sz.reach, q // sz.reach]
            n = lax.rem(m, sz.blocks)
            a = (n // (sz.cols // BSIDE)) // side
            b = lax.rem(n, sz.cols // BSIDE) // side
            at = jnp.where(
                m < sz.blocks,
                (a + 1) * (sz.py + 2) + b + 1,
                sz.ext_patches + a * sz.py + b,
            )
            lifts.append(lift_ref[pl.ds(at, 1), :])
    lane = iota((PAD, LANES), 1)
    row = iota((PAD, LANES), 0)
    diag = row == lane // BSIDE
    per_row = sz.cols // BSIDE
    per_lanes = LANES // BSIDE
    for q in range(sz.obs * sz.reach):
        m = cols_ref[0, 0, 0, q % sz.reach, q // sz.reach]
        var, n = m // sz.blocks, lax.rem(m, sz.blocks)
        i, j = n // per_row, lax.rem(n, per_row)
        lanes = pl.ds(pl.multiple_of((j // per_lanes) * LANES, LANES), LANES)
        here = lane // BSIDE == lax.rem(j, per_lanes)
        both = []
        for h in range(2):
            line = spread_ref[q // sz.reach, pl.ds(q % sz.reach, 1), pl.ds(h * LANES, LANES)]
            if flat_ref is not None:
                o, k = q // sz.reach, q % sz.reach
                for i_k in range(sz.reach):
                    line = line + lifts[sz.reach * o + i_k] * flat_ref[
                        o, pl.ds(sz.reach * (i_k + 2) + k, 1), pl.ds(h * LANES, LANES)
                    ]
                value = spread_ref[o, pl.ds(sz.reach + k, 1), pl.ds(h * LANES, LANES)] + lifts[q]
                crossed = crossed + jnp.where(m >= sz.blocks, line * value, 0.0)
            part = jnp.where(diag, line, 0.0)
            for step in (16, 32, 64):
                part = part + pltpu.roll(part, step, 1)
            both.append(jnp.where(here, part, 0.0))
        at = pl.ds(pl.multiple_of(i * BSIDE, BSIDE), BSIDE)
        t_ref[var, at, lanes] = t_ref[var, at, lanes] + sign * jnp.concatenate(both, axis=0)
    return crossed


def start_phi(sz, phi_ref, buf_ref, sems):
    for o in range(sz.obs):
        pltpu.make_async_copy(phi_ref.at[0, 0, 0, o], buf_ref.at[o], sems.at[o]).start()


def observe_spread(sz, phi_ref, buf_ref, sems, out_ref, flat):
    parts = [(k, h) for k in range(sz.reach) for h in range(BSIDE * BSIDE // LANES)]

    def body(o, carry):
        pltpu.make_async_copy(phi_ref.at[0, 0, 0, o], buf_ref.at[o], sems.at[o]).wait()

        def block(k, h):
            return buf_ref[o, k, :, pl.ds(h * LANES, LANES)]

        acc = None
        for k, h in parts:
            term = block(k, h) * out_ref[o, pl.ds(sz.reach + k, 1), pl.ds(h * LANES, LANES)]
            acc = term if acc is None else acc + term
        sources = [(0, jnp.sum(acc, axis=1, keepdims=True))]
        if flat:
            for k in range(sz.reach):
                total = block(k, 0)
                for h in range(1, BSIDE * BSIDE // LANES):
                    total = total + block(k, h)
                sources.append((k + 2, jnp.sum(total, axis=1, keepdims=True)))
        for k, h in parts:
            for first, observed in sources:
                out_ref[o, pl.ds(sz.reach * first + k, 1), pl.ds(h * LANES, LANES)] = jnp.sum(
                    block(k, h) * observed, axis=0, keepdims=True
                )
        return carry

    lax.fori_loop(0, sz.obs, body, 0)


def smooth(sz, v_ref, ke_ref, y_ref):
    xi, yi = lax.axis_index("gx"), lax.axis_index("gy")
    r, c = sz.rows, sz.cols
    rows, cols = sz.ext
    v = v_ref[...]
    beside = (
        pltpu.roll(v, 1, 0)
        + pltpu.roll(v, rows - 1, 0)
        + pltpu.roll(v, 1, 1)
        + pltpu.roll(v, cols - 1, 1)
    )
    y_ref[...] = (4.0 + ke_ref[...]) * v - beside

    row = iota((PAD, c), 0)
    keep = ((row < PAD // 2) & (xi < sz.tx - 1)) | ((row >= PAD // 2) & (xi > 0))
    below = pl.ds(r, PAD)
    y_ref[below, pl.ds(0, c)] = jnp.where(keep, y_ref[below, pl.ds(0, c)], 0.0)
    lane = iota((r, LANES), 1)
    keep = ((lane < LANES // 2) & (yi < sz.ty - 1)) | ((lane >= LANES // 2) & (yi > 0))
    side = pl.ds(c, LANES)
    y_ref[pl.ds(0, r), side] = jnp.where(keep, y_ref[pl.ds(0, r), side], 0.0)

    wide = y_ref[pl.ds(0, r), :]
    beside = (pltpu.roll(wide, 1, 1) + pltpu.roll(wide, cols - 1, 1))[:, 0:c]
    tall = y_ref[:, pl.ds(0, c)]
    beside = beside + (pltpu.roll(tall, 1, 0) + pltpu.roll(tall, rows - 1, 0))[0:r]
    return (4.0 + ke_ref[pl.ds(0, r), pl.ds(0, c)]) * wide[:, 0:c] - beside


def device_at(sz, x, y, v):
    return (x * sz.ty + y) * 2 + v


def pack_payload(sz, t_ref, pay_ref):
    xi, yi, vi = lax.axis_index("gx"), lax.axis_index("gy"), lax.axis_index("vert")
    flat = iota((sz.head, LANES), 0) * LANES + iota((sz.head, LANES), 1)
    lane = iota((1, LANES), 1)
    vec = jnp.zeros((sz.head, LANES), F32)
    tiles = sz.tx * sz.ty
    for t in range(2):
        var = vi if t == 0 else 1 - vi
        total = jnp.zeros((1, LANES), F32)
        for a in range(sz.px):
            for j in range(sz.groups):
                seg = jnp.sum(
                    t_ref[t, pl.ds(a * PATCH, PATCH), pl.ds(j * LANES, LANES)],
                    axis=0,
                    keepdims=True,
                )
                total = total + seg
                for half in range(2):
                    keep = (lane >= PATCH) if half else (lane < PATCH)
                    value = jnp.sum(jnp.where(keep, seg, 0.0), axis=1, keepdims=True)
                    at = (
                        var * sz.per_var
                        + tiles
                        + (xi * sz.px + a) * (sz.ty * sz.py)
                        + yi * sz.py
                        + 2 * j
                        + half
                    )
                    vec = jnp.where(flat == at, value * (1.0 / sz.mid_div), vec)
        value = jnp.sum(total, axis=1, keepdims=True)
        at = var * sz.per_var + xi * sz.ty + yi
        vec = jnp.where(flat == at, value * (1.0 / sz.top_div), vec)

    def fill(s, carry):
        pay_ref[s, pl.ds(0, sz.head), :] = vec
        return carry

    lax.fori_loop(0, sz.devices, fill, 0, unroll=True if sz.devices <= 16 else 1)

    r, c = sz.rows, sz.cols
    for t in range(2):
        var = vi if t == 0 else 1 - vi
        for dx, first in ((-1, 0), (1, r - 2)):
            @pl.when((xi + dx >= 0) & (xi + dx < sz.tx))
            def _(t=t, var=var, dx=dx, first=first):
                dest = device_at(sz, xi + dx, yi, var)
                for j in range(sz.groups):
                    pay_ref[dest, pl.ds(sz.head + 2 * j, 2), :] = t_ref[
                        t, pl.ds(first, 2), pl.ds(j * LANES, LANES)
                    ]

        for dy in (-1, 1):
            @pl.when((yi + dy >= 0) & (yi + dy < sz.ty))
            def _(t=t, var=var, dy=dy):
                dest = device_at(sz, xi, yi + dy, var)
                if dy < 0:
                    pair = t_ref[t, :, pl.ds(0, LANES)].T[0:2]
                else:
                    pair = t_ref[t, :, pl.ds(c - LANES, LANES)].T[LANES - 2 : LANES]
                pay_ref[dest, pl.ds(sz.head, 2), :] = pair

            for dx in (-1, 1):
                @pl.when(
                    (xi + dx >= 0) & (xi + dx < sz.tx) & (yi + dy >= 0) & (yi + dy < sz.ty)
                )
                def _(t=t, var=var, dx=dx, dy=dy):
                    dest = device_at(sz, xi + dx, yi + dy, var)
                    lanes = pl.ds(0 if dy < 0 else c - LANES, LANES)
                    pay_ref[dest, pl.ds(sz.head, 1), :] = t_ref[
                        t, pl.ds(0 if dx < 0 else r - 1, 1), lanes
                    ]


def from_neighbour(sz, recv_ref, dx, dy, first, count, var=None):
    xi, yi = lax.axis_index("gx"), lax.axis_index("gy")
    x, y = xi + dx, yi + dy
    inside = (x >= 0) & (x < sz.tx) & (y >= 0) & (y < sz.ty)
    source = device_at(sz, jnp.clip(x, 0, sz.tx - 1), jnp.clip(y, 0, sz.ty - 1), 0)
    rows = pl.ds(first, count)
    if var is None:
        found = recv_ref[source, rows, :] + recv_ref[source + 1, rows, :]
    else:
        found = [recv_ref[source + var, row] for row in range(first, first + count)]
        found = jnp.concatenate(found, axis=0)
    return jnp.where(inside, found, 0.0)


def data_kernel(sz, stage, *refs):
    if stage == 0:
        x_ref, xp_ref, cols_ref, phi_ref, terms_ref, out_ref = refs[:6]
    else:
        to_ref, tm_ref, s_ref, sp_ref, cols_ref, phi_ref, out_ref = refs[:7]
    v2_ref, buf_ref, sems = refs[-3:]
    start_phi(sz, phi_ref, buf_ref, sems)
    if stage == 0:
        v2_ref[0] = x_ref[0]
        v2_ref[1] = xp_ref[0]
    else:
        scale = s_ref[pl.ds(0, sz.rows), pl.ds(0, sz.cols)]
        v2_ref[0] = scale * (to_ref[0] + tm_ref[1])
        v2_ref[1] = sp_ref[0] * (tm_ref[0] + to_ref[1])
    gather_patches(sz, v2_ref, cols_ref, out_ref)
    observe_spread(sz, phi_ref, buf_ref, sems, out_ref, stage == 1)
    if stage == 0:
        terms_ref[...] = jnp.zeros_like(terms_ref)
        scatter_patches(sz, terms_ref, cols_ref, out_ref, -1.0)


def first_kernel(sz, recv_ref, x0_ref, s_ref, k_ref, b_ref, terms_ref, w_ref,
                 t_ref, pay_ref, se_ref, ke_ref, v_ref, y_ref):
    vi = lax.axis_index("vert")
    r, c, g = sz.rows, sz.cols, sz.groups
    for (at, width), ref, src in zip(FIELDS, (v_ref, se_ref, ke_ref), (x0_ref, s_ref, k_ref)):
        first = at * 2 * g

        def beside(dx, dy, count):
            return from_neighbour(sz, recv_ref, dx, dy, first, count, vi)

        ref[pl.ds(0, r), pl.ds(0, c)] = src[0]
        put_borders(sz, ref, width, beside)
    t_ref[0] = (b_ref[0] + terms_ref[0]) - w_ref[0] * smooth(sz, v_ref, ke_ref, y_ref)
    t_ref[1] = terms_ref[1]
    pack_payload(sz, t_ref, pay_ref)


def precondition(sz, recv_ref, lg_ref, to_ref, tm_ref, se_ref, v_ref, state_ref, lift_ref):
    r, c, g = sz.rows, sz.cols, sz.groups
    lane = iota((1, LANES), 1)

    def add_head(s, vec):
        return vec + recv_ref[s, pl.ds(0, sz.head), :]

    vec = lax.fori_loop(
        1, sz.devices, add_head, recv_ref[0, pl.ds(0, sz.head), :],
        unroll=True if sz.devices <= 16 else 1,
    )
    acc = None
    for i in range(sz.vec_rows):
        term = lg_ref[pl.ds(i * sz.lift_rows, sz.lift_rows), :] * vec[i : i + 1]
        acc = term if acc is None else acc + term
    lift = jnp.broadcast_to(jnp.sum(acc, axis=1, keepdims=True), (sz.lift_rows, LANES))
    lift_ref[...] = lift

    whole = to_ref[0] + tm_ref[1]
    state_ref[0] = whole
    v_ref[pl.ds(0, r), pl.ds(0, c)] = whole

    def beside(dx, dy, count):
        return from_neighbour(sz, recv_ref, dx, dy, sz.head, count)

    put_borders(sz, v_ref, 2, beside)
    wide = sz.py + 2

    def line(band, j):
        low, high = (2 * j + 1, 2 * j + 2) if j < g else (wide - 1, 0)
        low, high = band * wide + low, band * wide + high
        return jnp.where(lane < PATCH, lift[low : low + 1], lift[high : high + 1])

    row = iota((PAD, LANES), 0)
    for j in range(g + 1):
        lanes = pl.ds(j * LANES, LANES)
        for a in range(sz.px):
            rows = pl.ds(a * PATCH, PATCH)
            v_ref[rows, lanes] = se_ref[rows, lanes] * v_ref[rows, lanes] + line(a + 1, j)
        rows = pl.ds(r, PAD)
        both = jnp.where(row < PAD // 2, line(sz.px + 1, j), line(0, j))
        v_ref[rows, lanes] = se_ref[rows, lanes] * v_ref[rows, lanes] + both


def row_dot(sz, left, right):
    line = jnp.sum(left * right, axis=0, keepdims=True)
    total = line[:, 0:LANES]
    for j in range(1, sz.groups):
        total = total + line[:, j * LANES : (j + 1) * LANES]
    return total


def apply_kernel(sz, last, recv_ref, lg_ref, to_ref, tm_ref, se_ref, ke_ref, cols_ref,
                 w_ref, dots_ref, spread_ref, flat_ref, t_ref, pay_ref, state_ref, out_dots_ref,
                 v_ref, y_ref, lift_ref):
    r, c = sz.rows, sz.cols
    precondition(sz, recv_ref, lg_ref, to_ref, tm_ref, se_ref, v_ref, state_ref, lift_ref)
    t_ref[0] = w_ref[0] * smooth(sz, v_ref, ke_ref, y_ref)
    t_ref[1] = jnp.zeros((r, c), F32)
    crossed = scatter_patches(sz, t_ref, cols_ref, spread_ref, 1.0, flat_ref, lift_ref)
    own = v_ref[pl.ds(0, r), pl.ds(0, c)]
    state_ref[1] = own
    gamma = row_dot(sz, state_ref[0], own)
    curve = row_dot(sz, own, t_ref[0]) + crossed
    if last:
        out_dots_ref[...] = dots_ref[...]
        lane = iota((1, LANES), 1)
        lines = jnp.zeros((1, LANES), F32)
        for i, part in enumerate((dots_ref[0:1], dots_ref[1:2], gamma, curve)):
            lines = jnp.where(lane == i, jnp.sum(part, axis=1, keepdims=True), lines)

        def fill(s, carry):
            pay_ref[s] = lines
            return carry

        lax.fori_loop(0, sz.devices, fill, 0, unroll=True if sz.devices <= 16 else 1)
    else:
        out_dots_ref[...] = jnp.concatenate(
            [gamma, curve, jnp.zeros((PAD - 2, LANES), F32)], axis=0
        )
        pack_payload(sz, t_ref, pay_ref)


def final_kernel(sz, recv_ref, x0_ref, rp_ref, wz_ref, to_ref, tm_ref, x_ref, res_ref):
    def add(s, lines):
        return lines + recv_ref[s]

    lines = lax.fori_loop(
        1, sz.devices, add, recv_ref[0], unroll=True if sz.devices <= 16 else 1
    )
    lane = iota((1, LANES), 1)
    gamma, delta, cross, far = (
        jnp.sum(jnp.where(lane == i, lines, 0.0), axis=1, keepdims=True) for i in range(4)
    )
    step = gamma / delta
    gamma_new = step * step * cross - gamma
    growth = step * cross / delta
    curve = step * step * (far - cross * cross / delta)
    step_new = gamma_new / curve
    along = step + step_new * growth
    back = step_new * step
    x_ref[0] = x0_ref[0] + (along * rp_ref[1] - back * wz_ref[1])
    image = to_ref[0] + tm_ref[1]
    res_ref[0] = rp_ref[0] - (along * wz_ref[0] - back * image)


def shape(*dims):
    return jax.ShapeDtypeStruct(dims, F32)


def data_space(sz):
    block = BSIDE * BSIDE
    return [
        pltpu.VMEM((2, sz.rows, sz.cols), F32),
        pltpu.VMEM((sz.obs, sz.reach, block, block), F32),
        pltpu.SemaphoreType.DMA((sz.obs,)),
    ]


def cost(micros):
    return pl.CostEstimate(flops=0, bytes_accessed=int(micros * 3.0e6), transcendentals=0)


def local(right_side, initial_guess, kappa_sq, smooth_weight, precond_scale, phi_vals, phi_cols,
          coarse_slots, slot_count, coarse_rows):
    tx, ty = lax.axis_size("gx"), lax.axis_size("gy")
    phi_cols = jnp.swapaxes(phi_cols, 3, 4)
    sz = Sizes(tx, ty, right_side.shape[1:], phi_vals.shape[3], phi_vals.shape[4],
               coarse_rows.shape[2])
    swap = [(0, 1), (1, 0)]
    x_partner = lax.ppermute(initial_guess, "vert", swap)
    s_partner = lax.ppermute(precond_scale, "vert", swap)

    def exchange(array):
        return lax.all_to_all(array, ALL, 0, 0, tiled=True)

    cap = coarse_slots.shape[1]
    edges, *shares = pl.pallas_call(
        functools.partial(setup_kernel, sz),
        out_shape=[shape(sz.devices, 5 * sz.groups, 1, LANES)]
        + [shape(sz.vec_rows * sz.lift_rows, LANES)] * tx,
        in_specs=[ANY] * 4 + [VMEM, SMEM],
        out_specs=[VMEM] * (1 + tx),
        scratch_shapes=[pltpu.VMEM((3, sz.rows, sz.cols), F32), pltpu.VMEM((cap, sz.nco), F32),
                        pltpu.SemaphoreType.DMA((4,))],
        compiler_params=EDGE_PARAMS,
        cost_estimate=cost(1.5),
    )(initial_guess, precond_scale, kappa_sq, coarse_rows, coarse_slots, slot_count)
    got = [lax.ppermute(shares[k], "gx", [(i, i ^ k) for i in range(tx)]) for k in range(1, tx)]
    lift_matrix = sum(got, shares[0])
    edges, x_partner = lax.optimization_barrier((edges, x_partner))
    edges = exchange(edges)

    r, c = sz.rows, sz.cols
    block = BSIDE * BSIDE
    pair = shape(2, r, c)
    payload = shape(sz.devices, sz.head + PAD, LANES)

    def data(stage, *fields):
        lines = (sz.obs, sz.reach * (2 + sz.reach * (stage == 1)))
        return pl.pallas_call(
            functools.partial(data_kernel, sz, stage),
            out_shape=pair if stage == 0 else shape(*lines, block),
            in_specs=[VMEM] * len(fields) + [SMEM, ANY],
            out_specs=VMEM,
            scratch_shapes=[pltpu.VMEM(lines + (block,), F32)] * (stage == 0) + data_space(sz),
            compiler_params=DATA_PARAMS,
            cost_estimate=cost(4),
        )(*fields, phi_cols, phi_vals)

    terms = data(0, initial_guess, x_partner)
    parts, sent, s_ext, k_ext = pl.pallas_call(
        functools.partial(first_kernel, sz),
        out_shape=[pair, payload, shape(*sz.ext), shape(*sz.ext)],
        in_specs=[VMEM] * 6 + [SMEM],
        out_specs=[VMEM] * 4,
        scratch_shapes=[pltpu.VMEM(sz.ext, F32)] * 2,
        compiler_params=PARAMS,
        cost_estimate=cost(3),
    )(edges, initial_guess, precond_scale, kappa_sq, right_side, terms, smooth_weight)

    def apply(last, received, parts, mirrored, dots, spread, flat):
        return pl.pallas_call(
            functools.partial(apply_kernel, sz, last),
            out_shape=[pair, shape(sz.devices, 1, LANES) if last else payload,
                       pair, shape(PAD, LANES)],
            in_specs=[VMEM] * 6 + [SMEM, SMEM] + [VMEM] * 3,
            out_specs=[VMEM] * 4,
            scratch_shapes=[pltpu.VMEM(sz.ext, F32), pltpu.VMEM(sz.ext, F32),
                            pltpu.VMEM((sz.lift_rows, LANES), F32)],
            compiler_params=PARAMS,
            cost_estimate=cost(3),
        )(received, lift_matrix, parts, mirrored, s_ext, k_ext, phi_cols,
          smooth_weight, dots, spread, flat)

    dots = jnp.zeros((PAD, LANES), F32)
    mirrored = lax.ppermute(parts, "vert", swap)
    received = exchange(sent)
    flat = data(1, parts, mirrored, s_ext, s_partner)
    parts, sent, early, dots = apply(
        False, received, parts, mirrored, dots, flat, flat
    )
    mirrored = lax.ppermute(parts, "vert", swap)
    received = exchange(sent)
    spread = data(2, parts, mirrored, s_ext, s_partner)
    parts, sent, late, dots = apply(
        True, received, parts, mirrored, dots, spread, flat
    )
    mirrored = lax.ppermute(parts, "vert", swap)
    return tuple(pl.pallas_call(
        functools.partial(final_kernel, sz),
        out_shape=[shape(1, r, c)] * 2,
        in_specs=[VMEM] * 6,
        out_specs=[VMEM] * 2,
        compiler_params=PARAMS,
        cost_estimate=cost(1),
    )(exchange(sent), initial_guess, early, late, parts, mirrored))


def solution(mesh):
    return jax.shard_map(
        local,
        mesh=mesh,
        in_specs=(
            P(("groups", "vert"), "gx", "gy"),
            P(("groups", "vert"), "gx", "gy"),
            P(("groups", "vert"), "gx", "gy"),
            P(("groups", "vert")),
            P(("groups", "vert"), "gx", "gy"),
            P(("groups", "vert"), "gx", "gy", None, None, None, None),
            P(("groups", "vert"), "gx", "gy", None, None),
            P(("groups", "gx"), None),
            P(("groups", "gx")),
            P(("groups", "gx"), None, None),
        ),
        out_specs=(P(("groups", "vert"), "gx", "gy"), P(("groups", "vert"), "gx", "gy")),
        check_vma=False,
    )
```

```python
import functools
import math

import jax
import jax.numpy as jnp
from jax import lax
from jax.experimental import pallas as pl
from jax.experimental.pallas import tpu as pltpu
from jax.sharding import PartitionSpec as P

BSIDE = 16
PATCH = 64
LANES = 128
PAD = 8
ALL = ("gx", "gy", "vert")
FIELDS = ((0, 2), (1, 2), (2, 1))
F32 = jnp.float32
VMEM = pl.BlockSpec(memory_space=pltpu.VMEM)
SMEM = pl.BlockSpec(memory_space=pltpu.SMEM)
ANY = pl.BlockSpec(memory_space=pl.ANY)
PARAMS = pltpu.CompilerParams(vmem_limit_bytes=20 * 1024 * 1024)
EDGE_PARAMS = pltpu.CompilerParams(vmem_limit_bytes=58 * 1024 * 1024)
DATA_PARAMS = pltpu.CompilerParams(vmem_limit_bytes=50 * 1024 * 1024)


class Sizes:
    def __init__(self, tx, ty, tile_shape, obs, reach, nco):
        self.tx, self.ty = tx, ty
        self.rows, self.cols = tile_shape
        self.obs, self.reach = obs, reach
        self.nco = nco
        self.px, self.py = self.rows // PATCH, self.cols // PATCH
        self.groups = self.cols // LANES
        self.ext = (self.rows + PAD, self.cols + LANES)
        self.devices = tx * ty * 2
        self.per_var = tx * ty * (1 + self.px * self.py)
        self.vec_rows = -(-nco // LANES)
        self.head = PAD * (-(-(self.vec_rows + 1) // PAD))
        self.ext_patches = (self.px + 2) * (self.py + 2)
        self.lift_rows = PAD * (-(-(self.ext_patches + self.px * self.py) // PAD))
        self.blocks = (self.rows // BSIDE) * (self.cols // BSIDE)
        self.top_div = math.sqrt(self.rows * self.cols)
        self.mid_div = float(PATCH)


def iota(shape, dim):
    return lax.broadcasted_iota(jnp.int32, shape, dim)


def lift_ids(sz, xt):
    yi, vi = lax.axis_index("gy"), lax.axis_index("vert")
    at = iota((sz.lift_rows, 1), 0)
    wide, tiles = sz.py + 2, sz.tx * sz.ty

    def steps(index, width, count):
        total = jnp.zeros_like(index)
        for a in range(1, count):
            total = total + jnp.where(index >= a * width, 1, 0)
        return total

    band = steps(at, wide, sz.px + 2)
    spot = at - band * wide
    gi, gj = xt * sz.px + band - 1, yi * sz.py + spot - 1
    near_x = xt - jnp.where(band == 0, 1, 0) + jnp.where(band == sz.px + 1, 1, 0)
    near_y = yi - jnp.where(spot == 0, 1, 0) + jnp.where(spot == sz.py + 1, 1, 0)
    inside = (near_x >= 0) & (near_x < sz.tx) & (near_y >= 0) & (near_y < sz.ty)
    mid = vi * sz.per_var + tiles + gi * (sz.ty * sz.py) + gj
    top = vi * sz.per_var + near_x * sz.ty + near_y
    mid, top = jnp.where(inside, mid, -1), jnp.where(inside, top, -1)
    rest = at - sz.ext_patches
    band = steps(rest, sz.py, sz.px)
    other = (1 - vi) * sz.per_var
    place = (xt * sz.px + band) * (sz.ty * sz.py) + yi * sz.py + rest - band * sz.py
    last = sz.ext_patches + sz.px * sz.py
    own = at < sz.ext_patches
    mid = jnp.where(own, mid, jnp.where(at < last, other + tiles + place, -1))
    top = jnp.where(own, top, jnp.where(at < last, other + xt * sz.ty + yi, -1))
    return mid, top


def share_rows(sz, slots_ref, count_ref, rows_ref, outs):
    slots = slots_ref[...]
    live = iota(slots.shape, 1) < count_ref[0]
    slots = jnp.where(live, slots, -2)
    for k, out_ref in enumerate(outs):
        mid, top = lift_ids(sz, lax.bitwise_xor(lax.axis_index("gx"), k))
        select = jnp.where(mid == slots, 1.0 / sz.mid_div, 0.0) + jnp.where(
            top == slots, 1.0 / sz.top_div, 0.0
        )
        share = jnp.dot(
            select, rows_ref[...], precision=lax.Precision.HIGHEST, preferred_element_type=F32
        )
        for i in range(sz.vec_rows):
            part = share[:, i * LANES : min((i + 1) * LANES, sz.nco)]
            if part.shape[1] < LANES:
                blank = jnp.zeros((sz.lift_rows, LANES - part.shape[1]), F32)
                part = jnp.concatenate([part, blank], axis=1)
            out_ref[pl.ds(i * sz.lift_rows, sz.lift_rows), :] = part


def put_rows(pay_ref, dest, first, block):
    for i in range(block.shape[0]):
        pay_ref[dest, first + i] = block[i : i + 1]


def setup_kernel(sz, x0_ref, s_ref, k_ref, rows_ref, slots_ref, count_ref, pay_ref, *refs):
    outs, (tiles_ref, held_ref, live_ref, sems) = refs[: sz.tx], refs[sz.tx :]
    copies = [
        pltpu.make_async_copy(ref.at[0], tiles_ref.at[at], sems.at[at])
        for at, ref in enumerate((x0_ref, s_ref, k_ref))
    ]
    copies = [
        pltpu.make_async_copy(rows_ref.at[0], held_ref, sems.at[3]),
        pltpu.make_async_copy(slots_ref, live_ref, sems.at[4]),
    ] + copies
    for copy in copies:
        copy.start()
    copies[0].wait()
    copies[1].wait()
    share_rows(sz, live_ref, count_ref, held_ref, outs)
    for copy in copies[2:]:
        copy.wait()
    xi, yi, vi = lax.axis_index("gx"), lax.axis_index("gy"), lax.axis_index("vert")
    r, c, g = sz.rows, sz.cols, sz.groups
    for dx in (-1, 1):
        @pl.when((xi + dx >= 0) & (xi + dx < sz.tx))
        def _(dx=dx):
            dest = device_at(sz, xi + dx, yi, vi)
            for at, width in FIELDS:
                rows = pl.ds(0 if dx < 0 else r - width, width)
                for j in range(g):
                    put_rows(
                        pay_ref, dest, at * 2 * g + j * width,
                        tiles_ref[at, rows, pl.ds(j * LANES, LANES)],
                    )

    for dy in (-1, 1):
        @pl.when((yi + dy >= 0) & (yi + dy < sz.ty))
        def _(dy=dy):
            dest = device_at(sz, xi, yi + dy, vi)
            lanes = pl.ds(0 if dy < 0 else c - LANES, LANES)
            for at, width in FIELDS:
                first = 0 if dy < 0 else LANES - width
                pair = tiles_ref[at, :, lanes].T[first : first + width]
                put_rows(pay_ref, dest, at * 2 * g, pair)

        for dx in (-1, 1):
            @pl.when((xi + dx >= 0) & (xi + dx < sz.tx) & (yi + dy >= 0) & (yi + dy < sz.ty))
            def _(dx=dx, dy=dy):
                dest = device_at(sz, xi + dx, yi + dy, vi)
                lanes = pl.ds(0 if dy < 0 else c - LANES, LANES)
                rows = pl.ds(0 if dx < 0 else r - 1, 1)
                for at, width in FIELDS:
                    if width == 2:
                        put_rows(pay_ref, dest, at * 2 * g, tiles_ref[at, rows, lanes])


def put_borders(sz, ref, width, beside):
    r, c, g = sz.rows, sz.cols, sz.groups
    gap = jnp.zeros((LANES - 2 * width, LANES), F32)
    sides = [beside(0, 1, width), gap, beside(0, -1, width)]
    ref[pl.ds(0, r), pl.ds(c, LANES)] = jnp.concatenate(sides, axis=0).T
    up, down = beside(-1, 0, width * g), beside(1, 0, width * g)
    gap = jnp.zeros((PAD - 2 * width, LANES), F32)
    for j in range(g):
        rows = slice(j * width, (j + 1) * width)
        ref[pl.ds(r, PAD), pl.ds(j * LANES, LANES)] = jnp.concatenate(
            [down[rows], gap, up[rows]], axis=0
        )
    if width == 2:
        left = iota((1, LANES), 1) >= LANES // 2
        lines = [jnp.where(left, beside(dx, -1, 1), beside(dx, 1, 1)) for dx in (1, -1)]
        gap = jnp.zeros((PAD - 2, LANES), F32)
        block = jnp.concatenate([lines[0], gap, lines[1]], axis=0)
    else:
        block = jnp.zeros((PAD, LANES), F32)
    ref[pl.ds(r, PAD), pl.ds(c, LANES)] = block


def gather_patches(sz, v2_ref, cols_ref, out_ref):
    lane = iota((BSIDE, LANES), 1)
    row = iota((PAD, LANES), 0)
    diag = row == iota((PAD, LANES), 1) // BSIDE
    per_row = sz.cols // BSIDE
    per_lanes = LANES // BSIDE
    for q in range(sz.obs * sz.reach):
        m = cols_ref[0, 0, 0, q % sz.reach, q // sz.reach]
        var, n = m // sz.blocks, lax.rem(m, sz.blocks)
        i, j = n // per_row, lax.rem(n, per_row)
        at = pl.ds(pl.multiple_of(i * BSIDE, BSIDE), BSIDE)
        lanes = pl.ds(pl.multiple_of((j // per_lanes) * LANES, LANES), LANES)
        block = v2_ref[var, at, lanes]
        block = jnp.where(lane // BSIDE == lax.rem(j, per_lanes), block, 0.0)
        for step in (16, 32, 64):
            block = block + pltpu.roll(block, step, 1)
        for h in range(2):
            part = jnp.where(diag, block[h * PAD : (h + 1) * PAD], 0.0)
            out_ref[q // sz.reach, pl.ds(sz.reach + q % sz.reach, 1), pl.ds(h * LANES, LANES)] = jnp.sum(
                part, axis=0, keepdims=True
            )


def scatter_patches(sz, t_ref, cols_ref, spread_ref, sign, flat_ref=None, lift_ref=None):
    side = PATCH // BSIDE
    lifts = []
    crossed = jnp.zeros((1, LANES), F32)
    if flat_ref is not None:
        for q in range(sz.obs * sz.reach):
            m = cols_ref[0, 0, 0, q % sz.reach, q // sz.reach]
            n = lax.rem(m, sz.blocks)
            a = (n // (sz.cols // BSIDE)) // side
            b = lax.rem(n, sz.cols // BSIDE) // side
            at = jnp.where(
                m < sz.blocks,
                (a + 1) * (sz.py + 2) + b + 1,
                sz.ext_patches + a * sz.py + b,
            )
            lifts.append(lift_ref[pl.ds(at, 1), :])
    lane = iota((PAD, LANES), 1)
    row = iota((PAD, LANES), 0)
    diag = row == lane // BSIDE
    per_row = sz.cols // BSIDE
    per_lanes = LANES // BSIDE
    for q in range(sz.obs * sz.reach):
        m = cols_ref[0, 0, 0, q % sz.reach, q // sz.reach]
        var, n = m // sz.blocks, lax.rem(m, sz.blocks)
        i, j = n // per_row, lax.rem(n, per_row)
        lanes = pl.ds(pl.multiple_of((j // per_lanes) * LANES, LANES), LANES)
        here = lane // BSIDE == lax.rem(j, per_lanes)
        both = []
        for h in range(2):
            line = spread_ref[q // sz.reach, pl.ds(q % sz.reach, 1), pl.ds(h * LANES, LANES)]
            if flat_ref is not None:
                o, k = q // sz.reach, q % sz.reach
                for i_k in range(sz.reach):
                    line = line + lifts[sz.reach * o + i_k] * flat_ref[
                        o, pl.ds(sz.reach * (i_k + 2) + k, 1), pl.ds(h * LANES, LANES)
                    ]
                value = spread_ref[o, pl.ds(sz.reach + k, 1), pl.ds(h * LANES, LANES)] + lifts[q]
                crossed = crossed + jnp.where(m >= sz.blocks, line * value, 0.0)
            part = jnp.where(diag, line, 0.0)
            for step in (16, 32, 64):
                part = part + pltpu.roll(part, step, 1)
            both.append(jnp.where(here, part, 0.0))
        at = pl.ds(pl.multiple_of(i * BSIDE, BSIDE), BSIDE)
        t_ref[var, at, lanes] = t_ref[var, at, lanes] + sign * jnp.concatenate(both, axis=0)
    return crossed


def start_phi(sz, phi_ref, buf_ref, sems):
    for o in range(sz.obs):
        pltpu.make_async_copy(phi_ref.at[0, 0, 0, o], buf_ref.at[o], sems.at[o]).start()


def observe_spread(sz, phi_ref, buf_ref, sems, out_ref, flat):
    parts = [(k, h) for k in range(sz.reach) for h in range(BSIDE * BSIDE // LANES)]

    def body(o, carry):
        pltpu.make_async_copy(phi_ref.at[0, 0, 0, o], buf_ref.at[o], sems.at[o]).wait()

        def block(k, h):
            return buf_ref[o, k, :, pl.ds(h * LANES, LANES)]

        acc = None
        for k, h in parts:
            term = block(k, h) * out_ref[o, pl.ds(sz.reach + k, 1), pl.ds(h * LANES, LANES)]
            acc = term if acc is None else acc + term
        sources = [(0, jnp.sum(acc, axis=1, keepdims=True))]
        if flat:
            for k in range(sz.reach):
                total = block(k, 0)
                for h in range(1, BSIDE * BSIDE // LANES):
                    total = total + block(k, h)
                sources.append((k + 2, jnp.sum(total, axis=1, keepdims=True)))
        for k, h in parts:
            for first, observed in sources:
                out_ref[o, pl.ds(sz.reach * first + k, 1), pl.ds(h * LANES, LANES)] = jnp.sum(
                    block(k, h) * observed, axis=0, keepdims=True
                )
        return carry

    lax.fori_loop(0, sz.obs, body, 0)


def smooth(sz, v_ref, ke_ref, y_ref):
    xi, yi = lax.axis_index("gx"), lax.axis_index("gy")
    r, c = sz.rows, sz.cols
    rows, cols = sz.ext
    v = v_ref[...]
    beside = (
        pltpu.roll(v, 1, 0)
        + pltpu.roll(v, rows - 1, 0)
        + pltpu.roll(v, 1, 1)
        + pltpu.roll(v, cols - 1, 1)
    )
    y_ref[...] = (4.0 + ke_ref[...]) * v - beside

    row = iota((PAD, c), 0)
    keep = ((row < PAD // 2) & (xi < sz.tx - 1)) | ((row >= PAD // 2) & (xi > 0))
    below = pl.ds(r, PAD)
    y_ref[below, pl.ds(0, c)] = jnp.where(keep, y_ref[below, pl.ds(0, c)], 0.0)
    lane = iota((r, LANES), 1)
    keep = ((lane < LANES // 2) & (yi < sz.ty - 1)) | ((lane >= LANES // 2) & (yi > 0))
    side = pl.ds(c, LANES)
    y_ref[pl.ds(0, r), side] = jnp.where(keep, y_ref[pl.ds(0, r), side], 0.0)

    wide = y_ref[pl.ds(0, r), :]
    beside = (pltpu.roll(wide, 1, 1) + pltpu.roll(wide, cols - 1, 1))[:, 0:c]
    tall = y_ref[:, pl.ds(0, c)]
    beside = beside + (pltpu.roll(tall, 1, 0) + pltpu.roll(tall, rows - 1, 0))[0:r]
    return (4.0 + ke_ref[pl.ds(0, r), pl.ds(0, c)]) * wide[:, 0:c] - beside


def device_at(sz, x, y, v):
    return (x * sz.ty + y) * 2 + v


def pack_payload(sz, t_ref, pay_ref):
    xi, yi, vi = lax.axis_index("gx"), lax.axis_index("gy"), lax.axis_index("vert")
    flat = iota((sz.head, LANES), 0) * LANES + iota((sz.head, LANES), 1)
    lane = iota((1, LANES), 1)
    vec = jnp.zeros((sz.head, LANES), F32)
    tiles = sz.tx * sz.ty
    for t in range(2):
        var = vi if t == 0 else 1 - vi
        total = jnp.zeros((1, LANES), F32)
        for a in range(sz.px):
            for j in range(sz.groups):
                seg = jnp.sum(
                    t_ref[t, pl.ds(a * PATCH, PATCH), pl.ds(j * LANES, LANES)],
                    axis=0,
                    keepdims=True,
                )
                total = total + seg
                for half in range(2):
                    keep = (lane >= PATCH) if half else (lane < PATCH)
                    value = jnp.sum(jnp.where(keep, seg, 0.0), axis=1, keepdims=True)
                    at = (
                        var * sz.per_var
                        + tiles
                        + (xi * sz.px + a) * (sz.ty * sz.py)
                        + yi * sz.py
                        + 2 * j
                        + half
                    )
                    vec = jnp.where(flat == at, value * (1.0 / sz.mid_div), vec)
        value = jnp.sum(total, axis=1, keepdims=True)
        at = var * sz.per_var + xi * sz.ty + yi
        vec = jnp.where(flat == at, value * (1.0 / sz.top_div), vec)

    def fill(s, carry):
        pay_ref[s, pl.ds(0, sz.head), :] = vec
        return carry

    lax.fori_loop(0, sz.devices, fill, 0, unroll=True if sz.devices <= 16 else 1)

    r, c = sz.rows, sz.cols
    for t in range(2):
        var = vi if t == 0 else 1 - vi
        for dx, first in ((-1, 0), (1, r - 2)):
            @pl.when((xi + dx >= 0) & (xi + dx < sz.tx))
            def _(t=t, var=var, dx=dx, first=first):
                dest = device_at(sz, xi + dx, yi, var)
                for j in range(sz.groups):
                    pay_ref[dest, pl.ds(sz.head + 2 * j, 2), :] = t_ref[
                        t, pl.ds(first, 2), pl.ds(j * LANES, LANES)
                    ]

        for dy in (-1, 1):
            @pl.when((yi + dy >= 0) & (yi + dy < sz.ty))
            def _(t=t, var=var, dy=dy):
                dest = device_at(sz, xi, yi + dy, var)
                if dy < 0:
                    pair = t_ref[t, :, pl.ds(0, LANES)].T[0:2]
                else:
                    pair = t_ref[t, :, pl.ds(c - LANES, LANES)].T[LANES - 2 : LANES]
                pay_ref[dest, pl.ds(sz.head, 2), :] = pair

            for dx in (-1, 1):
                @pl.when(
                    (xi + dx >= 0) & (xi + dx < sz.tx) & (yi + dy >= 0) & (yi + dy < sz.ty)
                )
                def _(t=t, var=var, dx=dx, dy=dy):
                    dest = device_at(sz, xi + dx, yi + dy, var)
                    lanes = pl.ds(0 if dy < 0 else c - LANES, LANES)
                    pay_ref[dest, pl.ds(sz.head, 1), :] = t_ref[
                        t, pl.ds(0 if dx < 0 else r - 1, 1), lanes
                    ]


def from_neighbour(sz, recv_ref, dx, dy, first, count, var=None):
    xi, yi = lax.axis_index("gx"), lax.axis_index("gy")
    x, y = xi + dx, yi + dy
    inside = (x >= 0) & (x < sz.tx) & (y >= 0) & (y < sz.ty)
    source = device_at(sz, jnp.clip(x, 0, sz.tx - 1), jnp.clip(y, 0, sz.ty - 1), 0)
    rows = pl.ds(first, count)
    if var is None:
        found = recv_ref[source, rows, :] + recv_ref[source + 1, rows, :]
    else:
        found = [recv_ref[source + var, row] for row in range(first, first + count)]
        found = jnp.concatenate(found, axis=0)
    return jnp.where(inside, found, 0.0)


def data_kernel(sz, stage, *refs):
    if stage == 0:
        x_ref, xp_ref, cols_ref, phi_ref, terms_ref, out_ref = refs[:6]
    else:
        to_ref, tm_ref, s_ref, sp_ref, cols_ref, phi_ref, out_ref = refs[:7]
    v2_ref, buf_ref, sems = refs[-3:]
    start_phi(sz, phi_ref, buf_ref, sems)
    if stage == 0:
        v2_ref[0] = x_ref[0]
        v2_ref[1] = xp_ref[0]
    else:
        scale = s_ref[pl.ds(0, sz.rows), pl.ds(0, sz.cols)]
        v2_ref[0] = scale * (to_ref[0] + tm_ref[1])
        v2_ref[1] = sp_ref[0] * (tm_ref[0] + to_ref[1])
    gather_patches(sz, v2_ref, cols_ref, out_ref)
    observe_spread(sz, phi_ref, buf_ref, sems, out_ref, stage == 1)
    if stage == 0:
        terms_ref[...] = jnp.zeros_like(terms_ref)
        scatter_patches(sz, terms_ref, cols_ref, out_ref, -1.0)


def first_kernel(sz, recv_ref, x0_ref, s_ref, k_ref, b_ref, terms_ref, w_ref,
                 t_ref, pay_ref, se_ref, ke_ref, v_ref, y_ref):
    vi = lax.axis_index("vert")
    r, c, g = sz.rows, sz.cols, sz.groups
    for (at, width), ref, src in zip(FIELDS, (v_ref, se_ref, ke_ref), (x0_ref, s_ref, k_ref)):
        first = at * 2 * g

        def beside(dx, dy, count):
            return from_neighbour(sz, recv_ref, dx, dy, first, count, vi)

        ref[pl.ds(0, r), pl.ds(0, c)] = src[0]
        put_borders(sz, ref, width, beside)
    t_ref[0] = (b_ref[0] + terms_ref[0]) - w_ref[0] * smooth(sz, v_ref, ke_ref, y_ref)
    t_ref[1] = terms_ref[1]
    pack_payload(sz, t_ref, pay_ref)


def precondition(sz, recv_ref, lg_ref, to_ref, tm_ref, se_ref, v_ref, state_ref, lift_ref):
    r, c, g = sz.rows, sz.cols, sz.groups
    lane = iota((1, LANES), 1)

    def add_head(s, vec):
        return vec + recv_ref[s, pl.ds(0, sz.head), :]

    vec = lax.fori_loop(
        1, sz.devices, add_head, recv_ref[0, pl.ds(0, sz.head), :],
        unroll=True if sz.devices <= 16 else 1,
    )
    acc = None
    for i in range(sz.vec_rows):
        term = lg_ref[pl.ds(i * sz.lift_rows, sz.lift_rows), :] * vec[i : i + 1]
        acc = term if acc is None else acc + term
    lift = jnp.broadcast_to(jnp.sum(acc, axis=1, keepdims=True), (sz.lift_rows, LANES))
    lift_ref[...] = lift

    whole = to_ref[0] + tm_ref[1]
    state_ref[0] = whole
    v_ref[pl.ds(0, r), pl.ds(0, c)] = whole

    def beside(dx, dy, count):
        return from_neighbour(sz, recv_ref, dx, dy, sz.head, count)

    put_borders(sz, v_ref, 2, beside)
    wide = sz.py + 2

    def line(band, j):
        low, high = (2 * j + 1, 2 * j + 2) if j < g else (wide - 1, 0)
        low, high = band * wide + low, band * wide + high
        return jnp.where(lane < PATCH, lift[low : low + 1], lift[high : high + 1])

    row = iota((PAD, LANES), 0)
    for j in range(g + 1):
        lanes = pl.ds(j * LANES, LANES)
        for a in range(sz.px):
            rows = pl.ds(a * PATCH, PATCH)
            v_ref[rows, lanes] = se_ref[rows, lanes] * v_ref[rows, lanes] + line(a + 1, j)
        rows = pl.ds(r, PAD)
        both = jnp.where(row < PAD // 2, line(sz.px + 1, j), line(0, j))
        v_ref[rows, lanes] = se_ref[rows, lanes] * v_ref[rows, lanes] + both


def row_dot(sz, left, right):
    line = jnp.sum(left * right, axis=0, keepdims=True)
    total = line[:, 0:LANES]
    for j in range(1, sz.groups):
        total = total + line[:, j * LANES : (j + 1) * LANES]
    return total


def apply_kernel(sz, last, recv_ref, lg_ref, to_ref, tm_ref, se_ref, ke_ref, cols_ref,
                 w_ref, dots_ref, spread_ref, flat_ref, t_ref, pay_ref, state_ref, out_dots_ref,
                 v_ref, y_ref, lift_ref):
    r, c = sz.rows, sz.cols
    precondition(sz, recv_ref, lg_ref, to_ref, tm_ref, se_ref, v_ref, state_ref, lift_ref)
    t_ref[0] = w_ref[0] * smooth(sz, v_ref, ke_ref, y_ref)
    t_ref[1] = jnp.zeros((r, c), F32)
    crossed = scatter_patches(sz, t_ref, cols_ref, spread_ref, 1.0, flat_ref, lift_ref)
    own = v_ref[pl.ds(0, r), pl.ds(0, c)]
    state_ref[1] = own
    gamma = row_dot(sz, state_ref[0], own)
    curve = row_dot(sz, own, t_ref[0]) + crossed
    if last:
        out_dots_ref[...] = dots_ref[...]
        lane = iota((1, LANES), 1)
        lines = jnp.zeros((1, LANES), F32)
        for i, part in enumerate((dots_ref[0:1], dots_ref[1:2], gamma, curve)):
            lines = jnp.where(lane == i, jnp.sum(part, axis=1, keepdims=True), lines)

        def fill(s, carry):
            pay_ref[s] = lines
            return carry

        lax.fori_loop(0, sz.devices, fill, 0, unroll=True if sz.devices <= 16 else 1)
    else:
        out_dots_ref[...] = jnp.concatenate(
            [gamma, curve, jnp.zeros((PAD - 2, LANES), F32)], axis=0
        )
        pack_payload(sz, t_ref, pay_ref)


def final_kernel(sz, recv_ref, x0_ref, rp_ref, wz_ref, to_ref, tm_ref, x_ref, res_ref):
    def add(s, lines):
        return lines + recv_ref[s]

    lines = lax.fori_loop(
        1, sz.devices, add, recv_ref[0], unroll=True if sz.devices <= 16 else 1
    )
    lane = iota((1, LANES), 1)
    gamma, delta, cross, far = (
        jnp.sum(jnp.where(lane == i, lines, 0.0), axis=1, keepdims=True) for i in range(4)
    )
    step = gamma / delta
    gamma_new = step * step * cross - gamma
    growth = step * cross / delta
    curve = step * step * (far - cross * cross / delta)
    step_new = gamma_new / curve
    along = step + step_new * growth
    back = step_new * step
    x_ref[0] = x0_ref[0] + (along * rp_ref[1] - back * wz_ref[1])
    image = to_ref[0] + tm_ref[1]
    res_ref[0] = rp_ref[0] - (along * wz_ref[0] - back * image)


def shape(*dims):
    return jax.ShapeDtypeStruct(dims, F32)


def data_space(sz):
    block = BSIDE * BSIDE
    return [
        pltpu.VMEM((2, sz.rows, sz.cols), F32),
        pltpu.VMEM((sz.obs, sz.reach, block, block), F32),
        pltpu.SemaphoreType.DMA((sz.obs,)),
    ]


def cost(micros):
    return pl.CostEstimate(flops=0, bytes_accessed=int(micros * 3.0e6), transcendentals=0)


def local(right_side, initial_guess, kappa_sq, smooth_weight, precond_scale, phi_vals, phi_cols,
          coarse_slots, slot_count, coarse_rows):
    tx, ty = lax.axis_size("gx"), lax.axis_size("gy")
    phi_cols = jnp.swapaxes(phi_cols, 3, 4)
    sz = Sizes(tx, ty, right_side.shape[1:], phi_vals.shape[3], phi_vals.shape[4],
               coarse_rows.shape[2])
    swap = [(0, 1), (1, 0)]
    x_partner = lax.ppermute(initial_guess, "vert", swap)
    s_partner = lax.ppermute(precond_scale, "vert", swap)

    def exchange(array):
        return lax.all_to_all(array, ALL, 0, 0, tiled=True)

    cap = coarse_slots.shape[1]
    edges, *shares = pl.pallas_call(
        functools.partial(setup_kernel, sz),
        out_shape=[shape(sz.devices, 5 * sz.groups, 1, LANES)]
        + [shape(sz.vec_rows * sz.lift_rows, LANES)] * tx,
        in_specs=[ANY] * 5 + [SMEM],
        out_specs=[VMEM] * (1 + tx),
        scratch_shapes=[pltpu.VMEM((3, sz.rows, sz.cols), F32), pltpu.VMEM((cap, sz.nco), F32),
                        pltpu.VMEM((1, cap), jnp.int32), pltpu.SemaphoreType.DMA((5,))],
        compiler_params=EDGE_PARAMS,
        cost_estimate=cost(1.5),
    )(initial_guess, precond_scale, kappa_sq, coarse_rows, coarse_slots, slot_count)
    got = [lax.ppermute(shares[k], "gx", [(i, i ^ k) for i in range(tx)]) for k in range(1, tx)]
    lift_matrix = sum(got, shares[0])
    edges, x_partner = lax.optimization_barrier((edges, x_partner))
    edges = exchange(edges)

    r, c = sz.rows, sz.cols
    block = BSIDE * BSIDE
    pair = shape(2, r, c)
    payload = shape(sz.devices, sz.head + PAD, LANES)

    def data(stage, *fields):
        lines = (sz.obs, sz.reach * (2 + sz.reach * (stage == 1)))
        return pl.pallas_call(
            functools.partial(data_kernel, sz, stage),
            out_shape=pair if stage == 0 else shape(*lines, block),
            in_specs=[VMEM] * len(fields) + [SMEM, ANY],
            out_specs=VMEM,
            scratch_shapes=[pltpu.VMEM(lines + (block,), F32)] * (stage == 0) + data_space(sz),
            compiler_params=DATA_PARAMS,
            cost_estimate=cost(4),
        )(*fields, phi_cols, phi_vals)

    terms = data(0, initial_guess, x_partner)
    parts, sent, s_ext, k_ext = pl.pallas_call(
        functools.partial(first_kernel, sz),
        out_shape=[pair, payload, shape(*sz.ext), shape(*sz.ext)],
        in_specs=[VMEM] * 6 + [SMEM],
        out_specs=[VMEM] * 4,
        scratch_shapes=[pltpu.VMEM(sz.ext, F32)] * 2,
        compiler_params=PARAMS,
        cost_estimate=cost(3),
    )(edges, initial_guess, precond_scale, kappa_sq, right_side, terms, smooth_weight)

    def apply(last, received, parts, mirrored, dots, spread, flat):
        return pl.pallas_call(
            functools.partial(apply_kernel, sz, last),
            out_shape=[pair, shape(sz.devices, 1, LANES) if last else payload,
                       pair, shape(PAD, LANES)],
            in_specs=[VMEM] * 6 + [SMEM, SMEM] + [VMEM] * 3,
            out_specs=[VMEM] * 4,
            scratch_shapes=[pltpu.VMEM(sz.ext, F32), pltpu.VMEM(sz.ext, F32),
                            pltpu.VMEM((sz.lift_rows, LANES), F32)],
            compiler_params=PARAMS,
            cost_estimate=cost(3),
        )(received, lift_matrix, parts, mirrored, s_ext, k_ext, phi_cols,
          smooth_weight, dots, spread, flat)

    dots = jnp.zeros((PAD, LANES), F32)
    mirrored = lax.ppermute(parts, "vert", swap)
    received = exchange(sent)
    flat = data(1, parts, mirrored, s_ext, s_partner)
    parts, sent, early, dots = apply(
        False, received, parts, mirrored, dots, flat, flat
    )
    mirrored = lax.ppermute(parts, "vert", swap)
    received = exchange(sent)
    spread = data(2, parts, mirrored, s_ext, s_partner)
    parts, sent, late, dots = apply(
        True, received, parts, mirrored, dots, spread, flat
    )
    mirrored = lax.ppermute(parts, "vert", swap)
    return tuple(pl.pallas_call(
        functools.partial(final_kernel, sz),
        out_shape=[shape(1, r, c)] * 2,
        in_specs=[VMEM] * 6,
        out_specs=[VMEM] * 2,
        compiler_params=PARAMS,
        cost_estimate=cost(1),
    )(exchange(sent), initial_guess, early, late, parts, mirrored))


def solution(mesh):
    return jax.shard_map(
        local,
        mesh=mesh,
        in_specs=(
            P(("groups", "vert"), "gx", "gy"),
            P(("groups", "vert"), "gx", "gy"),
            P(("groups", "vert"), "gx", "gy"),
            P(("groups", "vert")),
            P(("groups", "vert"), "gx", "gy"),
            P(("groups", "vert"), "gx", "gy", None, None, None, None),
            P(("groups", "vert"), "gx", "gy", None, None),
            P(("groups", "gx"), None),
            P(("groups", "gx")),
            P(("groups", "gx"), None, None),
        ),
        out_specs=(P(("groups", "vert"), "gx", "gy"), P(("groups", "vert"), "gx", "gy")),
        check_vma=False,
    )
```
